128 devices in a mesh: rows: 32 (over z_lo, y, x), seq: 4 (over z_hi, core).
Axes of the slice: x: 4, y: 4, z: 4 (z_hi: 2, z_lo: 2; z = z_hi * 2 + z_lo), core: 2. Of those that a mesh axis runs over, the one named last changes fastest.
Arguments:
- block_input: bfloat16 [32, 512, 768], P('rows', 'seq'), may hold values from -6 to 6
- out_cotangent: bfloat16 [32, 512, 768], P('rows', 'seq'), may hold values from -6 to 6
- image_lengths: int32 [32, 4], P('rows'), may hold values from 12 to 476, as said below
- span_order: int32 [32, 4], P('rows'), may hold values from 0 to 3, each once within a row
- attn_gain: float32 [768], replicated, may hold values from 0.25 to 1.75
- attn_shift: float32 [768], replicated, may hold values from -4 to 4
- qkv_weight: bfloat16 [768, 2304], replicated, may hold values from -0.21875 to 0.21875
- query_bias: float32 [768], replicated, may hold values from -4 to 4
- value_bias: float32 [768], replicated, may hold values from -4 to 4
- proj_weight: bfloat16 [768, 768], replicated, may hold values from -0.875 to 0.875
- proj_bias: float32 [768], replicated, may hold values from -4 to 4
- mlp_gain: float32 [768], replicated, may hold values from 0.25 to 1.75
- mlp_shift: float32 [768], replicated, may hold values from -4 to 4
- up_weight: bfloat16 [768, 3072], replicated, may hold values from -0.21875 to 0.21875
- up_bias: float32 [3072], replicated, may hold values from -4 to 4
- down_weight: bfloat16 [3072, 768], replicated, may hold values from -0.109375 to 0.109375
- down_bias: float32 [768], replicated, may hold values from -4 to 4
Outputs:
- block_output: bfloat16 [32, 512, 768], P('rows', 'seq')
- input_grad: bfloat16 [32, 512, 768], P('rows', 'seq')
- attn_gain_grad: float32 [768], replicated
- attn_shift_grad: float32 [768], replicated
- qkv_weight_grad: float32 [768, 2304], replicated
- query_bias_grad: float32 [768], replicated
- value_bias_grad: float32 [768], replicated
- proj_weight_grad: float32 [768, 768], replicated
- proj_bias_grad: float32 [768], replicated
- mlp_gain_grad: float32 [768], replicated
- mlp_shift_grad: float32 [768], replicated
- up_weight_grad: float32 [768, 3072], replicated
- up_bias_grad: float32 [3072], replicated
- down_weight_grad: float32 [3072, 768], replicated
- down_bias_grad: float32 [768], replicated
The draws below stay inside these ranges and needn't reach their ends.
Inputs may be any that keep to these rules, and one draw needn't show every extreme that they name: `image_lengths`: the 4 lengths of each row sum to 512. In each row one of them, at a place drawn for that row, holds the rest of the row and is 386 or more, so that this image covers tokens of every block of the row; each of the others is 12, 18 or 32. Each row of span_order is an ordering of the numbers 0 to 4 - 1; the device at index j of seq holds the row's tokens span_order[row, j] * 128 to span_order[row, j] * 128 + 127.
All inputs are finite; a program needn't handle non-finite values.
Results may differ from the reference program's by a relative error of at most 0.02.
Values may be sent and summed in bfloat16 or wider, within the bound.
A program may use at most 192 MiB of HBM per device.

```python
import jax
import jax.numpy as jnp
from jax import lax

D = 768
HEADS = 12
HEAD_DIM = 64
FF = 3072
SEG_TOK = 128
IMAGES = 4
LEN = 512
ROWS = 32
N_SEQ = 4


def draw_image_lengths(key, part):
    key = jax.random.fold_in(key, 11)
    grid_sizes = jnp.array([25, 36, 64], dtype=jnp.int32) * SEG_TOK // 256
    picks = jax.random.randint(jax.random.fold_in(key, 1), (ROWS, IMAGES), 0, 3)
    smalls = jnp.sum(jnp.where(picks[:, :, None] == jnp.arange(3, dtype=jnp.int32)[None, None, :], grid_sizes[None, None, :], 0), axis=2, dtype=jnp.int32)
    big_place = jax.random.randint(jax.random.fold_in(key, 2), (ROWS, 1), 0, IMAGES)
    single_row = jax.random.randint(jax.random.fold_in(key, 3), (), 0, ROWS)
    is_single = jnp.arange(ROWS)[:, None] == single_row
    smalls = jnp.where(is_single, grid_sizes[0], smalls)
    is_big = jnp.arange(IMAGES)[None, :] == big_place
    smalls = jnp.where(is_big, 0, smalls)
    big_len = LEN - jnp.sum(smalls, axis=1, keepdims=True)
    return jnp.where(is_big, big_len, smalls).astype(jnp.int32)


def block_scale(stream_key, dims, split, low, high):
    gain = 1.0
    for position, blocks in split:
        draws = jax.random.uniform(jax.random.fold_in(jax.random.fold_in(stream_key, 6), position), (blocks,), jnp.float32, low / len(split), high / len(split))
        gain = gain * jnp.repeat(jnp.exp(draws), dims[position] // blocks).reshape((-1,) + (1,) * (len(dims) - 1 - position))
    return gain


def noise(rng, extent, scale, bound, pieces=(), held_as=jnp.bfloat16):
    result = scale * jax.random.normal(rng, extent, jnp.float32)
    if pieces:
        result = result * block_scale(rng, extent, pieces, -0.22, 0.18)
    return jnp.clip(result, -bound, bound).astype(held_as)


def setup_inputs(seed: int = 0) -> dict:
    key_list = jax.random.split(jax.random.key(seed), 18)
    return {
        "block_input": noise(key_list[0], (ROWS, LEN, D), 1.0, 6.0, ((0, 32), (1, 4))),
        "out_cotangent": noise(key_list[1], (ROWS, LEN, D), 1.0, 6.0, ((0, 32), (1, 4))),
        "image_lengths": draw_image_lengths(jax.random.fold_in(key_list[17], 71), 0),
        "span_order": jax.vmap(lambda own: jax.random.permutation(own, N_SEQ))(jax.random.split(key_list[3], ROWS)).reshape((ROWS, N_SEQ)).astype(jnp.int32),
        "attn_gain": jnp.clip(1.0 + 0.15 * jax.random.normal(key_list[4], (D,), jnp.float32), 0.25, 1.75),
        "attn_shift": noise(key_list[5], (D,), 0.3, 4.0, (), jnp.float32),
        "qkv_weight": noise(key_list[6], (D, 3 * D), D ** -0.5, 0.21875),
        "query_bias": noise(key_list[7], (D,), 0.3, 4.0, (), jnp.float32),
        "value_bias": noise(key_list[8], (D,), 0.3, 4.0, (), jnp.float32),
        "proj_weight": noise(key_list[9], (D, D), (D // 16) ** -0.5, 0.875),
        "proj_bias": noise(key_list[10], (D,), 0.3, 4.0, (), jnp.float32),
        "mlp_gain": jnp.clip(1.0 + 0.15 * jax.random.normal(key_list[11], (D,), jnp.float32), 0.25, 1.75),
        "mlp_shift": noise(key_list[12], (D,), 0.3, 4.0, (), jnp.float32),
        "up_weight": noise(key_list[13], (D, FF), D ** -0.5, 0.21875),
        "up_bias": noise(key_list[14], (FF,), 0.3, 4.0, (), jnp.float32),
        "down_weight": noise(key_list[15], (FF, D), FF ** -0.5, 0.109375),
        "down_bias": noise(key_list[16], (D,), 0.3, 4.0, (), jnp.float32),
    }


@jax.custom_vjp
def low(v):
    return lax.optimization_barrier(v.astype(jnp.bfloat16)).astype(jnp.float32)

@jax.custom_vjp
def low_back(v):
    return v

def low_keep(v):
    return (low(v), None)

def low_pass(kept, grad):
    return (grad,)

def back_keep(v):
    return (v, None)

def back_low(kept, grad):
    return (low(grad),)
low.defvjp(low_keep, low_pass)
low_back.defvjp(back_keep, back_low)
epsilon = 1e-06

def matmul(left, right):
    return jnp.dot(left, right, precision=lax.Precision.HIGHEST, preferred_element_type=jnp.float32)

def segment_ids(image_lengths, span_order, span_len):
    part_count = span_order.shape[1]
    places = jnp.arange(part_count * span_len, dtype=jnp.int32)
    span_index = places // span_len
    matches = span_index[None, :, None] == jnp.arange(part_count, dtype=jnp.int32)[None, None, :]
    picked = lax.optimization_barrier(jnp.sum(jnp.where(matches, span_order[:, None, :], 0), axis=2, dtype=jnp.int32))
    anchor = picked * span_len + places[None, :] % span_len
    image_ends = jnp.cumsum(image_lengths, axis=1, dtype=jnp.int32)[:, :-1]
    return lax.optimization_barrier(jnp.sum((anchor[:, :, None] >= image_ends[:, None, :]).astype(jnp.int32), axis=2, dtype=jnp.int32))

def layer_norm(values, gain_vec, shift_vec):
    mean_val = lax.optimization_barrier(jnp.mean(values, axis=-1, keepdims=True))
    centred = values - mean_val
    factor = lax.rsqrt(lax.optimization_barrier(jnp.mean(centred * centred, axis=-1, keepdims=True)) + epsilon)
    return centred * factor * gain_vec + shift_vec

def row_forward(row_input, row_segments, params):
    attn_gain, attn_shift, qkv_weight, query_bias, value_bias, proj_weight, proj_bias, mlp_gain, mlp_shift, up_weight, up_bias, down_weight, down_bias = params
    length = row_input.shape[0]
    attn_in = low(layer_norm(row_input, attn_gain, attn_shift))
    qkv_out = low_back(matmul(attn_in, qkv_weight))
    queries = low(qkv_out[:, :D] + query_bias).reshape(length, HEADS, HEAD_DIM)
    keys_all = low(qkv_out[:, D:2 * D]).reshape(length, HEADS, HEAD_DIM)
    values = low(qkv_out[:, 2 * D:] + value_bias).reshape(length, HEADS, HEAD_DIM)
    scores = jnp.einsum('qhd,khd->hqk', queries, keys_all, precision=lax.Precision.HIGHEST) * HEAD_DIM ** (-0.5)
    scores = low_back(scores)
    same_image = row_segments[:, None] == row_segments[None, :]
    scores = jnp.where(same_image[None], scores, -1e+30)
    row_max = lax.optimization_barrier(jnp.max(scores, axis=2, keepdims=True))
    exp_scores = jnp.exp(scores - row_max)
    weights = low(exp_scores / lax.optimization_barrier(jnp.sum(exp_scores, axis=2, keepdims=True)))
    attended = jnp.einsum('hqk,khd->qhd', weights, values, precision=lax.Precision.HIGHEST).reshape(length, D)
    attended = low(low_back(attended))
    resid = row_input + low_back(matmul(attended, proj_weight)) + proj_bias
    mlp_in = low(layer_norm(resid, mlp_gain, mlp_shift))
    hidden = low(jax.nn.gelu(low_back(matmul(mlp_in, up_weight)) + up_bias, approximate=False))
    return resid + matmul(hidden, down_weight) + down_bias

def forward(inputs, params, segments):
    row_step = jax.checkpoint(row_forward)

    def one_row(row_pair):
        return row_step(row_pair[0], row_pair[1], params)
    return lax.map(one_row, (inputs, segments))

def reference(block_input, out_cotangent, image_lengths, span_order, attn_gain, attn_shift, qkv_weight, query_bias, value_bias, proj_weight, proj_bias, mlp_gain, mlp_shift, up_weight, up_bias, down_weight, down_bias):
    segments = segment_ids(image_lengths, span_order, SEG_TOK)
    params = (attn_gain.astype(jnp.float32), attn_shift.astype(jnp.float32), qkv_weight.astype(jnp.float32), query_bias.astype(jnp.float32), value_bias.astype(jnp.float32), proj_weight.astype(jnp.float32), proj_bias.astype(jnp.float32), mlp_gain.astype(jnp.float32), mlp_shift.astype(jnp.float32), up_weight.astype(jnp.float32), up_bias.astype(jnp.float32), down_weight.astype(jnp.float32), down_bias.astype(jnp.float32))
    inputs = block_input.astype(jnp.float32)

    def whole(input_arg, param_arg):
        return forward(input_arg, param_arg, segments)
    output, pullback = jax.vjp(whole, inputs, params)
    input_grad, grads = pullback(out_cotangent.astype(jnp.float32))
    return (output.astype(jnp.bfloat16), input_grad.astype(jnp.bfloat16), grads[0], grads[1], grads[2], grads[3], grads[4], grads[5], grads[6], grads[7], grads[8], grads[9], grads[10], grads[11], grads[12])
```

```python
from functools import partial

import jax
import jax.numpy as jnp
from jax import lax
from jax.experimental import pallas as pl
from jax.experimental.pallas import tpu as pltpu
from jax.sharding import PartitionSpec as P

HEADS = 12
HEAD_DIM = 64


epsilon = 1e-06


def segment_ids(image_lengths, span_order, span_len):
    part_count = span_order.shape[1]
    places = jnp.arange(part_count * span_len, dtype=jnp.int32)
    span_index = places // span_len
    matches = span_index[None, :, None] == jnp.arange(part_count, dtype=jnp.int32)[None, None, :]
    picked = jnp.sum(jnp.where(matches, span_order[:, None, :], 0), axis=2, dtype=jnp.int32)
    anchor = picked * span_len + places[None, :] % span_len
    image_ends = jnp.cumsum(image_lengths, axis=1, dtype=jnp.int32)[:, :-1]
    return jnp.sum(
        (anchor[:, :, None] >= image_ends[:, None, :]).astype(jnp.int32), axis=2, dtype=jnp.int32
    )


def layer_norm(values, gain_vec, shift_vec):
    mean_val = jnp.mean(values, axis=-1, keepdims=True)
    centred = values - mean_val
    factor = lax.rsqrt(jnp.mean(centred * centred, axis=-1, keepdims=True) + epsilon)
    normed = centred * factor
    return (normed * gain_vec + shift_vec, normed, factor)


def norm_back(upstream, normed, factor, gain_vec):
    scaled_grad = upstream * gain_vec
    return factor * (
        scaled_grad
        - jnp.mean(scaled_grad, axis=-1, keepdims=True)
        - normed * jnp.mean(scaled_grad * normed, axis=-1, keepdims=True)
    )


def weight_product(left, right):
    return jnp.einsum("td,te->de", left, right, preferred_element_type=jnp.float32)


def times_transposed(left, right):
    return jnp.einsum("te,de->td", left, right, preferred_element_type=jnp.float32)


def pairs_joined(stacked, row_count, length, width):
    return stacked.transpose(1, 2, 0, 3).reshape(row_count, length, width)


MESH = pl.DeviceIdType.MESH
DIMS = 6
SETS = 3
STEPS = 10


def place():
    row, seq = lax.axis_index("rows"), lax.axis_index("seq")
    x, y, z_lo = row % 4, (row // 4) % 4, row // 16
    z_hi, core = seq // 2, seq % 2
    z = z_hi * 2 + z_lo

    def device(x, y, z, core):
        return ((z % 2) * 16 + y * 4 + x, (z // 2) * 2 + core)

    near = lambda v: v + 1 - 2 * (v % 2)
    far = lambda v: 3 - v
    partners = (
        device(near(x), y, z, core),
        device(far(x), y, z, core),
        device(x, near(y), z, core),
        device(x, far(y), z, core),
        device(x, y, near(z), core),
        device(x, y, far(z), core),
    )
    first = lambda v: (v % 2 + v // 2) % 2
    bits = (first(x), x // 2, first(y), y // 2, first(z), z // 2)
    sibling = device(x, y, z, 1 - core)
    return partners, bits, sibling, core


def add_into(target, source):
    target[...] = (target[...].astype(jnp.float32) + source[...].astype(jnp.float32)).astype(
        jnp.bfloat16
    )


class Exchange:
    def __init__(self, grads, whole, landing, send_sem, recv_sem):
        self.partners, self.bits, self.sibling, self.core = place()
        self.grads, self.whole, self.landing = grads, whole, landing
        self.send_sem, self.recv_sem = send_sem, recv_sem
        self.copies = {}

    def dim(self, k, s):
        return (k + s) % DIMS

    def rows(self, k, s):
        low = 128 * k
        for t in range(min(s, 3)):
            low = low + self.bits[self.dim(k, t)] * (64 >> t)
        return low

    def block(self, w, k, s, mine, whole=False):
        held = self.whole.at[w, self.core] if whole else self.grads.at[w]
        bit = self.bits[self.dim(k, s)]
        pick = bit if mine else 1 - bit
        if s < 3:
            size = 64 >> s
            low = pl.multiple_of(self.rows(k, s) + pick * size, 16)
            return held.at[pl.ds(low, size)]
        low = pl.multiple_of(self.rows(k, 3), 16)
        return held.at[pl.ds(low, 16), pl.ds(pl.multiple_of(pick * 768, 128), 768)]

    def slot(self, w, k, s):
        if s < 3:
            return self.landing.at[w, k, pl.ds((0, 64, 96)[s], 64 >> s)]
        return self.landing.at[w, k, pl.ds((112, 112, 128)[s - 3], 16), pl.ds((0, 768, 0)[s - 3], 768)]

    def start(self, w, k, s):
        if s < 4:
            src, dst, d = self.block(w, k, s, False), self.slot(w, k, s), self.dim(k, s)
        elif s < 6:
            src, dst, d = self.block(w, k, 3, True), self.slot(w, k, s), self.dim(k, s)
        else:
            t = 9 - s
            src = dst = self.block(w, k, t, True, True)
            d = self.dim(k, t)
        copy = pltpu.make_async_remote_copy(
            src_ref=src,
            dst_ref=dst,
            send_sem=self.send_sem.at[w, k, s],
            recv_sem=self.recv_sem.at[w, k, s],
            device_id=self.partners[d],
            device_id_type=MESH,
        )
        copy.start()
        self.copies[w, k, s] = copy

    def across(self, w, k, part):
        src = self.block(w, k, 0, part == 0, True)
        copy = pltpu.make_async_remote_copy(
            src_ref=src,
            dst_ref=src,
            send_sem=self.send_sem.at[w, k, STEPS + part],
            recv_sem=self.recv_sem.at[w, k, STEPS + part],
            device_id=self.sibling,
            device_id_type=MESH,
        )
        copy.start()
        self.copies[w, k, STEPS + part] = copy

    def finish(self, w, s):
        for k in range(DIMS):
            self.copies[w, k, s].wait()
            if s < 4:
                add_into(self.block(w, k, s, True), self.slot(w, k, s))
            elif s < 6:
                add_into(self.block(w, k, 3, True), self.slot(w, k, s))
            if s == 5:
                self.block(w, k, 3, True, True)[...] = self.block(w, k, 3, True)[...]
            if s < STEPS - 1:
                self.start(w, k, s + 1)
                if s == STEPS - 2:
                    self.across(w, k, 0)
            else:
                self.across(w, k, 1)

    def done(self, w):
        for k in range(DIMS):
            self.copies[w, k, STEPS].wait()
            self.copies[w, k, STEPS + 1].wait()


def reduce_kernel(parts, grads_out, grads, whole, halves, landing, send_sem, recv_sem, half_sem, local_sem):
    ex = Exchange(grads, whole, landing, send_sem, recv_sem)
    barrier = pltpu.get_barrier_semaphore()
    for device in ex.partners + (ex.sibling,):
        pl.semaphore_signal(barrier, inc=1, device_id=device, device_id_type=MESH)
    load = pltpu.make_async_copy(parts.at[:, ex.core], grads, local_sem)
    load.start()
    pl.semaphore_wait(barrier, DIMS + 1)
    load.wait()
    copies = []
    for w in range(SETS):
        copy = pltpu.make_async_remote_copy(
            src_ref=parts.at[w, 1 - ex.core],
            dst_ref=halves.at[w],
            send_sem=half_sem.at[0, w],
            recv_sem=half_sem.at[1, w],
            device_id=ex.sibling,
            device_id_type=MESH,
        )
        copy.start()
        copies.append(copy)
    for w in range(SETS):
        copies[w].wait()

        def add(i, carry):
            rows = pl.ds(pl.multiple_of(i * 64, 64), 64)
            add_into(grads.at[w, rows], halves.at[w, rows])
            return carry

        lax.fori_loop(0, 12, add, 0)
        for k in range(DIMS):
            ex.start(w, k, 0)
    for s in range(STEPS):
        for w in range(SETS):
            ex.finish(w, s)
    for w in range(SETS):
        ex.done(w)
    store = pltpu.make_async_copy(whole, grads_out, local_sem)
    store.start()
    store.wait()


def reduce_grads(parts):
    return pl.pallas_call(
        reduce_kernel,
        out_shape=jax.ShapeDtypeStruct((SETS, 2, 768, 1536), jnp.bfloat16),
        in_specs=[pl.BlockSpec(memory_space=pl.ANY)],
        out_specs=pl.BlockSpec(memory_space=pl.ANY),
        scratch_shapes=[
            pltpu.VMEM((SETS, 768, 1536), jnp.bfloat16),
            pltpu.VMEM((SETS, 2, 768, 1536), jnp.bfloat16),
            pltpu.VMEM((SETS, 768, 1536), jnp.bfloat16),
            pltpu.VMEM((SETS, DIMS, 144, 1536), jnp.bfloat16),
            pltpu.SemaphoreType.DMA((SETS, DIMS, STEPS + 2)),
            pltpu.SemaphoreType.DMA((SETS, DIMS, STEPS + 2)),
            pltpu.SemaphoreType.DMA((2, SETS)),
            pltpu.SemaphoreType.DMA,
        ],
        compiler_params=pltpu.CompilerParams(
            collective_id=0, has_side_effects=True, vmem_limit_bytes=48 << 20
        ),
    )(parts)


def body(
    block_input,
    out_cotangent,
    image_lengths,
    span_order,
    attn_gain,
    attn_shift,
    qkv_weight,
    query_bias,
    value_bias,
    proj_weight,
    proj_bias,
    mlp_gain,
    mlp_shift,
    up_weight,
    up_bias,
    down_weight,
    down_bias,
):
    row_count, span_len, model_width = block_input.shape
    seq_parts = lax.axis_size("seq")
    full_len = span_len * seq_parts
    token_count = row_count * span_len
    pair_count = HEADS // 2
    pair_width = 2 * HEAD_DIM
    head_scale = HEAD_DIM ** (-0.5)
    pair_numbers = jnp.arange(pair_count, dtype=jnp.int32)
    segments = segment_ids(image_lengths, span_order, span_len)
    own_segments = lax.dynamic_slice_in_dim(segments, lax.axis_index("seq") * span_len, span_len, 1)
    same_image = own_segments[:, :, None] == segments[:, None, :]
    flat_input = block_input.reshape(token_count, model_width).astype(jnp.float32)
    attn_normed, attn_hat, attn_factor = layer_norm(flat_input, attn_gain, attn_shift)
    attn_low = attn_normed.astype(jnp.bfloat16)
    qkv_out = jnp.dot(attn_low, qkv_weight, preferred_element_type=jnp.float32)
    queries = (
        (qkv_out[:, :model_width] + query_bias)
        .astype(jnp.bfloat16)
        .reshape(row_count, span_len, model_width)
    )
    keys_local = (
        qkv_out[:, model_width : 2 * model_width]
        .astype(jnp.bfloat16)
        .reshape(row_count, span_len, model_width)
    )
    values_local = (
        (qkv_out[:, 2 * model_width :] + value_bias)
        .astype(jnp.bfloat16)
        .reshape(row_count, span_len, model_width)
    )
    keys_whole, values_whole = (
        lax.all_gather(keys_local, "seq", axis=1, tiled=True),
        lax.all_gather(values_local, "seq", axis=1, tiled=True),
    )

    def pair_slice(source, pair_index, source_len):
        picked = lax.dynamic_slice_in_dim(source, pair_index * pair_width, pair_width, 2)
        return picked.reshape(row_count, source_len, 2, HEAD_DIM)

    def pair_scores(pair_index, key_source):
        query_part = pair_slice(queries, pair_index, span_len)
        key_part = pair_slice(key_source, pair_index, full_len)
        scores = (
            jnp.einsum("rqhd,rkhd->rhqk", query_part, key_part, preferred_element_type=jnp.float32)
            * head_scale
        )
        return (jnp.where(same_image[:, None], scores, -1e30), query_part, key_part)

    def attend_pair(pair_index):
        scores, query_part, key_part = pair_scores(pair_index, keys_whole)
        row_max = jnp.max(scores, axis=3, keepdims=True)
        exp_scores = jnp.exp(scores - row_max)
        row_sum = jnp.sum(exp_scores, axis=3, keepdims=True)
        weights = (exp_scores / row_sum).astype(jnp.bfloat16)
        value_part = pair_slice(values_whole, pair_index, full_len)
        attended = jnp.einsum(
            "rhqk,rkhd->rqhd", weights, value_part, preferred_element_type=jnp.float32
        )
        return (
            attended.reshape(row_count, span_len, pair_width).astype(jnp.bfloat16),
            row_max + jnp.log(row_sum),
        )

    attended_pairs, log_sums = lax.map(attend_pair, pair_numbers)
    attended_low = attended_pairs.transpose(1, 2, 0, 3).reshape(token_count, model_width)
    resid = (
        flat_input
        + jnp.dot(attended_low, proj_weight, preferred_element_type=jnp.float32)
        + proj_bias
    )
    mlp_normed, mlp_hat, mlp_factor = layer_norm(resid, mlp_gain, mlp_shift)
    mlp_low = mlp_normed.astype(jnp.bfloat16)
    up_pre = jnp.dot(mlp_low, up_weight, preferred_element_type=jnp.float32) + up_bias
    hidden, gelu_back = jax.vjp(partial(jax.nn.gelu, approximate=False), up_pre)
    hidden_low = hidden.astype(jnp.bfloat16)
    block_output = (
        resid + jnp.dot(hidden_low, down_weight, preferred_element_type=jnp.float32) + down_bias
    )
    block_output = block_output.astype(jnp.bfloat16).reshape(row_count, span_len, model_width)
    cotangent = out_cotangent.reshape(token_count, model_width)
    cotangent_full = cotangent.astype(jnp.float32)
    down_weight_grad = weight_product(hidden_low, cotangent)
    down_bias_grad = jnp.sum(cotangent_full, axis=0)
    hidden_grad = times_transposed(cotangent, down_weight)
    up_grad = gelu_back(hidden_grad)[0]
    up_bias_grad = jnp.sum(up_grad, axis=0)
    up_low = up_grad.astype(jnp.bfloat16)
    up_weight_grad = weight_product(mlp_low, up_low)
    mlp_grad = times_transposed(up_low, up_weight)
    mlp_gain_grad = jnp.sum(mlp_grad * mlp_hat, axis=0)
    mlp_shift_grad = jnp.sum(mlp_grad, axis=0)
    resid_grad = cotangent_full + norm_back(mlp_grad, mlp_hat, mlp_factor, mlp_gain)
    proj_bias_grad = jnp.sum(resid_grad, axis=0)
    resid_low = resid_grad.astype(jnp.bfloat16)
    proj_weight_grad = weight_product(attended_low, resid_low)
    attended_grad = times_transposed(resid_low, proj_weight).astype(jnp.bfloat16)
    attended_grad = attended_grad.reshape(row_count, span_len, model_width)
    keys_again, values_again = (
        lax.all_gather(keys_local, "seq", axis=1, tiled=True),
        lax.all_gather(values_local, "seq", axis=1, tiled=True),
    )

    def query_side_pair(pair_index):
        scores, query_part, key_part = pair_scores(pair_index, keys_again)
        probs = jnp.exp(scores - log_sums[pair_index])
        grad_part = pair_slice(attended_grad, pair_index, span_len)
        value_part = pair_slice(values_again, pair_index, full_len)
        prob_grad = jnp.einsum(
            "rqhd,rkhd->rhqk", grad_part, value_part, preferred_element_type=jnp.float32
        )
        totals = jnp.sum(probs * prob_grad, axis=3, keepdims=True)
        score_low = (probs * (prob_grad - totals)).astype(jnp.bfloat16)
        query_grad = (
            jnp.einsum("rhqk,rkhd->rqhd", score_low, key_part, preferred_element_type=jnp.float32)
            * head_scale
        )
        return (probs, score_low, query_part, grad_part, query_grad, totals)

    def pair_backward(pair_index):
        probs, score_low, query_part, grad_part, query_grad, totals = query_side_pair(pair_index)
        weights = probs.astype(jnp.bfloat16)
        value_grad = jnp.einsum(
            "rhqk,rqhd->rkhd", weights, grad_part, preferred_element_type=jnp.float32
        )
        key_grad = (
            jnp.einsum("rhqk,rqhd->rkhd", score_low, query_part, preferred_element_type=jnp.float32)
            * head_scale
        )
        return (
            query_grad.reshape(row_count, span_len, pair_width),
            key_grad.reshape(row_count, full_len, pair_width),
            value_grad.reshape(row_count, full_len, pair_width),
        )

    query_pairs, key_pairs, value_pairs = lax.map(pair_backward, pair_numbers)
    key_value_term = jnp.concatenate(
        (
            pairs_joined(key_pairs, row_count, full_len, model_width),
            pairs_joined(value_pairs, row_count, full_len, model_width),
        ),
        axis=2,
    )
    key_value_grad = (
        lax.psum_scatter(
            key_value_term.astype(jnp.bfloat16), "seq", scatter_dimension=1, tiled=True
        )
        .astype(jnp.float32)
        .reshape(token_count, 2 * model_width)
    )
    query_grad = query_pairs.transpose(1, 2, 0, 3).reshape(token_count, model_width)
    query_bias_grad = jnp.sum(query_grad, axis=0)
    value_bias_grad = jnp.sum(key_value_grad[:, model_width:], axis=0)
    qkv_low = jnp.concatenate((query_grad, key_value_grad), axis=1).astype(jnp.bfloat16)
    qkv_weight_grad = weight_product(attn_low, qkv_low)
    attn_grad = times_transposed(qkv_low, qkv_weight)
    attn_gain_grad = jnp.sum(attn_grad * attn_hat, axis=0)
    attn_shift_grad = jnp.sum(attn_grad, axis=0)
    input_grad = resid_grad + norm_back(attn_grad, attn_hat, attn_factor, attn_gain)
    input_grad = input_grad.astype(jnp.bfloat16).reshape(row_count, span_len, model_width)
    low = jnp.bfloat16
    down_parts = down_weight_grad.reshape(2, 2, 768, 768).transpose(0, 2, 1, 3).reshape(2, 768, 1536)
    up_parts = up_weight_grad.reshape(768, 2, 1536).transpose(1, 0, 2)
    attn_parts = jnp.concatenate(
        (
            qkv_weight_grad.reshape(768, 2, 1152).transpose(1, 0, 2),
            proj_weight_grad.reshape(768, 2, 384).transpose(1, 0, 2),
        ),
        axis=2,
    )
    total = reduce_grads(
        jnp.stack((down_parts.astype(low), up_parts.astype(low), attn_parts.astype(low)))
    )
    down_sum = (
        total[0].reshape(2, 768, 2, 768).transpose(0, 2, 1, 3).reshape(3072, 768).astype(jnp.float32)
    )
    up_sum = total[1].transpose(1, 0, 2).reshape(768, 3072).astype(jnp.float32)
    qkv_sum = total[2, :, :, :1152].transpose(1, 0, 2).reshape(768, 2304).astype(jnp.float32)
    proj_sum = total[2, :, :, 1152:].transpose(1, 0, 2).reshape(768, 768).astype(jnp.float32)
    vectors = lax.psum(
        (
            attn_gain_grad,
            attn_shift_grad,
            query_bias_grad,
            value_bias_grad,
            proj_bias_grad,
            mlp_gain_grad,
            mlp_shift_grad,
            up_bias_grad,
            down_bias_grad,
        ),
        ("rows", "seq"),
    )
    summed = (
        vectors[0],
        vectors[1],
        qkv_sum,
        vectors[2],
        vectors[3],
        proj_sum,
        vectors[4],
        vectors[5],
        vectors[6],
        up_sum,
        vectors[7],
        down_sum,
        vectors[8],
    )
    return (
        block_output,
        input_grad,
        summed[0],
        summed[1],
        summed[2],
        summed[3],
        summed[4],
        summed[5],
        summed[6],
        summed[7],
        summed[8],
        summed[9],
        summed[10],
        summed[11],
        summed[12],
    )


def solution(mesh):
    return jax.shard_map(
        body,
        mesh=mesh,
        in_specs=(
            P("rows", "seq", None),
            P("rows", "seq", None),
            P("rows", None),
            P("rows", None),
            P(),
            P(),
            P(),
            P(),
            P(),
            P(),
            P(),
            P(),
            P(),
            P(),
            P(),
            P(),
            P(),
        ),
        out_specs=(
            P("rows", "seq", None),
            P("rows", "seq", None),
            P(),
            P(),
            P(),
            P(),
            P(),
            P(),
            P(),
            P(),
            P(),
            P(),
            P(),
            P(),
            P(),
        ),
        check_vma=False,
    )
```

```python
from types import SimpleNamespace

import jax
import jax.numpy as jnp
from jax import lax
from jax.experimental import pallas as pl
from jax.experimental.pallas import tpu as pltpu
from jax.sharding import PartitionSpec as P

MESH = pl.DeviceIdType.MESH
BF, F32 = jnp.bfloat16, jnp.float32
WIDTH = 768
HIDDEN = 3072
HALF = HIDDEN // 2
TOK = 128
LEN = 512
PAIRS = 6
SCALE = 64**-0.5
EPSILON = 1e-6

DIMS = 6
SETS = 3
STEPS = 10

TAIL = (
    0.14361835615286447,
    0.14366105191010822,
    0.12424683572786965,
    0.09467827005043768,
    0.003990377379362003,
    0.09912410558005538,
    -0.21460327937017376,
    0.13425173188400444,
    -0.02896737861797067,
)
DENSITY = 0.3989422804014327


def rows_of(start, size):
    return pl.ds(pl.multiple_of(start, size), size)


def dot(a, b):
    return lax.dot_general(a, b, (((1,), (0,)), ((), ())), preferred_element_type=F32)


def dot_rt(a, b):
    return lax.dot_general(a, b, (((1,), (1,)), ((), ())), preferred_element_type=F32)


def dot_lt(a, b):
    return lax.dot_general(a, b, (((0,), (0,)), ((), ())), preferred_element_type=F32)


def place():
    row, seq = lax.axis_index("rows"), lax.axis_index("seq")
    x, y, z_lo = row % 4, (row // 4) % 4, row // 16
    z_hi, core = seq // 2, seq % 2
    z = z_hi * 2 + z_lo

    def device(x, y, z, core):
        return ((z % 2) * 16 + y * 4 + x, (z // 2) * 2 + core)

    near = lambda v: v + 1 - 2 * (v % 2)
    far = lambda v: 3 - v
    first = lambda v: (v % 2 + v // 2) % 2
    return SimpleNamespace(
        seq=seq,
        core=core,
        chip=z_hi,
        partners=(
            device(near(x), y, z, core),
            device(far(x), y, z, core),
            device(x, near(y), z, core),
            device(x, far(y), z, core),
            device(x, y, near(z), core),
            device(x, y, far(z), core),
        ),
        bits=(first(x), x // 2, first(y), y // 2, first(z), z // 2),
        sibling=(row, z_hi * 2 + 1 - core),
        across=(row, (1 - z_hi) * 2 + core),
    )


class Exchange:
    def __init__(self, at, grads, whole, landing, send_sem, recv_sem):
        self.at = at
        self.grads, self.whole, self.landing = grads, whole, landing
        self.send_sem, self.recv_sem = send_sem, recv_sem
        self.copies = {}

    def dim(self, k, s):
        return (k + s) % DIMS

    def rows(self, k, s):
        low = TOK * k
        for t in range(min(s, 3)):
            low = low + self.at.bits[self.dim(k, t)] * (64 >> t)
        return low

    def block(self, w, k, s, mine, whole=False):
        held = self.whole.at[w, self.at.core] if whole else self.grads.at[w]
        bit = self.at.bits[self.dim(k, s)]
        pick = bit if mine else 1 - bit
        if s < 3:
            size = 64 >> s
            return held.at[pl.ds(pl.multiple_of(self.rows(k, s) + pick * size, 16), size)]
        return held.at[
            pl.ds(pl.multiple_of(self.rows(k, 3), 16), 16),
            pl.ds(pl.multiple_of(pick * WIDTH, 128), WIDTH),
        ]

    def slot(self, w, k, s):
        if s < 3:
            return self.landing.at[w, k, pl.ds((0, 64, 96)[s], 64 >> s)]
        return self.landing.at[
            w, k, pl.ds((112, 112, 128)[s - 3], 16), pl.ds((0, WIDTH, 0)[s - 3], WIDTH)
        ]

    def send(self, w, k, s, src, dst, device):
        copy = pltpu.make_async_remote_copy(
            src_ref=src,
            dst_ref=dst,
            send_sem=self.send_sem.at[w, k, s],
            recv_sem=self.recv_sem.at[w, k, s],
            device_id=device,
            device_id_type=MESH,
        )
        copy.start()
        self.copies[w, k, s] = copy

    def start(self, w, k, s):
        if s < 4:
            src, dst, d = self.block(w, k, s, False), self.slot(w, k, s), self.dim(k, s)
        elif s < 6:
            src, dst, d = self.block(w, k, 3, True), self.slot(w, k, s), self.dim(k, s)
        else:
            src = dst = self.block(w, k, 9 - s, True, True)
            d = self.dim(k, 9 - s)
        self.send(w, k, s, src, dst, self.at.partners[d])

    def over(self, w, k, part):
        half = self.block(w, k, 0, part == 0, True)
        self.send(w, k, STEPS + part, half, half, self.at.sibling)

    def finish(self, w, s):
        for k in range(DIMS):
            self.copies[w, k, s].wait()
            if s < 6:
                kept, slot = self.block(w, k, min(s, 3), True), self.slot(w, k, s)
                total = (kept[...].astype(F32) + slot[...].astype(F32)).astype(BF)
                if s < 5:
                    kept[...] = total
                else:
                    self.block(w, k, 3, True, True)[...] = total
            if s < STEPS - 1:
                self.start(w, k, s + 1)
                if s == STEPS - 2:
                    self.over(w, k, 0)
            else:
                self.over(w, k, 1)


def normalize(load, gain, shift, normed, factor, result, base):
    def step(i, carry):
        rows = rows_of(i * 16, 16)
        v = load(rows)
        c = v - jnp.mean(v, axis=1, keepdims=True)
        f = lax.rsqrt(jnp.mean(c * c, axis=1, keepdims=True) + EPSILON)
        n = c * f
        normed[rows, :] = n
        factor[rows, :] = f
        result[rows_of(base + i * 16, 16), :] = (n * gain[...] + shift[...]).astype(BF)
        return carry

    lax.fori_loop(0, TOK // 16, step, 0)


def folded(v):
    return jnp.sum(v.reshape(2, 8, WIDTH), axis=0)


def norm_back(load_grad, load_rest, gain, normed, factor, vec, where, keep):
    zero = jnp.zeros((8, WIDTH), F32)

    def step(i, carry):
        rows = rows_of(i * 16, 16)
        e, n = load_grad(rows), normed[rows, :]
        g = e * gain[...]
        a = jnp.mean(g, axis=1, keepdims=True)
        b = jnp.mean(g * n, axis=1, keepdims=True)
        back = load_rest(rows) + factor[rows, :] * (g - a - n * b)
        keep(rows, back)
        return carry[0] + folded(e * n), carry[1] + folded(e), carry[2] + folded(back)

    sums = lax.fori_loop(0, TOK // 16, step, (zero, zero, zero))
    for row, total in zip(where, sums):
        vec[row : row + 1, :] = jnp.sum(total, axis=0, keepdims=True)


def scratch():
    v = pltpu.VMEM
    dma = pltpu.SemaphoreType.DMA
    return dict(
        qkv_w=v((WIDTH, 3 * WIDTH), BF),
        proj_w=v((WIDTH, WIDTH), BF),
        up_w=v((WIDTH, HALF), BF),
        down_w=v((HALF, WIDTH), BF),
        normed_in=v((LEN, WIDTH), BF),
        queries=v((LEN, WIDTH), BF),
        keys=v((LEN, WIDTH), BF),
        values=v((LEN, WIDTH), BF),
        hat1=v((TOK, WIDTH), F32),
        fac1=v((TOK, 1), F32),
        bias=v((TOK, LEN), F32),
        probs=v((PAIRS, 2 * TOK, LEN), F32),
        attended_full=v((TOK, WIDTH), F32),
        attended=v((2 * TOK, WIDTH), BF),
        resid=v((TOK, WIDTH), F32),
        hat2=v((TOK, WIDTH), F32),
        fac2=v((TOK, 1), F32),
        mlp_in=v((2 * TOK, WIDTH), BF),
        cot2=v((2 * TOK, WIDTH), BF),
        hidden_grad=v((2 * TOK, HALF), F32),
        hidden=v((2 * TOK, HALF), BF),
        up_low=v((2 * TOK, HALF), BF),
        mlp_part=v((2 * TOK, WIDTH), F32),
        mlp_came=v((TOK, WIDTH), F32),
        out_part=v((2 * TOK, WIDTH), F32),
        out_came=v((TOK, WIDTH), F32),
        resid_grad=v((TOK, WIDTH), F32),
        resid_low=v((TOK, WIDTH), BF),
        attended_grad=v((LEN, WIDTH), BF),
        stat=v((TOK, 128), F32),
        stats=v((4, 32, 128), F32),
        qkv_low=v((TOK, 3 * WIDTH), BF),
        qkv_half=v((2 * TOK, 1152), BF),
        resid_half=v((2 * TOK, 384), BF),
        key_grad=v((TOK, WIDTH), F32),
        value_grad=v((TOK, WIDTH), F32),
        scores=v((2 * TOK, LEN), F32),
        scores2=v((2 * TOK, 256), F32),
        low1=v((2 * TOK, LEN), BF),
        low2=v((2 * TOK, 256), BF),
        pre=v((2 * TOK, 256), F32),
        up_bias_half=v((1, HALF), F32),
        vec=v((16, WIDTH), F32),
        lines=v((8, WIDTH), F32),
        vec_came=v((DIMS + 1, 16, WIDTH), F32),
        grads=v((SETS, WIDTH, HALF), BF),
        whole=v((SETS, 2, WIDTH, HALF), BF),
        landing=v((SETS, DIMS, 144, HALF), BF),
        send_sem=dma((SETS, DIMS, STEPS + 2)),
        recv_sem=dma((SETS, DIMS, STEPS + 2)),
        side_send=dma((16,)),
        side_recv=dma((16,)),
        vec_send=dma((DIMS + 1,)),
        vec_recv=dma((DIMS + 1,)),
        load_sem=dma((4,)),
        out_sem=dma((SETS, 2)),
    )


NAMES = tuple(scratch())


def kernel(
    lengths,
    order,
    x,
    cot,
    attn_gain,
    attn_shift,
    query_bias,
    value_bias,
    proj_bias,
    mlp_gain,
    mlp_shift,
    up_bias,
    down_bias,
    qkv_weight,
    proj_weight,
    up_weight,
    down_weight,
    block_output,
    input_grad,
    whole_out,
    vec_out,
    *refs,
):
    m = SimpleNamespace(**dict(zip(NAMES, refs)))
    at = place()
    core, seq = at.core, at.seq
    ex = Exchange(at, m.grads, m.whole, m.landing, m.send_sem, m.recv_sem)

    barrier = pltpu.get_barrier_semaphore()
    for device in at.partners + (at.sibling, at.across):
        pl.semaphore_signal(barrier, inc=1, device_id=device, device_id_type=MESH)

    loads = [
        pltpu.make_async_copy(src, dst, m.load_sem.at[i])
        for i, (src, dst) in enumerate(
            (
                (qkv_weight, m.qkv_w),
                (down_weight.at[rows_of(core * HALF, HALF)], m.down_w),
                (proj_weight, m.proj_w),
                (up_weight.at[:, rows_of(core * HALF, HALF)], m.up_w),
            )
        )
    ]
    for load in loads:
        load.start()

    def side(i, src, dst, device):
        copy = pltpu.make_async_remote_copy(
            src_ref=src,
            dst_ref=dst,
            send_sem=m.side_send.at[i],
            recv_sem=m.side_recv.at[i],
            device_id=device,
            device_id_type=MESH,
        )
        copy.start()
        return copy

    own = rows_of(seq * TOK, TOK)
    two = rows_of(core * TOK, TOK)
    two_other = rows_of((1 - core) * TOK, TOK)
    far_block = (1 - at.chip) * 2 + core
    far = rows_of(far_block * TOK, TOK)

    vectors = (attn_gain, attn_shift, query_bias, value_bias, proj_bias, mlp_gain, mlp_shift, down_bias)
    for i, vector in enumerate(vectors):
        m.lines[i : i + 1, :] = vector[...][None]
    attn_gain, attn_shift, query_bias, value_bias, proj_bias, mlp_gain, mlp_shift, down_bias = (
        m.lines.at[i : i + 1] for i in range(8)
    )

    normalize(
        lambda rows: x[0, rows, :].astype(F32), attn_gain, attn_shift, m.hat1, m.fac1, m.normed_in, seq * TOK
    )
    m.cot2[two, :] = cot[0]
    ends = [lengths[0, 0]]
    for i in (1, 2):
        ends.append(ends[-1] + lengths[0, i])
    segment = lambda t: sum((t >= end).astype(jnp.int32) for end in ends)
    mine = segment(lax.broadcasted_iota(jnp.int32, (TOK, TOK), 0) + order[0, seq] * TOK)
    for j in range(4):
        other = segment(lax.broadcasted_iota(jnp.int32, (TOK, TOK), 1) + order[0, j] * TOK)
        m.bias[:, j * TOK : (j + 1) * TOK] = jnp.where(mine == other, 0.0, -1e30)
    m.up_bias_half[...] = jnp.where(core == 0, up_bias[:HALF], up_bias[HALF:])[None]
    m.vec[...] = jnp.zeros((16, WIDTH), F32)
    m.vec[7:8, :] = jnp.sum(
        jnp.sum(cot[0].astype(F32).reshape(TOK // 8, 8, WIDTH), axis=0), axis=0, keepdims=True
    )
    m.stat[...] = jnp.zeros((TOK, 128), F32)
    lane = lax.broadcasted_iota(jnp.int32, (1, 128), 1)
    low_lanes = (lane < 64).astype(BF)
    high_lanes = (lane >= 64).astype(BF)

    def both(v):
        return jnp.concatenate((v * low_lanes, v * high_lanes), axis=0)

    def joined(v):
        return jnp.where(lane < 64, v[:TOK], v[TOK:])

    pl.semaphore_wait(barrier, DIMS + 2)
    in_sib = side(0, m.normed_in.at[own], m.normed_in.at[own], at.sibling)
    in_far = side(1, m.normed_in.at[own], m.normed_in.at[own], at.across)
    cot_sib = side(3, m.cot2.at[two], m.cot2.at[two], at.sibling)

    def project(base):
        rows = rows_of(base, 2 * TOK)

        def step(i, carry):
            tile = lambda part: rows_of(i * 256, 256) if part == 0 else pl.ds(
                pl.multiple_of(part * WIDTH + i * 256, 256), 256
            )
            cols = tile(0)
            a = m.normed_in[rows, :]
            m.keys[rows, cols] = dot(a, m.qkv_w[:, tile(1)]).astype(BF)
            m.values[rows, cols] = (dot(a, m.qkv_w[:, tile(2)]) + value_bias[:, cols]).astype(BF)
            m.queries[rows, cols] = ((dot(a, m.qkv_w[:, tile(0)]) + query_bias[:, cols]) * SCALE).astype(BF)
            return carry

        lax.fori_loop(0, 3, step, 0)

    loads[0].wait()
    in_sib.wait()
    project(at.chip * 2 * TOK)
    loads[1].wait()
    cot_sib.wait()

    def hidden_back(i, carry):
        cols = rows_of(i * 256, 256)
        m.hidden_grad[:, cols] = dot_rt(m.cot2[...], m.down_w[cols, :])
        return carry

    lax.fori_loop(0, HALF // 256, hidden_back, 0)
    in_far.wait()
    in_pass = side(2, m.normed_in.at[far], m.normed_in.at[far], at.sibling)
    in_pass.wait()
    project((1 - at.chip) * 2 * TOK)

    def attend(i, carry):
        cols = rows_of(i * 128, 128)
        m.scores[...] = dot_rt(both(m.queries[own, cols]), m.keys[:, cols])

        def soften(r, carry):
            rows = rows_of(r * 32, 32)
            token = rows_of((r % 4) * 32, 32)
            s = m.scores[rows, :] + m.bias[token, :]
            top = jnp.max(s, axis=1, keepdims=True)
            e = jnp.exp(s - top)
            total = jnp.sum(e, axis=1, keepdims=True)
            p = e * (1.0 / total)
            m.probs[i, rows, :] = p
            m.low1[rows, :] = p.astype(BF)
            head = 2 * i + r // 4
            m.stat[token, :] = jnp.where(lane == head, top + jnp.log(total), m.stat[token, :])
            return carry

        lax.fori_loop(0, 8, soften, 0, unroll=2)
        out = joined(dot(m.low1[...], m.values[:, cols]))
        m.attended_full[:, cols] = out
        m.attended[two, cols] = out.astype(BF)
        return carry

    lax.fori_loop(0, PAIRS, attend, 0)

    loads[2].wait()

    def project_out(i, carry):
        cols = rows_of(i * 256, 256)
        m.resid[:, cols] = (
            x[0, :, cols].astype(F32) + dot(m.attended[two, :], m.proj_w[:, cols]) + proj_bias[:, cols]
        )
        return carry

    lax.fori_loop(0, 3, project_out, 0)
    normalize(lambda rows: m.resid[rows, :], mlp_gain, mlp_shift, m.hat2, m.fac2, m.mlp_in, core * TOK)
    mlp_sib = side(4, m.mlp_in.at[two], m.mlp_in.at[two], at.sibling)
    att_sib = side(5, m.attended.at[two], m.attended.at[two], at.sibling)
    loads[3].wait()
    mlp_sib.wait()

    def feed(i, carry):
        cols = rows_of(i * 256, 256)
        m.pre[...] = dot(m.mlp_in[...], m.up_w[:, cols])

        def act(r, total):
            rows = rows_of(r * 32, 32)
            u = m.pre[rows, :] + m.up_bias_half[:, cols]
            t = 1.0 / (1.0 + 0.36 * jnp.abs(u))
            tail = jnp.full_like(t, TAIL[-1])
            for c in TAIL[-2::-1]:
                tail = tail * t + c
            e = jnp.exp(-0.5 * (u * u))
            tail = tail * (t * e)
            phi = jnp.where(u >= 0, 1.0 - tail, tail)
            m.hidden[rows, cols] = (u * phi).astype(BF)
            g = m.hidden_grad[rows, cols] * (phi + u * (DENSITY * e))
            m.up_low[rows, cols] = g.astype(BF)
            return total + jnp.sum(g.reshape(4, 8, 256), axis=0)

        total = lax.fori_loop(0, 8, act, jnp.zeros((8, 256), F32), unroll=2)
        m.up_bias_half[:, cols] = jnp.sum(total, axis=0, keepdims=True)
        return carry

    lax.fori_loop(0, HALF // 256, feed, 0)
    for k in range(DIMS):
        for h in range(2):
            first = h * WIDTH + k * TOK
            m.grads[0, k * TOK : (k + 1) * TOK, h * WIDTH : (h + 1) * WIDTH] = dot_lt(
                m.hidden[:, first : first + TOK], m.cot2[...]
            ).astype(BF)
        ex.start(0, k, 0)
    for k in range(DIMS):
        m.grads[1, k * TOK : (k + 1) * TOK, :] = dot_lt(
            m.mlp_in[:, k * TOK : (k + 1) * TOK], m.up_low[...]
        ).astype(BF)
        ex.start(1, k, 0)
    for h in range(2):
        for t in range(2):
            m.vec[8 + 2 * h + t : 9 + 2 * h + t, :] = jnp.where(
                core == h, m.up_bias_half[:, t * WIDTH : (t + 1) * WIDTH], 0.0
            )

    def mlp_back(i, carry):
        cols = rows_of(i * 256, 256)
        m.mlp_part[:, cols] = dot_rt(m.up_low[...], m.up_w[cols, :])
        return carry

    lax.fori_loop(0, 3, mlp_back, 0)
    part_sib = side(6, m.mlp_part.at[two_other], m.mlp_came, at.sibling)

    def feed_out(i, carry):
        cols = rows_of(i * 256, 256)
        m.out_part[:, cols] = dot(m.hidden[...], m.down_w[:, cols])
        return carry

    lax.fori_loop(0, 3, feed_out, 0)
    out_sib = side(7, m.out_part.at[two_other], m.out_came, at.sibling)
    part_sib.wait()

    def keep_resid(rows, back):
        m.resid_grad[rows, :] = back
        m.resid_low[rows, :] = back.astype(BF)

    norm_back(
        lambda rows: m.mlp_part[rows_of_shift(rows, core * TOK), :] + m.mlp_came[rows, :],
        lambda rows: cot[0, rows, :].astype(F32),
        mlp_gain,
        m.hat2,
        m.fac2,
        m.vec,
        (5, 6, 4),
        keep_resid,
    )

    def attended_back(i, carry):
        cols = rows_of(i * 256, 256)
        m.attended_grad[own, cols] = dot_rt(m.resid_low[...], m.proj_w[cols, :]).astype(BF)
        return carry

    lax.fori_loop(0, 3, attended_back, 0)
    grad_sib = side(8, m.attended_grad.at[own], m.attended_grad.at[own], at.sibling)
    grad_far = side(9, m.attended_grad.at[own], m.attended_grad.at[own], at.across)

    def means(i, carry):
        cols = rows_of(i * 128, 128)
        v = m.attended_grad[own, cols].astype(F32) * m.attended_full[:, cols]
        a = jnp.sum(jnp.where(lane < 64, v, 0.0), axis=1, keepdims=True)
        b = jnp.sum(jnp.where(lane < 64, 0.0, v), axis=1, keepdims=True)
        m.stat[...] = jnp.where(
            lane == 16 + 2 * i, a, jnp.where(lane == 17 + 2 * i, b, m.stat[...])
        )
        return carry

    lax.fori_loop(0, PAIRS, means, 0)
    m.stats[seq] = jnp.transpose(m.stat[...])[:32]
    stat_sib = side(11, m.stats.at[seq], m.stats.at[seq], at.sibling)
    stat_far = side(12, m.stats.at[seq], m.stats.at[seq], at.across)
    half = lambda c, size: pl.ds(pl.multiple_of(c * size, 128), size)
    m.resid_half[two, :] = m.resid_low[:, half(core, 384)]
    resid_sib = side(14, m.resid_low.at[:, half(1 - core, 384)], m.resid_half.at[two], at.sibling)

    ex.finish(0, 0)

    def query_side(i, carry):
        cols = rows_of(i * 128, 128)
        m.scores[...] = dot_rt(both(m.attended_grad[own, cols]), m.values[:, cols])

        def back(r, carry):
            rows = rows_of(r * 32, 32)
            head = 16 + 2 * i + r // 4
            stat = m.stat[rows_of((r % 4) * 32, 32), :]
            mean = jnp.sum(jnp.where(lane == head, stat, 0.0), axis=1, keepdims=True)
            m.low1[rows, :] = (m.probs[i, rows, :] * (m.scores[rows, :] - mean)).astype(BF)
            return carry

        lax.fori_loop(0, 8, back, 0, unroll=2)
        g = joined(dot(m.low1[...], m.keys[:, cols])) * SCALE
        m.vec[2:3, cols] = jnp.sum(g, axis=0, keepdims=True)
        m.qkv_low[:, cols] = g.astype(BF)
        return carry

    lax.fori_loop(0, PAIRS, query_side, 0)
    ex.finish(1, 0)

    def key_side(chip, first):
        rows_q = rows_of(chip * 256, 256)

        def step(i, carry):
            cols = rows_of(i * 128, 128)
            q, g = m.queries[rows_q, cols], m.attended_grad[rows_q, cols]
            m.scores[:, :256] = dot_rt(both(m.keys[own, cols]), q)
            m.scores2[...] = dot_rt(both(m.values[own, cols]), g)

            def back(r, carry):
                rows = rows_of(r * 32, 32)
                head = 2 * i + r // 4
                line = lambda h: jnp.concatenate(
                    (m.stats[chip * 2, pl.ds(h, 1), :], m.stats[chip * 2 + 1, pl.ds(h, 1), :]), axis=1
                )
                bias = m.bias[rows_of((r % 4) * 32, 32), rows_q]
                p = jnp.exp(m.scores[rows, :256] + bias - line(head))
                m.low1[rows, :256] = p.astype(BF)
                m.low2[rows, :] = (p * (m.scores2[rows, :] - line(16 + head))).astype(BF)
                return carry

            lax.fori_loop(0, 8, back, 0, unroll=2)
            dv = joined(dot(m.low1[:, :256], g))
            dk = joined(dot(m.low2[...], q))
            if first:
                m.value_grad[:, cols] = dv
                m.key_grad[:, cols] = dk
            else:
                dv = dv + m.value_grad[:, cols]
                dk = dk + m.key_grad[:, cols]
                m.vec[3:4, cols] = jnp.sum(dv, axis=0, keepdims=True)
                m.qkv_low[:, pl.ds(pl.multiple_of(WIDTH + i * 128, 128), 128)] = dk.astype(BF)
                m.qkv_low[:, pl.ds(pl.multiple_of(2 * WIDTH + i * 128, 128), 128)] = dv.astype(BF)
            return carry

        lax.fori_loop(0, PAIRS, step, 0)

    grad_sib.wait()
    stat_sib.wait()
    key_side(at.chip, True)
    ex.finish(0, 1)
    ex.finish(1, 1)

    grad_far.wait()
    grad_pass = side(10, m.attended_grad.at[far], m.attended_grad.at[far], at.sibling)
    stat_far.wait()
    stat_pass = side(13, m.stats.at[far_block], m.stats.at[far_block], at.sibling)
    ex.finish(0, 2)
    grad_pass.wait()
    stat_pass.wait()
    key_side(1 - at.chip, False)

    m.qkv_half[two, :] = m.qkv_low[:, half(core, 1152)]
    qkv_sib = side(15, m.qkv_low.at[:, half(1 - core, 1152)], m.qkv_half.at[two], at.sibling)
    ex.finish(1, 2)
    ex.finish(0, 3)

    att_sib.wait()
    resid_sib.wait()
    qkv_sib.wait()
    chip_rows = rows_of(at.chip * 2 * TOK, 2 * TOK)
    for k in range(DIMS):
        rows = slice(k * TOK, (k + 1) * TOK)
        m.grads[2, rows, :1152] = dot_lt(m.normed_in[chip_rows, rows], m.qkv_half[...]).astype(BF)
        m.grads[2, rows, 1152:] = dot_lt(m.attended[:, rows], m.resid_half[...]).astype(BF)
        ex.start(2, k, 0)

    def input_back(i, carry):
        cols = rows_of(i * 256, 256)
        m.mlp_came[:, cols] = dot_rt(m.qkv_low[...], m.qkv_w[cols, :])
        return carry

    lax.fori_loop(0, 3, input_back, 0)

    def keep_input(rows, back):
        input_grad[0, rows, :] = back.astype(BF)

    norm_back(
        lambda rows: m.mlp_came[rows, :],
        lambda rows: m.resid_grad[rows, :],
        attn_gain,
        m.hat1,
        m.fac1,
        m.vec,
        (0, 1),
        keep_input,
    )

    def vec_start(s):
        copy = pltpu.make_async_remote_copy(
            src_ref=m.vec,
            dst_ref=m.vec_came.at[s],
            send_sem=m.vec_send.at[s],
            recv_sem=m.vec_recv.at[s],
            device_id=(at.partners + (at.sibling,))[s],
            device_id_type=MESH,
        )
        copy.start()
        return copy

    vec_copy = [vec_start(0)]

    def vec_finish(s):
        vec_copy[0].wait()
        m.vec[...] = m.vec[...] + m.vec_came[s]
        if s < DIMS:
            vec_copy[0] = vec_start(s + 1)
        else:
            vec_out[...] = m.vec[...]

    ex.finish(1, 3)
    ex.finish(0, 4)
    out_sib.wait()

    def close(i, carry):
        rows = rows_of(i * 16, 16)
        block_output[0, rows, :] = (
            m.resid[rows, :]
            + (m.out_part[rows_of(core * TOK + i * 16, 16), :] + m.out_came[rows, :])
            + down_bias[...]
        ).astype(BF)
        return carry

    lax.fori_loop(0, TOK // 16, close, 0)

    events = [(1, 4), (0, 5), (2, 0), (1, 5), (0, 6), (2, 1), (1, 6), (0, 7), (2, 2), (1, 7), (0, 8), (2, 3), (1, 8)]
    events += [(2, 4), (0, 9), (2, 5), (1, 9), (2, 6), (2, 7), (2, 8), (2, 9)]
    for n, (w, s) in enumerate(events):
        ex.finish(w, s)
        if n % 2 == 0 and n // 2 <= DIMS:
            vec_finish(n // 2)

    stores = []
    for w in range(SETS):
        for k in range(DIMS):
            for part in range(2):
                ex.copies[w, k, STEPS + part].wait()
        store = pltpu.make_async_copy(m.whole.at[w], whole_out.at[w], m.out_sem.at[w, 0])
        store.start()
        stores.append(store)
    for store in stores:
        store.wait()


def rows_of_shift(rows, shift):
    return pl.ds(pl.multiple_of(rows.start + shift, 16), rows.size)


def spread_kernel(
    parts,
    vec,
    block_output_in,
    input_grad_in,
    block_output,
    input_grad,
    attn_gain,
    attn_shift,
    qkv,
    query_bias,
    value_bias,
    proj,
    proj_bias,
    mlp_gain,
    mlp_shift,
    up,
    up_bias,
    down,
    down_bias,
):
    for c in range(2):
        up[:, c * HALF : (c + 1) * HALF] = parts[1, c].astype(F32)
        qkv[:, c * 1152 : (c + 1) * 1152] = parts[2, c, :, :1152].astype(F32)
        proj[:, c * 384 : (c + 1) * 384] = parts[2, c, :, 1152:].astype(F32)
        for h in range(2):
            down[2 * c + h] = parts[0, c, :, h * WIDTH : (h + 1) * WIDTH].astype(F32)

    @pl.when(pl.program_id(0) == 0)
    def _():
        block_output[...] = block_output_in[...]
        input_grad[...] = input_grad_in[...]
        for row, ref in enumerate(
            (attn_gain, attn_shift, query_bias, value_bias, proj_bias, mlp_gain, mlp_shift, down_bias)
        ):
            ref[...] = vec[row]
        for t in range(4):
            up_bias[t * WIDTH : (t + 1) * WIDTH] = vec[8 + t]


def spread(parts, vec, block_output, input_grad):
    rows = 64
    line = lambda n: (jax.ShapeDtypeStruct((n,), F32), pl.BlockSpec((n,), lambda i: (0,)))
    flat = lambda n: (jax.ShapeDtypeStruct((WIDTH, n), F32), pl.BlockSpec((rows, n), lambda i: (i, 0)))
    tokens = (jax.ShapeDtypeStruct((1, TOK, WIDTH), BF), pl.BlockSpec((1, TOK, WIDTH), lambda i: (0, 0, 0)))
    outs = [
        tokens,
        tokens,
        line(WIDTH),
        line(WIDTH),
        flat(3 * WIDTH),
        line(WIDTH),
        line(WIDTH),
        flat(WIDTH),
        line(WIDTH),
        line(WIDTH),
        line(WIDTH),
        flat(HIDDEN),
        line(HIDDEN),
        (
            jax.ShapeDtypeStruct((4, WIDTH, WIDTH), F32),
            pl.BlockSpec((4, rows, WIDTH), lambda i: (0, i, 0)),
        ),
        line(WIDTH),
    ]
    return pl.pallas_call(
        spread_kernel,
        grid=(WIDTH // rows,),
        out_shape=[o[0] for o in outs],
        in_specs=[
            pl.BlockSpec((SETS, 2, rows, HALF), lambda i: (0, 0, i, 0)),
            pl.BlockSpec((16, WIDTH), lambda i: (0, 0)),
            tokens[1],
            tokens[1],
        ],
        out_specs=[o[1] for o in outs],
        compiler_params=pltpu.CompilerParams(vmem_limit_bytes=VMEM_LIMIT),
    )(parts, vec, block_output, input_grad)


def body(
    block_input,
    out_cotangent,
    image_lengths,
    span_order,
    attn_gain,
    attn_shift,
    qkv_weight,
    query_bias,
    value_bias,
    proj_weight,
    proj_bias,
    mlp_gain,
    mlp_shift,
    up_weight,
    up_bias,
    down_weight,
    down_bias,
):
    vmem = pl.BlockSpec(memory_space=pltpu.VMEM)
    smem = pl.BlockSpec(memory_space=pltpu.SMEM)
    hbm = pl.BlockSpec(memory_space=pl.ANY)
    held = scratch()
    block_output, input_grad, parts, vec = pl.pallas_call(
        kernel,
        out_shape=[
            jax.ShapeDtypeStruct((1, TOK, WIDTH), BF),
            jax.ShapeDtypeStruct((1, TOK, WIDTH), BF),
            jax.ShapeDtypeStruct((SETS, 2, WIDTH, HALF), BF),
            jax.ShapeDtypeStruct((16, WIDTH), F32),
        ],
        in_specs=[smem, smem] + [vmem] * 11 + [hbm] * 4,
        out_specs=[vmem, vmem, hbm, vmem],
        scratch_shapes=[held[name] for name in NAMES],
        compiler_params=pltpu.CompilerParams(
            collective_id=0, has_side_effects=True, vmem_limit_bytes=VMEM_LIMIT
        ),
    )(
        image_lengths,
        span_order,
        block_input,
        out_cotangent,
        attn_gain,
        attn_shift,
        query_bias,
        value_bias,
        proj_bias,
        mlp_gain,
        mlp_shift,
        up_bias,
        down_bias,
        qkv_weight,
        proj_weight,
        up_weight,
        down_weight,
    )
    outs = list(spread(parts, vec, block_output, input_grad))
    outs[13] = outs[13].reshape(HIDDEN, WIDTH)
    return tuple(outs)


VMEM_LIMIT = 62 << 20


def solution(mesh):
    tokens = P("rows", "seq", None)
    return jax.shard_map(
        body,
        mesh=mesh,
        in_specs=(tokens, tokens, P("rows", None), P("rows", None)) + (P(),) * 13,
        out_specs=(tokens, tokens) + (P(),) * 13,
        check_vma=False,
    )
```

```python
from types import SimpleNamespace

import jax
import jax.numpy as jnp
from jax import lax
from jax.experimental import pallas as pl
from jax.experimental.pallas import tpu as pltpu
from jax.sharding import PartitionSpec as P

MESH = pl.DeviceIdType.MESH
BF, F32 = jnp.bfloat16, jnp.float32
WIDTH = 768
HIDDEN = 3072
HALF = HIDDEN // 2
TOK = 128
LEN = 512
PAIRS = 6
SCALE = 64**-0.5
EPSILON = 1e-6

DIMS = 6
STEPS = 10
DOWN, UP, PROJ, KEYS = range(4)
WIDTHS = (HALF, HALF, WIDTH, WIDTH)

TAIL = (
    0.14361835615286447,
    0.14366105191010822,
    0.12424683572786965,
    0.09467827005043768,
    0.003990377379362003,
    0.09912410558005538,
    -0.21460327937017376,
    0.13425173188400444,
    -0.02896737861797067,
)
DENSITY = 0.3989422804014327


def rows_of(start, size):
    return pl.ds(pl.multiple_of(start, size), size)


def dot(a, b):
    return lax.dot_general(a, b, (((1,), (0,)), ((), ())), preferred_element_type=F32)


def dot_rt(a, b):
    return lax.dot_general(a, b, (((1,), (1,)), ((), ())), preferred_element_type=F32)


def dot_lt(a, b):
    return lax.dot_general(a, b, (((0,), (0,)), ((), ())), preferred_element_type=F32)


def place():
    row, seq = lax.axis_index("rows"), lax.axis_index("seq")
    x, y, z_lo = row % 4, (row // 4) % 4, row // 16
    z_hi, core = seq // 2, seq % 2
    z = z_hi * 2 + z_lo

    def device(x, y, z, core):
        return ((z % 2) * 16 + y * 4 + x, (z // 2) * 2 + core)

    near = lambda v: v + 1 - 2 * (v % 2)
    far = lambda v: 3 - v
    first = lambda v: (v % 2 + v // 2) % 2
    return SimpleNamespace(
        seq=seq,
        core=core,
        chip=z_hi,
        partners=(
            device(near(x), y, z, core),
            device(far(x), y, z, core),
            device(x, near(y), z, core),
            device(x, far(y), z, core),
            device(x, y, near(z), core),
            device(x, y, far(z), core),
        ),
        bits=(first(x), x // 2, first(y), y // 2, first(z), z // 2),
        sibling=(row, z_hi * 2 + 1 - core),
        across=(row, (1 - z_hi) * 2 + core),
    )


class Exchange:
    def __init__(self, at, grads, whole, landing, send_sem, recv_sem):
        self.at = at
        self.grads, self.whole, self.landing = grads, whole, landing
        self.send_sem, self.recv_sem = send_sem, recv_sem
        self.copies = {}

    def dim(self, k, s):
        return (k + s) % DIMS

    def rows(self, k, s):
        low = TOK * k
        for t in range(min(s, 3)):
            low = low + self.at.bits[self.dim(k, t)] * (64 >> t)
        return low

    def block(self, w, k, s, mine, whole=False):
        held = self.whole[w].at[self.at.core] if whole else self.grads[w]
        bit = self.at.bits[self.dim(k, s)]
        pick = bit if mine else 1 - bit
        if s < 3:
            size = 64 >> s
            return held.at[pl.ds(pl.multiple_of(self.rows(k, s) + pick * size, 16), size)]
        width = WIDTHS[w] // 2
        return held.at[
            pl.ds(pl.multiple_of(self.rows(k, 3), 16), 16),
            pl.ds(pl.multiple_of(pick * width, 128), width),
        ]

    def slot(self, w, k, s):
        if s < 3:
            return self.landing[w].at[k, pl.ds((0, 64, 96)[s], 64 >> s)]
        width = WIDTHS[w] // 2
        return self.landing[w].at[k, pl.ds((112, 112, 128)[s - 3], 16), pl.ds((0, width, 0)[s - 3], width)]

    def send(self, w, k, s, src, dst, device):
        copy = pltpu.make_async_remote_copy(
            src_ref=src,
            dst_ref=dst,
            send_sem=self.send_sem.at[w, k, s],
            recv_sem=self.recv_sem.at[w, k, s],
            device_id=device,
            device_id_type=MESH,
        )
        copy.start()
        self.copies[w, k, s] = copy

    def start(self, w, k, s=0):
        if s < 4:
            src, dst, d = self.block(w, k, s, False), self.slot(w, k, s), self.dim(k, s)
        elif s < 6:
            src, dst, d = self.block(w, k, 3, True), self.slot(w, k, s), self.dim(k, s)
        else:
            src = dst = self.block(w, k, 9 - s, True, True)
            d = self.dim(k, 9 - s)
        self.send(w, k, s, src, dst, self.at.partners[d])

    def over(self, w, k, part):
        half = self.block(w, k, 0, part == 0, True)
        self.send(w, k, STEPS + part, half, half, self.at.sibling)

    def finish(self, w, s):
        for k in range(DIMS):
            self.copies[w, k, s].wait()
            if s < 6:
                kept, slot = self.block(w, k, min(s, 3), True), self.slot(w, k, s)
                total = (kept[...].astype(F32) + slot[...].astype(F32)).astype(BF)
                if s < 5:
                    kept[...] = total
                else:
                    self.block(w, k, 3, True, True)[...] = total
            if s < STEPS - 1:
                self.start(w, k, s + 1)
                if s == STEPS - 2:
                    self.over(w, k, 0)
            else:
                self.over(w, k, 1)


def normalize(load, gain, shift, normed, factor, result, base):
    def step(i, carry):
        rows = rows_of(i * 16, 16)
        v = load(rows)
        c = v - jnp.mean(v, axis=1, keepdims=True)
        f = lax.rsqrt(jnp.mean(c * c, axis=1, keepdims=True) + EPSILON)
        n = c * f
        normed[rows, :] = n
        factor[rows, :] = f
        result[rows_of(base + i * 16, 16), :] = (n * gain[...] + shift[...]).astype(BF)
        return carry

    lax.fori_loop(0, TOK // 16, step, 0, unroll=True)


def folded(v):
    return jnp.sum(v.reshape(2, 8, WIDTH), axis=0)


def norm_back(load_grad, load_rest, gain, normed, factor, vec, where, keep):
    zero = jnp.zeros((8, WIDTH), F32)

    def step(i, carry):
        rows = rows_of(i * 16, 16)
        e, n = load_grad(rows), normed[rows, :]
        g = e * gain[...]
        a = jnp.mean(g, axis=1, keepdims=True)
        b = jnp.mean(g * n, axis=1, keepdims=True)
        back = load_rest(rows) + factor[rows, :] * (g - a - n * b)
        keep(rows, back)
        return carry[0] + folded(e * n), carry[1] + folded(e), carry[2] + folded(back)

    sums = lax.fori_loop(0, TOK // 16, step, (zero, zero, zero), unroll=True)
    for row, total in zip(where, sums):
        vec[row : row + 1, :] = jnp.sum(total, axis=0, keepdims=True)


def scratch():
    v = pltpu.VMEM
    dma = pltpu.SemaphoreType.DMA
    sets = len(WIDTHS)
    return dict(
        qkv_w=v((WIDTH, 3 * WIDTH), BF),
        proj_w=v((WIDTH, WIDTH), BF),
        up_w=v((WIDTH, HALF), BF),
        down_w=v((HALF, WIDTH), BF),
        lines=v((8, WIDTH), F32),
        up_bias_half=v((1, HALF), F32),
        normed_in=v((LEN, WIDTH), BF),
        queries=v((LEN, WIDTH), BF),
        keys=v((LEN, WIDTH), BF),
        values=v((LEN, WIDTH), BF),
        key_ext=v((LEN, 128), BF),
        query_ext=v((LEN, 128), BF),
        stat=v((TOK, 128), F32),
        hat1=v((TOK, WIDTH), F32),
        fac1=v((TOK, 1), F32),
        attended_full=v((TOK, WIDTH), F32),
        attended=v((2 * TOK, WIDTH), BF),
        resid=v((TOK, WIDTH), F32),
        hat2=v((TOK, WIDTH), F32),
        fac2=v((TOK, 1), F32),
        mlp_in=v((2 * TOK, WIDTH), BF),
        cot2=v((2 * TOK, WIDTH), BF),
        hidden_grad=v((2 * TOK, HALF), F32),
        hidden=v((2 * TOK, HALF), BF),
        up_low=v((2 * TOK, HALF), BF),
        mlp_part=v((2 * TOK, WIDTH), F32),
        mlp_came=v((TOK, WIDTH), F32),
        out_part=v((2 * TOK, WIDTH), F32),
        out_came=v((TOK, WIDTH), F32),
        resid_grad=v((TOK, WIDTH), F32),
        resid_low=v((TOK, WIDTH), BF),
        attended_grad=v((LEN, WIDTH), BF),
        qkv_low=v((TOK, 3 * WIDTH), BF),
        resid_half=v((2 * TOK, 384), BF),
        query_half=v((2 * TOK, 384), BF),
        keys_half=v((2 * TOK, WIDTH), BF),
        key_grad=v((TOK, WIDTH), F32),
        value_grad=v((TOK, WIDTH), F32),
        attn_grad=v((TOK, WIDTH), F32),
        vec=v((16, WIDTH), F32),
        vec_came=v((DIMS + 1, 16, WIDTH), F32),
        grads_wide=v((2, WIDTH, HALF), BF),
        grads_slim=v((2, WIDTH, WIDTH), BF),
        landing_wide=v((2, DIMS, 144, HALF), BF),
        landing_slim=v((2, DIMS, 144, WIDTH), BF),
        send_sem=dma((sets, DIMS, STEPS + 2)),
        recv_sem=dma((sets, DIMS, STEPS + 2)),
        side_send=dma((18,)),
        side_recv=dma((18,)),
        vec_send=dma((DIMS + 1,)),
        vec_recv=dma((DIMS + 1,)),
        load_sem=dma((4,)),
    )


NAMES = tuple(scratch())


def kernel(
    lengths,
    order,
    x,
    cot,
    attn_gain,
    attn_shift,
    query_bias,
    value_bias,
    proj_bias,
    mlp_gain,
    mlp_shift,
    up_bias,
    down_bias,
    qkv_weight,
    proj_weight,
    up_weight,
    down_weight,
    block_output,
    input_grad,
    whole_wide,
    whole_slim,
    vec_out,
    *refs,
):
    m = SimpleNamespace(**dict(zip(NAMES, refs)))
    at = place()
    core, seq = at.core, at.seq
    pair_of = lambda wide, slim: (wide.at[0], wide.at[1], slim.at[0], slim.at[1])
    grads = pair_of(m.grads_wide, m.grads_slim)
    ex = Exchange(
        at,
        grads,
        pair_of(whole_wide, whole_slim),
        pair_of(m.landing_wide, m.landing_slim),
        m.send_sem,
        m.recv_sem,
    )

    barrier = pltpu.get_barrier_semaphore()
    for device in at.partners + (at.sibling, at.across):
        pl.semaphore_signal(barrier, inc=1, device_id=device, device_id_type=MESH)

    loads = [
        pltpu.make_async_copy(src, dst, m.load_sem.at[i])
        for i, (src, dst) in enumerate(
            (
                (qkv_weight, m.qkv_w),
                (down_weight.at[rows_of(core * HALF, HALF)], m.down_w),
                (proj_weight, m.proj_w),
                (up_weight.at[:, rows_of(core * HALF, HALF)], m.up_w),
            )
        )
    ]
    for load in loads:
        load.start()

    def side(i, src, dst, device):
        copy = pltpu.make_async_remote_copy(
            src_ref=src,
            dst_ref=dst,
            send_sem=m.side_send.at[i],
            recv_sem=m.side_recv.at[i],
            device_id=device,
            device_id_type=MESH,
        )
        copy.start()
        return copy

    own = rows_of(seq * TOK, TOK)
    two = rows_of(core * TOK, TOK)
    two_other = rows_of((1 - core) * TOK, TOK)
    far = rows_of(((1 - at.chip) * 2 + core) * TOK, TOK)
    chip_rows = lambda chip: rows_of(chip * 2 * TOK, 2 * TOK)
    cut = lambda start, size: pl.ds(pl.multiple_of(start, 128), size)

    vectors = (attn_gain, attn_shift, query_bias, value_bias, proj_bias, mlp_gain, mlp_shift, down_bias)
    for i, vector in enumerate(vectors):
        m.lines[i : i + 1, :] = vector[...][None]
    attn_gain, attn_shift, query_bias, value_bias, proj_bias, mlp_gain, mlp_shift, down_bias = (
        m.lines.at[i : i + 1] for i in range(8)
    )

    normalize(
        lambda rows: x[0, rows, :].astype(F32), attn_gain, attn_shift, m.hat1, m.fac1, m.normed_in, seq * TOK
    )
    m.cot2[two, :] = cot[0]

    pl.semaphore_wait(barrier, DIMS + 2)
    in_far = side(1, m.normed_in.at[own], m.normed_in.at[own], at.across)
    in_sib = side(0, m.normed_in.at[own], m.normed_in.at[own], at.sibling)
    cot_sib = side(3, m.cot2.at[two], m.cot2.at[two], at.sibling)

    ends = [lengths[0, 0]]
    for i in (1, 2):
        ends.append(ends[-1] + lengths[0, i])
    lane = lax.broadcasted_iota(jnp.int32, (1, 128), 1)
    token = lax.broadcasted_iota(jnp.int32, (TOK, 128), 0)

    def image(j):
        t = token + order[0, j] * TOK
        return sum((t >= end).astype(jnp.int32) for end in ends)

    for j in range(4):
        other = jnp.where(lane == image(j), 0.0, -1e30)
        m.key_ext[j * TOK : (j + 1) * TOK, :] = jnp.where(lane < 4, other, jnp.where(lane < 76, 1.0, 0.0)).astype(BF)
    image_own = jnp.where(lane == image(seq), 1.0, 0.0)
    m.query_ext[own, :] = image_own.astype(BF)
    m.up_bias_half[...] = jnp.where(core == 0, up_bias[:HALF], up_bias[HALF:])[None]
    m.vec[...] = jnp.zeros((16, WIDTH), F32)
    m.vec[7:8, :] = jnp.sum(
        jnp.sum(cot[0].astype(F32).reshape(TOK // 8, 8, WIDTH), axis=0), axis=0, keepdims=True
    )
    m.stat[...] = jnp.zeros((TOK, 128), F32)
    low_lanes = (lane < 64).astype(BF)
    high_lanes = (lane >= 64).astype(BF)

    def both(v):
        return jnp.concatenate((v * low_lanes, v * high_lanes), axis=0)

    def joined(v):
        return jnp.where(lane < 64, v[:TOK], v[TOK:])

    def beside(a, b):
        return jnp.concatenate((a, b), axis=1)

    def project(chip):
        rows = chip_rows(chip)
        a = m.normed_in[rows, :]
        m.keys[rows, :] = dot(a, m.qkv_w[:, WIDTH : 2 * WIDTH]).astype(BF)
        m.values[rows, :] = (dot(a, m.qkv_w[:, 2 * WIDTH :]) + value_bias[...]).astype(BF)
        m.queries[rows, :] = ((dot(a, m.qkv_w[:, :WIDTH]) + query_bias[...]) * SCALE).astype(BF)

    loads[0].wait()
    in_sib.wait()
    project(at.chip)
    loads[1].wait()
    cot_sib.wait()
    m.hidden_grad[...] = dot_rt(m.cot2[...], m.down_w[...])
    in_far.wait()
    in_pass = side(2, m.normed_in.at[far], m.normed_in.at[far], at.sibling)
    in_pass.wait()
    project(1 - at.chip)

    def attend(i, carry):
        cols = rows_of(i * 128, 128)
        ext = m.query_ext[own, :]
        s = dot_rt(
            beside(both(m.queries[own, cols]), jnp.concatenate((ext, ext), axis=0)),
            beside(m.keys[:, cols], m.key_ext[...]),
        )
        top = jnp.max(s, axis=1, keepdims=True)
        e = jnp.exp(s - top).astype(BF)
        out = dot(e, beside(m.values[:, cols], jnp.ones((LEN, 128), BF)))
        total = out[:, 128:]
        out = joined(out[:, :128] * (1.0 / total))
        m.attended_full[:, cols] = out
        m.attended[two, cols] = out.astype(BF)
        logs = top + jnp.log(total)
        m.stat[...] = jnp.where(
            lane == 2 * i, logs[:TOK], jnp.where(lane == 2 * i + 1, logs[TOK:], m.stat[...])
        )
        return carry

    lax.fori_loop(0, PAIRS, attend, 0, unroll=True)

    loads[2].wait()
    m.resid[...] = x[0].astype(F32) + dot(m.attended[two, :], m.proj_w[...]) + proj_bias[...]
    normalize(lambda rows: m.resid[rows, :], mlp_gain, mlp_shift, m.hat2, m.fac2, m.mlp_in, core * TOK)
    mlp_sib = side(4, m.mlp_in.at[two], m.mlp_in.at[two], at.sibling)
    att_sib = side(5, m.attended.at[two], m.attended.at[two], at.sibling)
    loads[3].wait()
    mlp_sib.wait()

    def feed(i, carry):
        cols = rows_of(i * 512, 512)
        u = dot(m.mlp_in[...], m.up_w[:, cols]) + m.up_bias_half[:, cols]
        t = 1.0 / (1.0 + 0.36 * jnp.abs(u))
        tail = jnp.full_like(t, TAIL[-1])
        for c in TAIL[-2::-1]:
            tail = tail * t + c
        e = jnp.exp(-0.5 * (u * u))
        tail = tail * (t * e)
        phi = jnp.where(u >= 0, 1.0 - tail, tail)
        m.hidden[:, cols] = (u * phi).astype(BF)
        g = m.hidden_grad[:, cols] * (phi + u * (DENSITY * e))
        m.up_low[:, cols] = g.astype(BF)
        m.up_bias_half[:, cols] = jnp.sum(
            jnp.sum(g.reshape(2 * TOK // 8, 8, 512), axis=0), axis=0, keepdims=True
        )
        return carry

    lax.fori_loop(0, HALF // 512, feed, 0)

    def block_of(k):
        return slice(k * TOK, (k + 1) * TOK)

    def start_up(ks):
        for k in ks:
            grads[UP][block_of(k), :] = dot_lt(m.mlp_in[:, block_of(k)], m.up_low[...]).astype(BF)
            ex.start(UP, k)

    for k in range(DIMS):
        for h in range(2):
            first = h * WIDTH + k * TOK
            grads[DOWN][block_of(k), h * WIDTH : (h + 1) * WIDTH] = dot_lt(
                m.hidden[:, first : first + TOK], m.cot2[...]
            ).astype(BF)
        ex.start(DOWN, k)
    m.mlp_part[...] = dot_rt(m.up_low[...], m.up_w[...])
    part_sib = side(6, m.mlp_part.at[two_other], m.mlp_came, at.sibling)
    start_up(range(4))
    for h in range(2):
        for t in range(2):
            m.vec[8 + 2 * h + t : 9 + 2 * h + t, :] = jnp.where(
                core == h, m.up_bias_half[:, t * WIDTH : (t + 1) * WIDTH], 0.0
            )
    part_sib.wait()

    def keep_resid(rows, back):
        m.resid_grad[rows, :] = back
        m.resid_low[rows, :] = back.astype(BF)

    norm_back(
        lambda rows: m.mlp_part[rows_of_shift(rows, core * TOK), :] + m.mlp_came[rows, :],
        lambda rows: cot[0, rows, :].astype(F32),
        mlp_gain,
        m.hat2,
        m.fac2,
        m.vec,
        (5, 6, 4),
        keep_resid,
    )
    back = dot_rt(m.resid_low[...], m.proj_w[...]).astype(BF)
    m.attended_grad[own, :] = back
    grad_far = side(9, m.attended_grad.at[own], m.attended_grad.at[own], at.across)
    grad_sib = side(8, m.attended_grad.at[own], m.attended_grad.at[own], at.sibling)

    def parts(v):
        found = []
        for _ in range(3):
            found.append(v.astype(BF))
            v = v - found[-1].astype(F32)
        return found

    feature = lax.broadcasted_iota(jnp.int32, (WIDTH, 128), 0)
    head_of = (feature // 64 + 16 == lax.broadcasted_iota(jnp.int32, (WIDTH, 128), 1)).astype(BF)
    sums = sum(dot(p, head_of) for p in parts(back.astype(F32) * m.attended_full[...]))
    ext = image_own
    for j, p in enumerate(parts(-(m.stat[...] + sums))):
        to = lax.broadcasted_iota(jnp.int32, (128, 128), 1)
        of = lax.broadcasted_iota(jnp.int32, (128, 128), 0)
        spot = jnp.where(of < 12, 4 + 3 * of + j, jnp.where((of >= 16) & (of < 28), 3 * of - 8 + j, -1))
        ext = ext + dot(p, (to == spot).astype(BF))
    m.query_ext[own, :] = ext.astype(BF)
    ext_far = side(12, m.query_ext.at[own], m.query_ext.at[own], at.across)
    ext_sib = side(11, m.query_ext.at[own], m.query_ext.at[own], at.sibling)
    start_up(range(4, DIMS))
    m.resid_half[two, :] = m.resid_low[:, cut(core * 384, 384)]
    resid_sib = side(14, m.resid_low.at[:, cut((1 - core) * 384, 384)], m.resid_half.at[two], at.sibling)

    def picks(i):
        a, b = lane - 4 - 6 * i, lane - 40 - 6 * i
        first = jnp.where((lane < 4) | ((a >= 0) & (a < 3)), 1.0, 0.0).astype(BF)
        second = jnp.where((lane < 4) | ((a >= 3) & (a < 6)), 1.0, 0.0).astype(BF)
        third = jnp.where((b >= 0) & (b < 3), 1.0, 0.0).astype(BF)
        fourth = jnp.where((b >= 3) & (b < 6), 1.0, 0.0).astype(BF)
        return (lambda v: jnp.concatenate((v * first, v * second), axis=0)), (
            lambda v: jnp.concatenate((v * third, v * fourth), axis=0)
        )

    def query_side(i, carry):
        cols = rows_of(i * 128, 128)
        of_scores, of_means = picks(i)
        ext, k = m.query_ext[own, :], m.keys[:, cols]
        p = jnp.exp(
            dot_rt(beside(both(m.queries[own, cols]), of_scores(ext)), beside(k, m.key_ext[...]))
        )
        y = dot_rt(
            beside(both(m.attended_grad[own, cols]), of_means(ext)),
            beside(m.values[:, cols], m.key_ext[...]),
        )
        g = joined(dot((p * y).astype(BF), k)) * SCALE
        m.vec[2:3, cols] = jnp.sum(g, axis=0, keepdims=True)
        m.qkv_low[:, cols] = g.astype(BF)
        return carry

    def key_side(chip, first):
        rows = chip_rows(chip)

        def step(i, carry):
            cols = rows_of(i * 128, 128)
            of_scores, of_means = picks(i)
            q, g, ext = m.queries[rows, cols], m.attended_grad[rows, cols], m.key_ext[own, :]
            other = m.query_ext[rows, :]
            p = jnp.exp(dot_rt(beside(both(m.keys[own, cols]), of_scores(ext)), beside(q, other)))
            y = dot_rt(beside(both(m.values[own, cols]), of_means(ext)), beside(g, other))
            dv = joined(dot(p.astype(BF), g))
            dk = joined(dot((p * y).astype(BF), q))
            if first:
                m.value_grad[:, cols] = dv
                m.key_grad[:, cols] = dk
            else:
                dv = dv + m.value_grad[:, cols]
                dk = dk + m.key_grad[:, cols]
                m.vec[3:4, cols] = jnp.sum(dv, axis=0, keepdims=True)
                m.qkv_low[:, cut(WIDTH + i * 128, 128)] = dk.astype(BF)
                m.qkv_low[:, cut(2 * WIDTH + i * 128, 128)] = dv.astype(BF)
            return carry

        lax.fori_loop(0, PAIRS, step, 0, unroll=3)

    def share(i, part, target):
        target.at[two][...] = m.qkv_low[:, cut(part * WIDTH + core * 384, 384)]
        return side(
            i, m.qkv_low.at[:, cut(part * WIDTH + (1 - core) * 384, 384)], target.at[two], at.sibling
        )

    lax.fori_loop(0, PAIRS, query_side, 0, unroll=3)
    query_sib = share(15, 0, m.query_half)
    ex.finish(DOWN, 0)
    grad_sib.wait()
    ext_sib.wait()
    key_side(at.chip, True)
    att_sib.wait()
    resid_sib.wait()
    query_sib.wait()
    for k in range(DIMS):
        grads[PROJ][block_of(k), :384] = dot_lt(m.attended[:, block_of(k)], m.resid_half[...]).astype(BF)
        grads[PROJ][block_of(k), 384:] = dot_lt(
            m.normed_in[chip_rows(at.chip), block_of(k)], m.query_half[...]
        ).astype(BF)
        ex.start(PROJ, k)
    ex.finish(DOWN, 1)
    grad_far.wait()
    grad_pass = side(10, m.attended_grad.at[far], m.attended_grad.at[far], at.sibling)
    ext_far.wait()
    ext_pass = side(13, m.query_ext.at[far], m.query_ext.at[far], at.sibling)
    ex.finish(UP, 0)
    grad_pass.wait()
    ext_pass.wait()
    key_side(1 - at.chip, False)
    key_sib = share(16, 1, m.keys_half.at[:, :384])
    value_sib = share(17, 2, m.keys_half.at[:, 384:])
    ex.finish(DOWN, 2)
    key_sib.wait()
    value_sib.wait()
    for k in range(DIMS):
        grads[KEYS][block_of(k), :] = dot_lt(
            m.normed_in[chip_rows(at.chip), block_of(k)], m.keys_half[...]
        ).astype(BF)
        ex.start(KEYS, k)
    ex.finish(PROJ, 0)
    ex.finish(UP, 1)
    ex.finish(DOWN, 3)

    m.attn_grad[...] = dot_rt(m.qkv_low[...], m.qkv_w[...])

    def keep_input(rows, back):
        input_grad[0, rows, :] = back.astype(BF)

    norm_back(
        lambda rows: m.attn_grad[rows, :],
        lambda rows: m.resid_grad[rows, :],
        attn_gain,
        m.hat1,
        m.fac1,
        m.vec,
        (0, 1),
        keep_input,
    )

    def vec_start(s):
        copy = pltpu.make_async_remote_copy(
            src_ref=m.vec,
            dst_ref=m.vec_came.at[s],
            send_sem=m.vec_send.at[s],
            recv_sem=m.vec_recv.at[s],
            device_id=(at.partners + (at.sibling,))[s],
            device_id_type=MESH,
        )
        copy.start()
        return copy

    vec_copy = [vec_start(0)]

    def vec_finish(s):
        vec_copy[0].wait()
        m.vec[...] = m.vec[...] + m.vec_came[s]
        if s < DIMS:
            vec_copy[0] = vec_start(s + 1)
        else:
            vec_out[...] = m.vec[...]

    ex.finish(PROJ, 1)
    ex.finish(KEYS, 0)
    m.out_part[...] = dot(m.hidden[...], m.down_w[...])
    out_sib = side(7, m.out_part.at[two_other], m.out_came, at.sibling)
    ex.finish(UP, 2)
    ex.finish(PROJ, 2)
    ex.finish(DOWN, 4)
    out_sib.wait()
    block_output[0] = (
        m.resid[...] + (m.out_part[two, :] + m.out_came[...]) + down_bias[...]
    ).astype(BF)

    for n, (w, s) in enumerate(LAST):
        ex.finish(w, s)
        if n % 3 == 0 and n // 3 <= DIMS:
            vec_finish(n // 3)

    for w in range(len(WIDTHS)):
        for k in range(DIMS):
            for part in range(2):
                ex.copies[w, k, STEPS + part].wait()


LAST = (
    (KEYS, 1), (PROJ, 3), (UP, 3), (DOWN, 5), (KEYS, 2), (PROJ, 4), (UP, 4),
    (DOWN, 6), (KEYS, 3), (PROJ, 5), (UP, 5), (PROJ, 6), (KEYS, 4), (UP, 6),
    (DOWN, 7), (PROJ, 7), (KEYS, 5), (UP, 7), (DOWN, 8), (KEYS, 6), (PROJ, 8),
    (UP, 8), (KEYS, 7), (DOWN, 9), (KEYS, 8), (PROJ, 9), (UP, 9), (KEYS, 9),
)


def rows_of_shift(rows, shift):
    return pl.ds(pl.multiple_of(rows.start + shift, 16), rows.size)


def spread_kernel(
    wide,
    slim,
    vec,
    block_output_in,
    input_grad_in,
    block_output,
    input_grad,
    attn_gain,
    attn_shift,
    qkv,
    query_bias,
    value_bias,
    proj,
    proj_bias,
    mlp_gain,
    mlp_shift,
    up,
    up_bias,
    down,
    down_bias,
):
    rows = rows_of(pl.program_id(0) * SPREAD_ROWS, SPREAD_ROWS)
    for c in range(2):
        up[:, c * HALF : (c + 1) * HALF] = wide[1, c, rows, :].astype(F32)
        proj[:, c * 384 : (c + 1) * 384] = slim[0, c, rows, :384].astype(F32)
        for part in range(3):
            first = part * WIDTH + c * 384
            source = slim[0, c, rows, 384:] if part == 0 else slim[1, c, rows, (part - 1) * 384 : part * 384]
            qkv[:, first : first + 384] = source.astype(F32)
        for h in range(2):
            down[2 * c + h] = wide[0, c, rows, h * WIDTH : (h + 1) * WIDTH].astype(F32)

    @pl.when(pl.program_id(0) == 0)
    def _():
        block_output[...] = block_output_in[...]
        input_grad[...] = input_grad_in[...]
        for row, ref in enumerate(
            (attn_gain, attn_shift, query_bias, value_bias, proj_bias, mlp_gain, mlp_shift, down_bias)
        ):
            ref[...] = vec[row]
        for t in range(4):
            up_bias[t * WIDTH : (t + 1) * WIDTH] = vec[8 + t]


SPREAD_ROWS = 64


def spread(*given):
    rows = SPREAD_ROWS
    line = lambda n: (jax.ShapeDtypeStruct((n,), F32), pl.BlockSpec((n,), lambda i: (0,)))
    flat = lambda n: (jax.ShapeDtypeStruct((WIDTH, n), F32), pl.BlockSpec((rows, n), lambda i: (i, 0)))
    tokens = (jax.ShapeDtypeStruct((1, TOK, WIDTH), BF), pl.BlockSpec((1, TOK, WIDTH), lambda i: (0, 0, 0)))
    outs = [
        tokens,
        tokens,
        line(WIDTH),
        line(WIDTH),
        flat(3 * WIDTH),
        line(WIDTH),
        line(WIDTH),
        flat(WIDTH),
        line(WIDTH),
        line(WIDTH),
        line(WIDTH),
        flat(HIDDEN),
        line(HIDDEN),
        (
            jax.ShapeDtypeStruct((4, WIDTH, WIDTH), F32),
            pl.BlockSpec((4, rows, WIDTH), lambda i: (0, i, 0)),
        ),
        line(WIDTH),
    ]
    return pl.pallas_call(
        spread_kernel,
        grid=(WIDTH // rows,),
        out_shape=[o[0] for o in outs],
        in_specs=[pl.BlockSpec(memory_space=pltpu.VMEM)] * len(given),
        out_specs=[o[1] for o in outs],
        compiler_params=pltpu.CompilerParams(vmem_limit_bytes=24 << 20),
    )(*(pltpu.with_memory_space_constraint(v, pltpu.VMEM) for v in given))


def body(
    block_input,
    out_cotangent,
    image_lengths,
    span_order,
    attn_gain,
    attn_shift,
    qkv_weight,
    query_bias,
    value_bias,
    proj_weight,
    proj_bias,
    mlp_gain,
    mlp_shift,
    up_weight,
    up_bias,
    down_weight,
    down_bias,
):
    vmem = pl.BlockSpec(memory_space=pltpu.VMEM)
    smem = pl.BlockSpec(memory_space=pltpu.SMEM)
    hbm = pl.BlockSpec(memory_space=pl.ANY)
    held = scratch()
    block_output, input_grad, wide, slim, vec = pl.pallas_call(
        kernel,
        out_shape=[
            pltpu.VMEM((1, TOK, WIDTH), BF),
            pltpu.VMEM((1, TOK, WIDTH), BF),
            pltpu.VMEM((2, 2, WIDTH, HALF), BF),
            pltpu.VMEM((2, 2, WIDTH, WIDTH), BF),
            pltpu.VMEM((16, WIDTH), F32),
        ],
        in_specs=[smem, smem] + [vmem] * 11 + [hbm] * 4,
        out_specs=[vmem] * 5,
        scratch_shapes=[held[name] for name in NAMES],
        compiler_params=pltpu.CompilerParams(
            collective_id=0, has_side_effects=True, vmem_limit_bytes=VMEM_LIMIT
        ),
    )(
        image_lengths,
        span_order,
        block_input,
        out_cotangent,
        attn_gain,
        attn_shift,
        query_bias,
        value_bias,
        proj_bias,
        mlp_gain,
        mlp_shift,
        up_bias,
        down_bias,
        qkv_weight,
        proj_weight,
        up_weight,
        down_weight,
    )
    outs = list(spread(wide, slim, vec, block_output, input_grad))
    outs[13] = outs[13].reshape(HIDDEN, WIDTH)
    return tuple(outs)


VMEM_LIMIT = 46 << 20


def solution(mesh):
    tokens = P("rows", "seq", None)
    return jax.shard_map(
        body,
        mesh=mesh,
        in_specs=(tokens, tokens, P("rows", None), P("rows", None)) + (P(),) * 13,
        out_specs=(tokens, tokens) + (P(),) * 13,
        check_vma=False,
    )
```

```python
from types import SimpleNamespace

import jax
import jax.numpy as jnp
from jax import lax
from jax.experimental import pallas as pl
from jax.experimental.pallas import tpu as pltpu
from jax.sharding import PartitionSpec as P

MESH = pl.DeviceIdType.MESH
BF, F32 = jnp.bfloat16, jnp.float32
WIDTH = 768
HIDDEN = 3072
HALF = HIDDEN // 2
TOK = 128
LEN = 512
PAIRS = 6
SCALE = 64**-0.5
EPSILON = 1e-6

DIMS = 6
STEPS = 10
DOWN, UP, PROJ, KEYS = range(4)
WIDTHS = (HALF, HALF, WIDTH, WIDTH)

TAIL = (
    0.14361835615286447,
    0.14366105191010822,
    0.12424683572786965,
    0.09467827005043768,
    0.003990377379362003,
    0.09912410558005538,
    -0.21460327937017376,
    0.13425173188400444,
    -0.02896737861797067,
)
DENSITY = 0.3989422804014327


def rows_of(start, size):
    return pl.ds(pl.multiple_of(start, size), size)


def dot(a, b):
    return lax.dot_general(a, b, (((1,), (0,)), ((), ())), preferred_element_type=F32)


def dot_rt(a, b):
    return lax.dot_general(a, b, (((1,), (1,)), ((), ())), preferred_element_type=F32)


def dot_lt(a, b):
    return lax.dot_general(a, b, (((0,), (0,)), ((), ())), preferred_element_type=F32)


def place():
    row, seq = lax.axis_index("rows"), lax.axis_index("seq")
    x, y, z_lo = row % 4, (row // 4) % 4, row // 16
    z_hi, core = seq // 2, seq % 2
    z = z_hi * 2 + z_lo

    def device(x, y, z, core):
        return ((z % 2) * 16 + y * 4 + x, (z // 2) * 2 + core)

    near = lambda v: v + 1 - 2 * (v % 2)
    far = lambda v: 3 - v
    first = lambda v: (v % 2 + v // 2) % 2
    return SimpleNamespace(
        seq=seq,
        core=core,
        chip=z_hi,
        partners=(
            device(near(x), y, z, core),
            device(far(x), y, z, core),
            device(x, near(y), z, core),
            device(x, far(y), z, core),
            device(x, y, near(z), core),
            device(x, y, far(z), core),
        ),
        bits=(first(x), x // 2, first(y), y // 2, first(z), z // 2),
        sibling=(row, z_hi * 2 + 1 - core),
        across=(row, (1 - z_hi) * 2 + core),
    )


class Exchange:
    def __init__(self, at, grads, whole, landing, send_sem, recv_sem, over_sem):
        self.at = at
        self.grads, self.whole, self.landing = grads, whole, landing
        self.send_sem, self.recv_sem, self.over_sem = send_sem, recv_sem, over_sem
        self.copies = {}

    def dim(self, k, s):
        return (k + s) % DIMS

    def rows(self, k, s):
        low = TOK * k
        for t in range(min(s, 3)):
            low = low + self.at.bits[self.dim(k, t)] * (64 >> t)
        return low

    def block(self, w, k, s, mine, whole=False):
        held = self.whole[w].at[self.at.core] if whole else self.grads[w]
        bit = self.at.bits[self.dim(k, s)]
        pick = bit if mine else 1 - bit
        if s < 3:
            size = 64 >> s
            return held.at[pl.ds(pl.multiple_of(self.rows(k, s) + pick * size, 16), size)]
        width = WIDTHS[w] // 2
        return held.at[
            pl.ds(pl.multiple_of(self.rows(k, 3), 16), 16),
            pl.ds(pl.multiple_of(pick * width, 128), width),
        ]

    def slot(self, w, k, s):
        if s < 3:
            return self.landing[w].at[k, pl.ds((0, 64, 96)[s], 64 >> s)]
        width = WIDTHS[w] // 2
        return self.landing[w].at[k, pl.ds((112, 112, 128)[s - 3], 16), pl.ds((0, width, 0)[s - 3], width)]

    def start(self, w, k, s=0):
        if s < 4:
            src, dst, d = self.block(w, k, s, False), self.slot(w, k, s), self.dim(k, s)
        elif s < 6:
            src, dst, d = self.block(w, k, 3, True), self.slot(w, k, s), self.dim(k, s)
        else:
            src = dst = self.block(w, k, 9 - s, True, True)
            d = self.dim(k, 9 - s)
        copy = pltpu.make_async_remote_copy(
            src_ref=src,
            dst_ref=dst,
            send_sem=self.send_sem.at[w, k],
            recv_sem=self.recv_sem.at[w, k, s],
            device_id=self.at.partners[d],
            device_id_type=MESH,
        )
        copy.start()
        self.copies[w, k, s] = copy

    def over(self, w, k, part):
        half = self.block(w, k, 0, part == 0, True)
        self.crossing(w, half, half).start()

    def crossing(self, w, src, dst):
        return pltpu.make_async_remote_copy(
            src_ref=src,
            dst_ref=dst,
            send_sem=self.over_sem.at[0, w],
            recv_sem=self.over_sem.at[1, w],
            device_id=self.at.sibling,
            device_id_type=MESH,
        )

    def done(self, w):
        self.crossing(w, self.whole[w].at[self.at.core], self.whole[w].at[1 - self.at.core]).wait()

    def finish(self, w, k, s):
        self.copies[w, k, s].wait()
        if s < 6:
            kept, slot = self.block(w, k, min(s, 3), True), self.slot(w, k, s)
            total = (kept[...].astype(F32) + slot[...].astype(F32)).astype(BF)
            if s < 5:
                kept[...] = total
            else:
                self.block(w, k, 3, True, True)[...] = total
        if s < STEPS - 1:
            self.start(w, k, s + 1)
        if s >= STEPS - 2:
            self.over(w, k, s - (STEPS - 2))


def normalize(load, gain, shift, normed, factor, result, base):
    def step(i, carry):
        rows = rows_of(i * 16, 16)
        v = load(rows)
        c = v - jnp.mean(v, axis=1, keepdims=True)
        f = lax.rsqrt(jnp.mean(c * c, axis=1, keepdims=True) + EPSILON)
        n = c * f
        normed[rows, :] = n
        factor[rows, :] = f
        result[rows_of(base + i * 16, 16), :] = (n * gain[...] + shift[...]).astype(BF)
        return carry

    lax.fori_loop(0, TOK // 16, step, 0, unroll=True)


def folded(v):
    return jnp.sum(v.reshape(2, 8, WIDTH), axis=0)


def norm_back(load_grad, load_rest, gain, normed, factor, vec, where, keep):
    zero = jnp.zeros((8, WIDTH), F32)

    def step(i, carry):
        rows = rows_of(i * 16, 16)
        e, n = load_grad(rows), normed[rows, :]
        g = e * gain[...]
        a = jnp.mean(g, axis=1, keepdims=True)
        b = jnp.mean(g * n, axis=1, keepdims=True)
        back = load_rest(rows) + factor[rows, :] * (g - a - n * b)
        keep(rows, back)
        return carry[0] + folded(e * n), carry[1] + folded(e), carry[2] + folded(back)

    sums = lax.fori_loop(0, TOK // 16, step, (zero, zero, zero), unroll=True)
    for row, total in zip(where, sums):
        vec[row : row + 1, :] = jnp.sum(total, axis=0, keepdims=True)


def scratch():
    v = pltpu.VMEM
    dma = pltpu.SemaphoreType.DMA
    sets = len(WIDTHS)
    return dict(
        qkv_w=v((WIDTH, 3 * WIDTH), BF),
        proj_w=v((WIDTH, WIDTH), BF),
        up_w=v((WIDTH, HALF), BF),
        down_w=v((HALF, WIDTH), BF),
        lines=v((8, WIDTH), F32),
        up_bias_half=v((1, HALF), F32),
        normed_in=v((LEN, WIDTH), BF),
        queries=v((LEN, WIDTH), BF),
        keys=v((LEN, WIDTH), BF),
        values=v((LEN, WIDTH), BF),
        key_ext=v((LEN, 128), BF),
        query_ext=v((LEN, 128), BF),
        stat=v((TOK, 128), F32),
        hat1=v((TOK, WIDTH), F32),
        fac1=v((TOK, 1), F32),
        attended_full=v((TOK, WIDTH), F32),
        attended=v((2 * TOK, WIDTH), BF),
        resid=v((TOK, WIDTH), F32),
        hat2=v((TOK, WIDTH), F32),
        fac2=v((TOK, 1), F32),
        mlp_in=v((2 * TOK, WIDTH), BF),
        cot2=v((2 * TOK, WIDTH), BF),
        hidden_grad=v((2 * TOK, HALF), F32),
        hidden=v((2 * TOK, HALF), BF),
        up_low=v((2 * TOK, HALF), BF),
        mlp_part=v((2 * TOK, WIDTH), F32),
        mlp_came=v((TOK, WIDTH), F32),
        out_part=v((2 * TOK, WIDTH), F32),
        out_came=v((TOK, WIDTH), F32),
        resid_grad=v((TOK, WIDTH), F32),
        resid_low=v((TOK, WIDTH), BF),
        attended_grad=v((LEN, WIDTH), BF),
        qkv_low=v((TOK, 3 * WIDTH), BF),
        resid_half=v((2 * TOK, 384), BF),
        query_half=v((2 * TOK, 384), BF),
        keys_half=v((2 * TOK, WIDTH), BF),
        key_grad=v((TOK, WIDTH), F32),
        value_grad=v((TOK, WIDTH), F32),
        attn_grad=v((TOK, WIDTH), F32),
        vec=v((16, WIDTH), F32),
        vec_came=v((DIMS + 1, 16, WIDTH), F32),
        grads_wide=v((2, WIDTH, HALF), BF),
        grads_slim=v((2, WIDTH, WIDTH), BF),
        landing_wide=v((2, DIMS, 144, HALF), BF),
        landing_slim=v((2, DIMS, 144, WIDTH), BF),
        send_sem=dma((sets, DIMS)),
        recv_sem=dma((sets, DIMS, STEPS)),
        over_sem=dma((2, sets)),
        side_send=dma((18,)),
        side_recv=dma((18,)),
        vec_send=dma((DIMS + 1,)),
        vec_recv=dma((DIMS + 1,)),
        load_sem=dma((4,)),
    )


NAMES = tuple(scratch())


def kernel(
    lengths,
    order,
    x,
    cot,
    attn_gain,
    attn_shift,
    query_bias,
    value_bias,
    proj_bias,
    mlp_gain,
    mlp_shift,
    up_bias,
    down_bias,
    qkv_weight,
    proj_weight,
    up_weight,
    down_weight,
    block_output,
    input_grad,
    whole_wide,
    whole_slim,
    vec_out,
    *refs,
):
    m = SimpleNamespace(**dict(zip(NAMES, refs)))
    at = place()
    core, seq = at.core, at.seq
    pair_of = lambda wide, slim: (wide.at[0], wide.at[1], slim.at[0], slim.at[1])
    grads = pair_of(m.grads_wide, m.grads_slim)
    ex = Exchange(
        at,
        grads,
        pair_of(whole_wide, whole_slim),
        pair_of(m.landing_wide, m.landing_slim),
        m.send_sem,
        m.recv_sem,
        m.over_sem,
    )

    barrier = pltpu.get_barrier_semaphore()
    for device in at.partners + (at.sibling, at.across):
        pl.semaphore_signal(barrier, inc=1, device_id=device, device_id_type=MESH)

    loads = [
        pltpu.make_async_copy(src, dst, m.load_sem.at[i])
        for i, (src, dst) in enumerate(
            (
                (qkv_weight, m.qkv_w),
                (down_weight.at[rows_of(core * HALF, HALF)], m.down_w),
                (proj_weight, m.proj_w),
                (up_weight.at[:, rows_of(core * HALF, HALF)], m.up_w),
            )
        )
    ]
    for load in loads:
        load.start()

    def side(i, src, dst, device):
        copy = pltpu.make_async_remote_copy(
            src_ref=src,
            dst_ref=dst,
            send_sem=m.side_send.at[i],
            recv_sem=m.side_recv.at[i],
            device_id=device,
            device_id_type=MESH,
        )
        copy.start()
        return copy

    own = rows_of(seq * TOK, TOK)
    two = rows_of(core * TOK, TOK)
    two_other = rows_of((1 - core) * TOK, TOK)
    far = rows_of(((1 - at.chip) * 2 + core) * TOK, TOK)
    chip_rows = lambda chip: rows_of(chip * 2 * TOK, 2 * TOK)
    cut = lambda start, size: pl.ds(pl.multiple_of(start, 128), size)

    vectors = (attn_gain, attn_shift, query_bias, value_bias, proj_bias, mlp_gain, mlp_shift, down_bias)
    for i, vector in enumerate(vectors):
        m.lines[i : i + 1, :] = vector[...][None]
    attn_gain, attn_shift, query_bias, value_bias, proj_bias, mlp_gain, mlp_shift, down_bias = (
        m.lines.at[i : i + 1] for i in range(8)
    )

    normalize(
        lambda rows: x[0, rows, :].astype(F32), attn_gain, attn_shift, m.hat1, m.fac1, m.normed_in, seq * TOK
    )
    m.cot2[two, :] = cot[0]

    pl.semaphore_wait(barrier, DIMS + 2)
    in_far = side(1, m.normed_in.at[own], m.normed_in.at[own], at.across)
    in_sib = side(0, m.normed_in.at[own], m.normed_in.at[own], at.sibling)
    cot_sib = side(3, m.cot2.at[two], m.cot2.at[two], at.sibling)

    ends = [lengths[0, 0]]
    for i in (1, 2):
        ends.append(ends[-1] + lengths[0, i])
    lane = lax.broadcasted_iota(jnp.int32, (1, 128), 1)
    token = lax.broadcasted_iota(jnp.int32, (TOK, 128), 0)

    def image(j):
        t = token + order[0, j] * TOK
        return sum((t >= end).astype(jnp.int32) for end in ends)

    for j in range(4):
        other = jnp.where(lane == image(j), 0.0, -1e30)
        m.key_ext[j * TOK : (j + 1) * TOK, :] = jnp.where(lane < 4, other, jnp.where(lane < 76, 1.0, 0.0)).astype(BF)
    image_own = jnp.where(lane == image(seq), 1.0, 0.0)
    m.query_ext[own, :] = image_own.astype(BF)
    m.up_bias_half[...] = jnp.where(core == 0, up_bias[:HALF], up_bias[HALF:])[None]
    m.vec[...] = jnp.zeros((16, WIDTH), F32)
    m.vec[7:8, :] = jnp.sum(
        jnp.sum(cot[0].astype(F32).reshape(TOK // 8, 8, WIDTH), axis=0), axis=0, keepdims=True
    )
    m.stat[...] = jnp.zeros((TOK, 128), F32)
    low_lanes = (lane < 64).astype(BF)
    high_lanes = (lane >= 64).astype(BF)

    def both(v):
        return jnp.concatenate((v * low_lanes, v * high_lanes), axis=0)

    def joined(v):
        return jnp.where(lane < 64, v[:TOK], v[TOK:])

    def beside(a, b):
        return jnp.concatenate((a, b), axis=1)

    def project(chip):
        rows = chip_rows(chip)
        a = m.normed_in[rows, :]
        m.keys[rows, :] = dot(a, m.qkv_w[:, WIDTH : 2 * WIDTH]).astype(BF)
        m.values[rows, :] = (dot(a, m.qkv_w[:, 2 * WIDTH :]) + value_bias[...]).astype(BF)
        m.queries[rows, :] = ((dot(a, m.qkv_w[:, :WIDTH]) + query_bias[...]) * SCALE).astype(BF)

    loads[0].wait()
    in_sib.wait()
    project(at.chip)
    loads[1].wait()
    cot_sib.wait()
    m.hidden_grad[...] = dot_rt(m.cot2[...], m.down_w[...])
    in_far.wait()
    in_pass = side(2, m.normed_in.at[far], m.normed_in.at[far], at.sibling)
    in_pass.wait()
    project(1 - at.chip)

    def attend(i, carry):
        cols = rows_of(i * 128, 128)
        ext = m.query_ext[own, :]
        s = dot_rt(
            beside(both(m.queries[own, cols]), jnp.concatenate((ext, ext), axis=0)),
            beside(m.keys[:, cols], m.key_ext[...]),
        )
        top = jnp.max(s, axis=1, keepdims=True)
        e = jnp.exp(s - top).astype(BF)
        out = dot(e, beside(m.values[:, cols], jnp.ones((LEN, 128), BF)))
        total = out[:, 128:]
        out = joined(out[:, :128] * (1.0 / total))
        m.attended_full[:, cols] = out
        m.attended[two, cols] = out.astype(BF)
        logs = top + jnp.log(total)
        m.stat[...] = jnp.where(
            lane == 2 * i, logs[:TOK], jnp.where(lane == 2 * i + 1, logs[TOK:], m.stat[...])
        )
        return carry

    lax.fori_loop(0, PAIRS, attend, 0, unroll=True)

    loads[2].wait()
    m.resid[...] = x[0].astype(F32) + dot(m.attended[two, :], m.proj_w[...]) + proj_bias[...]
    normalize(lambda rows: m.resid[rows, :], mlp_gain, mlp_shift, m.hat2, m.fac2, m.mlp_in, core * TOK)
    mlp_sib = side(4, m.mlp_in.at[two], m.mlp_in.at[two], at.sibling)
    att_sib = side(5, m.attended.at[two], m.attended.at[two], at.sibling)
    loads[3].wait()
    mlp_sib.wait()

    def feed(i, carry):
        cols = rows_of(i * 512, 512)
        u = dot(m.mlp_in[...], m.up_w[:, cols]) + m.up_bias_half[:, cols]
        t = 1.0 / (1.0 + 0.36 * jnp.abs(u))
        tail = jnp.full_like(t, TAIL[-1])
        for c in TAIL[-2::-1]:
            tail = tail * t + c
        e = jnp.exp(-0.5 * (u * u))
        tail = tail * (t * e)
        phi = jnp.where(u >= 0, 1.0 - tail, tail)
        m.hidden[:, cols] = (u * phi).astype(BF)
        g = m.hidden_grad[:, cols] * (phi + u * (DENSITY * e))
        m.up_low[:, cols] = g.astype(BF)
        m.up_bias_half[:, cols] = jnp.sum(
            jnp.sum(g.reshape(2 * TOK // 8, 8, 512), axis=0), axis=0, keepdims=True
        )
        return carry

    lax.fori_loop(0, HALF // 512, feed, 0)

    def block_of(k):
        return slice(k * TOK, (k + 1) * TOK)

    def start(w, k):
        block = block_of(k)
        if w == DOWN:
            for h in range(2):
                first = h * WIDTH + k * TOK
                grads[w][block, h * WIDTH : (h + 1) * WIDTH] = dot_lt(
                    m.hidden[:, first : first + TOK], m.cot2[...]
                ).astype(BF)
        elif w == UP:
            grads[w][block, :] = dot_lt(m.mlp_in[:, block], m.up_low[...]).astype(BF)
        elif w == PROJ:
            grads[w][block, :384] = dot_lt(m.attended[:, block], m.resid_half[...]).astype(BF)
            grads[w][block, 384:] = dot_lt(
                m.normed_in[chip_rows(at.chip), block], m.query_half[...]
            ).astype(BF)
        else:
            grads[w][block, :] = dot_lt(
                m.normed_in[chip_rows(at.chip), block], m.keys_half[...]
            ).astype(BF)
        ex.start(w, k)

    sides = {}

    def mlp_back():
        m.mlp_part[...] = dot_rt(m.up_low[...], m.up_w[...])
        sides["part"] = side(6, m.mlp_part.at[two_other], m.mlp_came, at.sibling)
        for h in range(2):
            for t in range(2):
                m.vec[8 + 2 * h + t : 9 + 2 * h + t, :] = jnp.where(
                    core == h, m.up_bias_half[:, t * WIDTH : (t + 1) * WIDTH], 0.0
                )

    def keep_resid(rows, back):
        m.resid_grad[rows, :] = back
        m.resid_low[rows, :] = back.astype(BF)

    def resid_back():
        sides["part"].wait()
        norm_back(
            lambda rows: m.mlp_part[rows_of_shift(rows, core * TOK), :] + m.mlp_came[rows, :],
            lambda rows: cot[0, rows, :].astype(F32),
            mlp_gain,
            m.hat2,
            m.fac2,
            m.vec,
            (5, 6, 4),
            keep_resid,
        )
        m.attended_grad[own, :] = dot_rt(m.resid_low[...], m.proj_w[...]).astype(BF)
        grad = m.attended_grad.at[own]
        sides["grad_far"] = side(9, grad, grad, at.across)
        sides["grad_sib"] = side(8, grad, grad, at.sibling)

    def parts(v):
        found = []
        for _ in range(3):
            found.append(v.astype(BF))
            v = v - found[-1].astype(F32)
        return found

    def extend():
        feature = lax.broadcasted_iota(jnp.int32, (WIDTH, 128), 0)
        head_of = (feature // 64 + 16 == lax.broadcasted_iota(jnp.int32, (WIDTH, 128), 1)).astype(BF)
        means = m.attended_grad[own, :].astype(F32) * m.attended_full[...]
        sums = sum(dot(p, head_of) for p in parts(means))
        ext = image_own
        for j, p in enumerate(parts(-(m.stat[...] + sums))):
            to = lax.broadcasted_iota(jnp.int32, (128, 128), 1)
            of = lax.broadcasted_iota(jnp.int32, (128, 128), 0)
            spot = jnp.where(
                of < 12, 4 + 3 * of + j, jnp.where((of >= 16) & (of < 28), 3 * of - 8 + j, -1)
            )
            ext = ext + dot(p, (to == spot).astype(BF))
        m.query_ext[own, :] = ext.astype(BF)
        ext = m.query_ext.at[own]
        sides["ext_far"] = side(12, ext, ext, at.across)
        sides["ext_sib"] = side(11, ext, ext, at.sibling)
        m.resid_half[two, :] = m.resid_low[:, cut(core * 384, 384)]
        sides["resid"] = side(
            14, m.resid_low.at[:, cut((1 - core) * 384, 384)], m.resid_half.at[two], at.sibling
        )

    def picks(i):
        a, b = lane - 4 - 6 * i, lane - 40 - 6 * i
        first = jnp.where((lane < 4) | ((a >= 0) & (a < 3)), 1.0, 0.0).astype(BF)
        second = jnp.where((lane < 4) | ((a >= 3) & (a < 6)), 1.0, 0.0).astype(BF)
        third = jnp.where((b >= 0) & (b < 3), 1.0, 0.0).astype(BF)
        fourth = jnp.where((b >= 3) & (b < 6), 1.0, 0.0).astype(BF)
        return (lambda v: jnp.concatenate((v * first, v * second), axis=0)), (
            lambda v: jnp.concatenate((v * third, v * fourth), axis=0)
        )

    def query_side(pairs):
        for i in pairs:
            cols = slice(i * 128, (i + 1) * 128)
            of_scores, of_means = picks(i)
            ext, k = m.query_ext[own, :], m.keys[:, cols]
            p = jnp.exp(
                dot_rt(beside(both(m.queries[own, cols]), of_scores(ext)), beside(k, m.key_ext[...]))
            )
            y = dot_rt(
                beside(both(m.attended_grad[own, cols]), of_means(ext)),
                beside(m.values[:, cols], m.key_ext[...]),
            )
            g = joined(dot((p * y).astype(BF), k)) * SCALE
            m.vec[2:3, cols] = jnp.sum(g, axis=0, keepdims=True)
            m.qkv_low[:, cols] = g.astype(BF)
        if PAIRS - 1 in pairs:
            sides["query"] = share(15, 0, m.query_half)

    def key_side(chip, first, pairs):
        rows = chip_rows(chip)
        for i in pairs:
            cols = slice(i * 128, (i + 1) * 128)
            of_scores, of_means = picks(i)
            q, g, ext = m.queries[rows, cols], m.attended_grad[rows, cols], m.key_ext[own, :]
            other = m.query_ext[rows, :]
            p = jnp.exp(dot_rt(beside(both(m.keys[own, cols]), of_scores(ext)), beside(q, other)))
            y = dot_rt(beside(both(m.values[own, cols]), of_means(ext)), beside(g, other))
            dv = joined(dot(p.astype(BF), g))
            dk = joined(dot((p * y).astype(BF), q))
            if first:
                m.value_grad[:, cols] = dv
                m.key_grad[:, cols] = dk
            else:
                dv = dv + m.value_grad[:, cols]
                dk = dk + m.key_grad[:, cols]
                m.vec[3:4, cols] = jnp.sum(dv, axis=0, keepdims=True)
                m.qkv_low[:, WIDTH + i * 128 : WIDTH + (i + 1) * 128] = dk.astype(BF)
                m.qkv_low[:, 2 * WIDTH + i * 128 : 2 * WIDTH + (i + 1) * 128] = dv.astype(BF)
        if not first and PAIRS - 1 in pairs:
            sides["keys"] = share(16, 1, m.keys_half.at[:, :384])
            sides["values"] = share(17, 2, m.keys_half.at[:, 384:])

    def share(i, part, target):
        target.at[two][...] = m.qkv_low[:, cut(part * WIDTH + core * 384, 384)]
        return side(
            i, m.qkv_low.at[:, cut(part * WIDTH + (1 - core) * 384, 384)], target.at[two], at.sibling
        )

    def near_ready():
        sides["grad_sib"].wait()
        sides["ext_sib"].wait()

    def proj_ready():
        att_sib.wait()
        sides["resid"].wait()
        sides["query"].wait()

    def far_here():
        sides["grad_far"].wait()
        sides["grad_pass"] = side(
            10, m.attended_grad.at[far], m.attended_grad.at[far], at.sibling
        )
        sides["ext_far"].wait()
        sides["ext_pass"] = side(13, m.query_ext.at[far], m.query_ext.at[far], at.sibling)

    def far_ready():
        sides["grad_pass"].wait()
        sides["ext_pass"].wait()

    def keys_ready():
        sides["keys"].wait()
        sides["values"].wait()

    def keep_input(rows, back):
        input_grad[0, rows, :] = back.astype(BF)

    def input_back():
        m.attn_grad[...] = dot_rt(m.qkv_low[...], m.qkv_w[...])
        norm_back(
            lambda rows: m.attn_grad[rows, :],
            lambda rows: m.resid_grad[rows, :],
            attn_gain,
            m.hat1,
            m.fac1,
            m.vec,
            (0, 1),
            keep_input,
        )

    def vec_step(s):
        if s > 0:
            sides["vec"].wait()
            m.vec[...] = m.vec[...] + m.vec_came[s - 1]
        if s > DIMS:
            vec_out[...] = m.vec[...]
            return
        copy = pltpu.make_async_remote_copy(
            src_ref=m.vec,
            dst_ref=m.vec_came.at[s],
            send_sem=m.vec_send.at[s],
            recv_sem=m.vec_recv.at[s],
            device_id=(at.partners + (at.sibling,))[s],
            device_id_type=MESH,
        )
        copy.start()
        sides["vec"] = copy

    def feed_out():
        m.out_part[...] = dot(m.hidden[...], m.down_w[...])
        sides["out"] = side(7, m.out_part.at[two_other], m.out_came, at.sibling)

    def close():
        sides["out"].wait()
        block_output[0] = (
            m.resid[...] + (m.out_part[two, :] + m.out_came[...]) + down_bias[...]
        ).astype(BF)

    near, other_chip = at.chip, 1 - at.chip
    pieces = dict(
        mlp_back=mlp_back,
        resid_back=resid_back,
        extend=extend,
        query1=lambda: query_side(range(3)),
        query2=lambda: query_side(range(3, 6)),
        near_ready=near_ready,
        near1=lambda: key_side(near, True, range(3)),
        near2=lambda: key_side(near, True, range(3, 6)),
        proj_ready=proj_ready,
        far_here=far_here,
        far_ready=far_ready,
        far1=lambda: key_side(other_chip, False, range(3)),
        far2=lambda: key_side(other_chip, False, range(3, 6)),
        keys_ready=keys_ready,
        input_back=input_back,
        feed_out=feed_out,
        close=close,
    )
    for step in PLAN:
        if isinstance(step, str):
            pieces[step]()
        elif len(step) == 1:
            vec_step(step[0])
        elif len(step) == 2:
            start(*step)
        else:
            ex.finish(*step)

    for w in range(len(WIDTHS)):
        ex.done(w)


PLAN = (
    (0, 4), (0, 5), (1, 1), "mlp_back", (1, 2), (0, 1), (1, 0), (0, 2),
    (1, 3), (0, 0), "resid_back", "extend", (0, 3), "query1", "query2", (1, 5),
    (1, 1, 0), (0, 4, 0), "near_ready", "near1", "proj_ready", (1, 2, 0), (2, 4), (2, 3),
    (1, 4), (1, 3, 0), (2, 2), (0, 5, 0), (2, 1), (1, 0, 0), (2, 0), (0, 1, 0),
    (2, 5), "far_here", (0, 2, 0), "near2", (0, 0, 0), "far_ready", "far1", "far2",
    (1, 5, 0), (1, 1, 1), "input_back", "keys_ready", (3, 5), (3, 1), (3, 2), (2, 3, 0),
    (3, 0), (2, 0, 0), (0, 3, 0), (1, 2, 1), (3, 3), (0, 4, 1), (2, 4, 0), (1, 0, 1),
    (0, 1, 1), (1, 4, 0), (1, 1, 2), (2, 1, 0), (0, 0, 1), (0, 2, 1), (1, 3, 1), (2, 2, 0),
    (1, 5, 1), (2, 3, 1), (0, 5, 1), (2, 5, 0), (3, 1, 0), (3, 0, 0), (2, 0, 1), (3, 3, 0),
    (2, 4, 1), (3, 5, 0), (0, 4, 2), (0, 3, 1), (3, 4), (2, 1, 1), (1, 2, 2), (1, 4, 1),
    (1, 0, 2), (1, 5, 2), (0, 0, 2), (2, 5, 1), (1, 1, 3), (1, 3, 2), (3, 2, 0), (2, 2, 1),
    (3, 1, 1), (2, 4, 2), (2, 3, 2), (0, 1, 2), (2, 0, 2), (0, 5, 2), (0, 2, 2), (0, 4, 3),
    (3, 0, 1), (0, 3, 2), (3, 3, 1), (1, 0, 3), (1, 2, 3), (1, 4, 2), (0,), (2, 5, 2),
    (3, 4, 0), (1, 5, 3), (1, 3, 3), (2, 2, 2), (2, 1, 2), (3, 2, 1), (2, 3, 3), (0, 1, 3),
    (3, 5, 1), (0, 0, 3), (0, 2, 3), (0, 3, 3), (0, 5, 3), (1, 1, 4), (3, 0, 2), (1, 2, 4),
    (1, 4, 3), (2, 0, 3), (0, 4, 4), (2, 5, 3), (3, 3, 2), (2, 1, 3), (1,), (2, 3, 4),
    (3, 1, 2), (1, 3, 4), (3, 4, 1), (1, 5, 4), (3, 5, 2), (0, 0, 4), (0, 3, 4), (0, 1, 4),
    (0, 2, 4), (0, 5, 4), (1, 0, 4), (3, 0, 3), (1, 4, 4), (3, 2, 2), (0, 4, 5), (2, 1, 4),
    (1, 2, 5), (2, 3, 5), (2, 4, 3), (2, 0, 4), (1, 3, 5), (1, 1, 5), (3, 5, 3), (3, 4, 2),
    (0, 0, 5), (1, 5, 5), (2, 2, 3), (2, 5, 4), (3, 1, 3), (0, 2, 5), (0, 5, 5), (3, 3, 3),
    (0, 1, 5), (1, 4, 5), (1, 0, 5), (2,), (0, 3, 5), (0, 4, 6), (2, 3, 6), (2, 1, 5),
    (3, 0, 4), (1, 2, 6), (2, 4, 4), (1, 3, 6), (1, 1, 6), (3, 4, 3), (3, 5, 4), (0, 0, 6),
    (1, 5, 6), (2, 0, 5), (2, 5, 5), (3, 1, 4), (3, 2, 3), (0, 2, 6), (2, 2, 4), (0, 5, 6),
    (0, 1, 6), (1, 4, 6), (1, 0, 6), (2, 3, 7), (0, 3, 6), (2, 1, 6), (2, 4, 5), (3, 4, 4),
    (0, 4, 7), (1, 2, 7), (3,), (3, 5, 5), (1, 3, 7), (1, 1, 7), (3, 2, 4), (1, 5, 7),
    (0, 0, 7), (3, 3, 4), (3, 1, 5), (3, 0, 5), (2, 2, 5), "feed_out", (0, 5, 7), (2, 0, 6),
    (0, 3, 7), (1, 4, 7), (3, 4, 5), (1, 0, 7), (0, 1, 7), (0, 2, 7), (2, 4, 6), (3, 5, 6),
    (2, 5, 6), (0, 4, 8), (1, 3, 8), (3, 2, 5), (1, 5, 8), (3, 3, 5), (0, 0, 8), (2, 0, 7),
    (3, 0, 6), (1, 2, 8), (2, 3, 8), (2, 2, 6), (3, 4, 6), (2, 1, 7), (1, 1, 8), (3, 3, 6),
    (3, 5, 7), (2, 4, 7), (3, 2, 6), (1, 0, 8), (0, 5, 8), (3, 1, 6), (0, 2, 8), (3, 0, 7),
    (1, 4, 8), (2, 2, 7), (3, 2, 7), (1, 3, 9), (0, 1, 8), (0, 3, 8), (1, 1, 9), (1, 2, 9),
    (4,), (3, 3, 7), (3, 4, 7), (2, 5, 7), (3, 5, 8), (3, 0, 8), (2, 4, 8), (2, 1, 8),
    (0, 0, 9), (2, 0, 8), (3, 1, 7), (1, 4, 9), (0, 4, 9), (2, 2, 8), (2, 3, 9), (3, 2, 8),
    (0, 5, 9), (1, 5, 9), (5,), (3, 4, 8), (3, 3, 8), (0, 2, 9), (1, 0, 9), (2, 5, 8),
    (3, 1, 8), (0, 1, 9), (2, 2, 9), (2, 4, 9), (3, 0, 9), (2, 1, 9), (6,), (3, 5, 9),
    (0, 3, 9), (3, 4, 9), (3, 3, 9), (3, 2, 9), (2, 0, 9), (2, 5, 9), (3, 1, 9), (7,),
    "close",
)


def rows_of_shift(rows, shift):
    return pl.ds(pl.multiple_of(rows.start + shift, 16), rows.size)


def spread_kernel(
    wide,
    slim,
    vec,
    block_output_in,
    input_grad_in,
    block_output,
    input_grad,
    attn_gain,
    attn_shift,
    qkv,
    query_bias,
    value_bias,
    proj,
    proj_bias,
    mlp_gain,
    mlp_shift,
    up,
    up_bias,
    down,
    down_bias,
):
    rows = rows_of(pl.program_id(0) * SPREAD_ROWS, SPREAD_ROWS)
    for c in range(2):
        up[:, c * HALF : (c + 1) * HALF] = wide[1, c, rows, :].astype(F32)
        proj[:, c * 384 : (c + 1) * 384] = slim[0, c, rows, :384].astype(F32)
        for part in range(3):
            first = part * WIDTH + c * 384
            source = slim[0, c, rows, 384:] if part == 0 else slim[1, c, rows, (part - 1) * 384 : part * 384]
            qkv[:, first : first + 384] = source.astype(F32)
        for h in range(2):
            down[2 * c + h] = wide[0, c, rows, h * WIDTH : (h + 1) * WIDTH].astype(F32)

    @pl.when(pl.program_id(0) == 0)
    def _():
        block_output[...] = block_output_in[...]
        input_grad[...] = input_grad_in[...]
        for row, ref in enumerate(
            (attn_gain, attn_shift, query_bias, value_bias, proj_bias, mlp_gain, mlp_shift, down_bias)
        ):
            ref[...] = vec[row]
        for t in range(4):
            up_bias[t * WIDTH : (t + 1) * WIDTH] = vec[8 + t]


SPREAD_ROWS = 64


def spread(*given):
    rows = SPREAD_ROWS
    line = lambda n: (jax.ShapeDtypeStruct((n,), F32), pl.BlockSpec((n,), lambda i: (0,)))
    flat = lambda n: (jax.ShapeDtypeStruct((WIDTH, n), F32), pl.BlockSpec((rows, n), lambda i: (i, 0)))
    tokens = (jax.ShapeDtypeStruct((1, TOK, WIDTH), BF), pl.BlockSpec((1, TOK, WIDTH), lambda i: (0, 0, 0)))
    outs = [
        tokens,
        tokens,
        line(WIDTH),
        line(WIDTH),
        flat(3 * WIDTH),
        line(WIDTH),
        line(WIDTH),
        flat(WIDTH),
        line(WIDTH),
        line(WIDTH),
        line(WIDTH),
        flat(HIDDEN),
        line(HIDDEN),
        (
            jax.ShapeDtypeStruct((4, WIDTH, WIDTH), F32),
            pl.BlockSpec((4, rows, WIDTH), lambda i: (0, i, 0)),
        ),
        line(WIDTH),
    ]
    return pl.pallas_call(
        spread_kernel,
        grid=(WIDTH // rows,),
        out_shape=[o[0] for o in outs],
        in_specs=[pl.BlockSpec(memory_space=pltpu.VMEM)] * len(given),
        out_specs=[o[1] for o in outs],
        compiler_params=pltpu.CompilerParams(vmem_limit_bytes=24 << 20),
    )(*(pltpu.with_memory_space_constraint(v, pltpu.VMEM) for v in given))


def body(
    block_input,
    out_cotangent,
    image_lengths,
    span_order,
    attn_gain,
    attn_shift,
    qkv_weight,
    query_bias,
    value_bias,
    proj_weight,
    proj_bias,
    mlp_gain,
    mlp_shift,
    up_weight,
    up_bias,
    down_weight,
    down_bias,
):
    vmem = pl.BlockSpec(memory_space=pltpu.VMEM)
    hbm = pl.BlockSpec(memory_space=pl.ANY)
    held = scratch()
    block_output, input_grad, wide, slim, vec = pl.pallas_call(
        kernel,
        out_shape=[
            pltpu.VMEM((1, TOK, WIDTH), BF),
            pltpu.VMEM((1, TOK, WIDTH), BF),
            pltpu.VMEM((2, 2, WIDTH, HALF), BF),
            pltpu.VMEM((2, 2, WIDTH, WIDTH), BF),
            pltpu.VMEM((16, WIDTH), F32),
        ],
        in_specs=[pl.BlockSpec(memory_space=pltpu.SMEM)] * 2 + [vmem] * 11 + [hbm] * 4,
        out_specs=[vmem] * 5,
        scratch_shapes=[held[name] for name in NAMES],
        compiler_params=pltpu.CompilerParams(
            collective_id=0, has_side_effects=True, vmem_limit_bytes=VMEM_LIMIT
        ),
    )(
        image_lengths,
        span_order,
        block_input,
        out_cotangent,
        attn_gain,
        attn_shift,
        query_bias,
        value_bias,
        proj_bias,
        mlp_gain,
        mlp_shift,
        up_bias,
        down_bias,
        qkv_weight,
        proj_weight,
        up_weight,
        down_weight,
    )
    outs = list(spread(wide, slim, vec, block_output, input_grad))
    outs[13] = outs[13].reshape(HIDDEN, WIDTH)
    return tuple(outs)


VMEM_LIMIT = 46 << 20


def solution(mesh):
    tokens = P("rows", "seq", None)
    return jax.shard_map(
        body,
        mesh=mesh,
        in_specs=(tokens, tokens, P("rows", None), P("rows", None)) + (P(),) * 13,
        out_specs=(tokens, tokens) + (P(),) * 13,
        check_vma=False,
    )
```

```python
from types import SimpleNamespace

import jax
import jax.numpy as jnp
from jax import lax
from jax.experimental import pallas as pl
from jax.experimental.pallas import tpu as pltpu
from jax.sharding import PartitionSpec as P

MESH = pl.DeviceIdType.MESH
BF, F32 = jnp.bfloat16, jnp.float32
WIDTH = 768
HIDDEN = 3072
HALF = HIDDEN // 2
TOK = 128
LEN = 512
PAIRS = 6
SCALE = 64**-0.5
EPSILON = 1e-6

DIMS = 6
DOWN, UP, PROJ, KEYS = range(4)
WIDTHS = (HALF, HALF, WIDTH, WIDTH)
HALVINGS = (4, 3, 3, 3)

TAIL = (
    0.14361835615286447,
    0.14366105191010822,
    0.12424683572786965,
    0.09467827005043768,
    0.003990377379362003,
    0.09912410558005538,
    -0.21460327937017376,
    0.13425173188400444,
    -0.02896737861797067,
)
DENSITY = 0.3989422804014327


def rows_of(start, size):
    return pl.ds(pl.multiple_of(start, size), size)


def dot(a, b):
    return lax.dot_general(a, b, (((1,), (0,)), ((), ())), preferred_element_type=F32)


def dot_rt(a, b):
    return lax.dot_general(a, b, (((1,), (1,)), ((), ())), preferred_element_type=F32)


def dot_lt(a, b):
    return lax.dot_general(a, b, (((0,), (0,)), ((), ())), preferred_element_type=F32)


def place():
    row, seq = lax.axis_index("rows"), lax.axis_index("seq")
    x, y, z_lo = row % 4, (row // 4) % 4, row // 16
    z_hi, core = seq // 2, seq % 2
    z = z_hi * 2 + z_lo

    def device(x, y, z, core):
        return ((z % 2) * 16 + y * 4 + x, (z // 2) * 2 + core)

    near = lambda v: v + 1 - 2 * (v % 2)
    far = lambda v: 3 - v
    first = lambda v: (v % 2 + v // 2) % 2
    return SimpleNamespace(
        seq=seq,
        core=core,
        chip=z_hi,
        partners=(
            device(near(x), y, z, core),
            device(far(x), y, z, core),
            device(x, near(y), z, core),
            device(x, far(y), z, core),
            device(x, y, near(z), core),
            device(x, y, far(z), core),
        ),
        bits=(first(x), x // 2, first(y), y // 2, first(z), z // 2),
        sibling=(row, z_hi * 2 + 1 - core),
        across=(row, (1 - z_hi) * 2 + core),
    )


class Exchange:
    def __init__(self, at, grads, whole, landing, send_sem, recv_sem, over_sem):
        self.at = at
        self.grads, self.whole, self.landing = grads, whole, landing
        self.send_sem, self.recv_sem, self.over_sem = send_sem, recv_sem, over_sem
        self.copies = {}

    def dim(self, k, s):
        return (k + s) % DIMS

    def rows(self, k, s):
        low = TOK * k
        for t in range(min(s, 3)):
            low = low + self.at.bits[self.dim(k, t)] * (64 >> t)
        return low

    def block(self, w, k, s, mine, whole=False):
        held = self.whole[w].at[self.at.core] if whole else self.grads[w]
        bit = self.at.bits[self.dim(k, s)]
        pick = bit if mine else 1 - bit
        if s < 3:
            size = 64 >> s
            return held.at[pl.ds(pl.multiple_of(self.rows(k, s) + pick * size, 16), size)]
        width = WIDTHS[w] // 2
        return held.at[
            pl.ds(pl.multiple_of(self.rows(k, 3), 16), 16),
            pl.ds(pl.multiple_of(pick * width, 128), width),
        ]

    def slot(self, w, k, s):
        held = self.landing[w].at[k]
        if s < 3:
            return held.at[pl.ds((0, 64, 96)[s], 64 >> s)]
        if HALVINGS[w] == 3:
            return held.at[pl.ds(64 + 16 * s, 16)]
        width = WIDTHS[w] // 2
        return held.at[pl.ds((112, 112, 128)[s - 3], 16), pl.ds((0, width, 0)[s - 3], width)]

    def start(self, w, k, s=0):
        last = HALVINGS[w] - 1
        if s <= last:
            src, dst, d = self.block(w, k, s, False), self.slot(w, k, s), self.dim(k, s)
        elif s < DIMS:
            src, dst, d = self.block(w, k, last, True), self.slot(w, k, s), self.dim(k, s)
        else:
            t = last + DIMS - s
            src = dst = self.block(w, k, t, True, True)
            d = self.dim(k, t)
        copy = pltpu.make_async_remote_copy(
            src_ref=src,
            dst_ref=dst,
            send_sem=self.send_sem.at[w, k],
            recv_sem=self.recv_sem.at[w, k, s],
            device_id=self.at.partners[d],
            device_id_type=MESH,
        )
        copy.start()
        self.copies[w, k, s] = copy

    def over(self, w, k, part):
        half = self.block(w, k, 0, part == 0, True)
        self.crossing(w, half, half).start()

    def crossing(self, w, src, dst):
        return pltpu.make_async_remote_copy(
            src_ref=src,
            dst_ref=dst,
            send_sem=self.over_sem.at[0, w],
            recv_sem=self.over_sem.at[1, w],
            device_id=self.at.sibling,
            device_id_type=MESH,
        )

    def done(self, w):
        self.crossing(w, self.whole[w].at[self.at.core], self.whole[w].at[1 - self.at.core]).wait()

    def finish(self, w, k, s):
        steps, last = DIMS + HALVINGS[w], HALVINGS[w] - 1
        self.copies[w, k, s].wait()
        if s < DIMS:
            kept, slot = self.block(w, k, min(s, last), True), self.slot(w, k, s)
            total = (kept[...].astype(F32) + slot[...].astype(F32)).astype(BF)
            if s < DIMS - 1:
                kept[...] = total
            else:
                self.block(w, k, last, True, True)[...] = total
        if s < steps - 1:
            self.start(w, k, s + 1)
        if s >= steps - 2:
            self.over(w, k, s - (steps - 2))


def normalize(load, gain, shift, normed, factor, result, base):
    def step(i, carry):
        rows = rows_of(i * 16, 16)
        v = load(rows)
        c = v - jnp.mean(v, axis=1, keepdims=True)
        f = lax.rsqrt(jnp.mean(c * c, axis=1, keepdims=True) + EPSILON)
        n = c * f
        normed[rows, :] = n
        factor[rows, :] = f
        result[rows_of(base + i * 16, 16), :] = (n * gain[...] + shift[...]).astype(BF)
        return carry

    lax.fori_loop(0, TOK // 16, step, 0, unroll=True)


def folded(v):
    return jnp.sum(v.reshape(2, 8, WIDTH), axis=0)


def norm_back(load_grad, load_rest, gain, normed, factor, vec, where, keep):
    zero = jnp.zeros((8, WIDTH), F32)

    def step(i, carry):
        rows = rows_of(i * 16, 16)
        e, n = load_grad(rows), normed[rows, :]
        g = e * gain[...]
        a = jnp.mean(g, axis=1, keepdims=True)
        b = jnp.mean(g * n, axis=1, keepdims=True)
        back = load_rest(rows) + factor[rows, :] * (g - a - n * b)
        keep(rows, back)
        return carry[0] + folded(e * n), carry[1] + folded(e), carry[2] + folded(back)

    sums = lax.fori_loop(0, TOK // 16, step, (zero, zero, zero), unroll=True)
    for row, total in zip(where, sums):
        vec[row : row + 1, :] = jnp.sum(total, axis=0, keepdims=True)


def scratch():
    v = pltpu.VMEM
    dma = pltpu.SemaphoreType.DMA
    sets = len(WIDTHS)
    return dict(
        qkv_w=v((WIDTH, 3 * WIDTH), BF),
        proj_w=v((WIDTH, WIDTH), BF),
        up_w=v((WIDTH, HALF), BF),
        down_w=v((HALF, WIDTH), BF),
        lines=v((8, WIDTH), F32),
        up_bias_half=v((1, HALF), F32),
        up_sum=v((1, HALF), F32),
        normed_in=v((LEN, WIDTH), BF),
        queries=v((LEN, WIDTH), BF),
        keys=v((LEN, WIDTH), BF),
        values=v((LEN, WIDTH), BF),
        key_ext=v((LEN, 128), BF),
        query_ext=v((LEN, 128), BF),
        stat=v((TOK, 128), F32),
        hat1=v((TOK, WIDTH), F32),
        fac1=v((TOK, 1), F32),
        attended_full=v((TOK, WIDTH), F32),
        attended=v((2 * TOK, WIDTH), BF),
        resid=v((TOK, WIDTH), F32),
        hat2=v((TOK, WIDTH), F32),
        fac2=v((TOK, 1), F32),
        mlp_in=v((2 * TOK, WIDTH), BF),
        cot2=v((2 * TOK, WIDTH), BF),
        hidden_grad=v((2 * TOK, HALF), F32),
        hidden=v((2 * TOK, HALF), BF),
        up_low=v((2 * TOK, HALF), BF),
        mlp_part=v((2 * TOK, WIDTH), F32),
        mlp_came=v((TOK, WIDTH), F32),
        out_part=v((2 * TOK, WIDTH), F32),
        out_came=v((TOK, WIDTH), F32),
        resid_grad=v((TOK, WIDTH), F32),
        resid_low=v((TOK, WIDTH), BF),
        attended_grad=v((LEN, WIDTH), BF),
        qkv_low=v((TOK, 3 * WIDTH), BF),
        resid_half=v((2 * TOK, 384), BF),
        query_half=v((2 * TOK, 384), BF),
        keys_half=v((2 * TOK, WIDTH), BF),
        key_grad=v((TOK, WIDTH), F32),
        value_grad=v((TOK, WIDTH), F32),
        attn_grad=v((TOK, WIDTH), F32),
        vec=v((16, WIDTH), F32),
        vec_came=v((DIMS + 1, 16, WIDTH), F32),
        grads_wide=v((2, WIDTH, HALF), BF),
        grads_slim=v((2, WIDTH, WIDTH), BF),
        landing_wide=v((2, DIMS, 160, HALF), BF),
        landing_slim=v((2, DIMS, 160, WIDTH), BF),
        send_sem=dma((sets, DIMS)),
        recv_sem=dma((sets, DIMS, DIMS + max(HALVINGS))),
        over_sem=dma((2, sets)),
        side_send=dma((20,)),
        side_recv=dma((20,)),
        vec_send=dma((DIMS + 1,)),
        vec_recv=dma((DIMS + 1,)),
        load_sem=dma((4,)),
    )


NAMES = tuple(scratch())


def kernel(
    lengths,
    order,
    x,
    cot,
    attn_gain,
    attn_shift,
    query_bias,
    value_bias,
    proj_bias,
    mlp_gain,
    mlp_shift,
    up_bias,
    down_bias,
    qkv_weight,
    proj_weight,
    up_weight,
    down_weight,
    block_output,
    input_grad,
    whole_wide,
    whole_slim,
    vec_out,
    *refs,
):
    m = SimpleNamespace(**dict(zip(NAMES, refs)))
    at = place()
    core, seq = at.core, at.seq
    pair_of = lambda wide, slim: (wide.at[0], wide.at[1], slim.at[0], slim.at[1])
    grads = pair_of(m.grads_wide, m.grads_slim)
    ex = Exchange(
        at,
        grads,
        pair_of(whole_wide, whole_slim),
        pair_of(m.landing_wide, m.landing_slim),
        m.send_sem,
        m.recv_sem,
        m.over_sem,
    )

    barrier = pltpu.get_barrier_semaphore()
    for device in at.partners + (at.sibling, at.across):
        pl.semaphore_signal(barrier, inc=1, device_id=device, device_id_type=MESH)

    loads = [
        pltpu.make_async_copy(src, dst, m.load_sem.at[i])
        for i, (src, dst) in enumerate(
            (
                (qkv_weight, m.qkv_w),
                (down_weight.at[rows_of(core * HALF, HALF)], m.down_w),
                (proj_weight, m.proj_w),
                (up_weight.at[:, rows_of(core * HALF, HALF)], m.up_w),
            )
        )
    ]
    for load in loads:
        load.start()

    def side(i, src, dst, device):
        copy = pltpu.make_async_remote_copy(
            src_ref=src,
            dst_ref=dst,
            send_sem=m.side_send.at[i],
            recv_sem=m.side_recv.at[i],
            device_id=device,
            device_id_type=MESH,
        )
        copy.start()
        return copy

    own = rows_of(seq * TOK, TOK)
    two = rows_of(core * TOK, TOK)
    two_other = rows_of((1 - core) * TOK, TOK)
    far_block = (1 - at.chip) * 2 + core
    far = rows_of(far_block * TOK, TOK)
    chip_rows = lambda chip: rows_of(chip * 2 * TOK, 2 * TOK)
    cut = lambda start, size: pl.ds(pl.multiple_of(start, 128), size)

    vectors = (attn_gain, attn_shift, query_bias, value_bias, proj_bias, mlp_gain, mlp_shift, down_bias)
    for i, vector in enumerate(vectors):
        m.lines[i : i + 1, :] = vector[...][None]
    attn_gain, attn_shift, query_bias, value_bias, proj_bias, mlp_gain, mlp_shift, down_bias = (
        m.lines.at[i : i + 1] for i in range(8)
    )

    normalize(
        lambda rows: x[0, rows, :].astype(F32), attn_gain, attn_shift, m.hat1, m.fac1, m.normed_in, seq * TOK
    )
    m.cot2[two, :] = cot[0]

    pl.semaphore_wait(barrier, DIMS + 2)
    in_far = []
    for i in range(2):
        piece = m.normed_in.at[rows_of((seq * 2 + i) * 64, 64)]
        in_far.append(side((1, 18)[i], piece, piece, at.across))
    in_sib = side(0, m.normed_in.at[own], m.normed_in.at[own], at.sibling)
    cot_sib = side(3, m.cot2.at[two], m.cot2.at[two], at.sibling)

    ends = [lengths[0, 0]]
    for i in (1, 2):
        ends.append(ends[-1] + lengths[0, i])
    lane = lax.broadcasted_iota(jnp.int32, (1, 128), 1)
    token = lax.broadcasted_iota(jnp.int32, (TOK, 128), 0)

    def image(j):
        t = token + order[0, j] * TOK
        return sum((t >= end).astype(jnp.int32) for end in ends)

    for j in range(4):
        other = jnp.where(lane == image(j), 0.0, -1e30)
        m.key_ext[j * TOK : (j + 1) * TOK, :] = jnp.where(lane < 4, other, jnp.where(lane < 76, 1.0, 0.0)).astype(BF)
    image_own = jnp.where(lane == image(seq), 1.0, 0.0)
    m.query_ext[own, :] = image_own.astype(BF)
    m.up_bias_half[...] = jnp.where(core == 0, up_bias[:HALF], up_bias[HALF:])[None]
    m.vec[...] = jnp.zeros((16, WIDTH), F32)
    m.vec[7:8, :] = jnp.sum(
        jnp.sum(cot[0].astype(F32).reshape(TOK // 8, 8, WIDTH), axis=0), axis=0, keepdims=True
    )
    m.stat[...] = jnp.zeros((TOK, 128), F32)
    low_lanes = (lane < 64).astype(BF)
    high_lanes = (lane >= 64).astype(BF)

    def both(v):
        return jnp.concatenate((v * low_lanes, v * high_lanes), axis=0)

    def joined(v):
        return jnp.where(lane < 64, v[:TOK], v[TOK:])

    def beside(a, b):
        return jnp.concatenate((a, b), axis=1)

    def project_keys(rows):
        a = m.normed_in[rows, :]
        m.keys[rows, :] = dot(a, m.qkv_w[:, WIDTH : 2 * WIDTH]).astype(BF)
        m.values[rows, :] = (dot(a, m.qkv_w[:, 2 * WIDTH :]) + value_bias[...]).astype(BF)

    def project_queries(rows):
        part = dot(m.normed_in[rows, :], m.qkv_w[:, :WIDTH])
        m.queries[rows, :] = ((part + query_bias[...]) * SCALE).astype(BF)

    loads[0].wait()
    in_sib.wait()
    project_keys(chip_rows(at.chip))
    project_queries(chip_rows(at.chip))
    loads[1].wait()
    cot_sib.wait()
    m.hidden_grad[...] = dot_rt(m.cot2[...], m.down_w[...])
    in_pass = []
    for i in range(2):
        in_far[i].wait()
        piece = m.normed_in.at[rows_of((far_block * 2 + i) * 64, 64)]
        in_pass.append(side((2, 19)[i], piece, piece, at.sibling))
    project_keys(far)
    for copy in in_pass:
        copy.wait()
    project_keys(rows_of(((1 - at.chip) * 2 + 1 - core) * TOK, TOK))

    def attend(i, carry):
        cols = rows_of(i * 128, 128)
        ext = m.query_ext[own, :]
        s = dot_rt(
            beside(both(m.queries[own, cols]), jnp.concatenate((ext, ext), axis=0)),
            beside(m.keys[:, cols], m.key_ext[...]),
        )
        top = jnp.max(s, axis=1, keepdims=True)
        e = jnp.exp(s - top).astype(BF)
        out = dot(e, beside(m.values[:, cols], jnp.ones((LEN, 128), BF)))
        total = out[:, 128:]
        out = joined(out[:, :128] * (1.0 / total))
        m.attended_full[:, cols] = out
        m.attended[two, cols] = out.astype(BF)
        logs = top + jnp.log(total)
        m.stat[...] = jnp.where(
            lane == 2 * i, logs[:TOK], jnp.where(lane == 2 * i + 1, logs[TOK:], m.stat[...])
        )
        return carry

    lax.fori_loop(0, PAIRS, attend, 0, unroll=True)

    loads[2].wait()
    m.resid[...] = x[0].astype(F32) + dot(m.attended[two, :], m.proj_w[...]) + proj_bias[...]
    normalize(lambda rows: m.resid[rows, :], mlp_gain, mlp_shift, m.hat2, m.fac2, m.mlp_in, core * TOK)
    mlp_sib = side(4, m.mlp_in.at[two], m.mlp_in.at[two], at.sibling)
    att_sib = side(5, m.attended.at[two], m.attended.at[two], at.sibling)
    loads[3].wait()

    def feed(rows, first):
        for i in range(3):
            cols = slice(i * 512, (i + 1) * 512)
            u = dot(m.mlp_in[rows, :], m.up_w[:, cols]) + m.up_bias_half[:, cols]
            t = 1.0 / (1.0 + 0.36 * jnp.abs(u))
            tail = jnp.full_like(t, TAIL[-1])
            for c in TAIL[-2::-1]:
                tail = tail * t + c
            e = jnp.exp(-0.5 * (u * u))
            tail = tail * (t * e)
            phi = jnp.where(u >= 0, 1.0 - tail, tail)
            m.hidden[rows, cols] = (u * phi).astype(BF)
            g = m.hidden_grad[rows, cols] * (phi + u * (DENSITY * e))
            m.up_low[rows, cols] = g.astype(BF)
            total = jnp.sum(g.reshape(TOK // 8, 8, 512), axis=0)
            total = jnp.sum(total, axis=0, keepdims=True)
            m.up_sum[:, cols] = total if first else m.up_sum[:, cols] + total

    feed(two, True)
    mlp_sib.wait()
    feed(two_other, False)

    def block_of(k):
        return slice(k * TOK, (k + 1) * TOK)

    def start(w, k):
        block = block_of(k)
        if w == DOWN:
            for h in range(2):
                first = h * WIDTH + k * TOK
                grads[w][block, h * WIDTH : (h + 1) * WIDTH] = dot_lt(
                    m.hidden[:, first : first + TOK], m.cot2[...]
                ).astype(BF)
        elif w == UP:
            grads[w][block, :] = dot_lt(m.mlp_in[:, block], m.up_low[...]).astype(BF)
        elif w == PROJ:
            grads[w][block, :384] = dot_lt(m.attended[:, block], m.resid_half[...]).astype(BF)
            grads[w][block, 384:] = dot_lt(
                m.normed_in[chip_rows(at.chip), block], m.query_half[...]
            ).astype(BF)
        else:
            grads[w][block, :] = dot_lt(
                m.normed_in[chip_rows(at.chip), block], m.keys_half[...]
            ).astype(BF)
        ex.start(w, k)

    sides = {}

    def mlp_back():
        m.mlp_part[...] = dot_rt(m.up_low[...], m.up_w[...])
        sides["part"] = side(6, m.mlp_part.at[two_other], m.mlp_came, at.sibling)
        for h in range(2):
            for t in range(2):
                m.vec[8 + 2 * h + t : 9 + 2 * h + t, :] = jnp.where(
                    core == h, m.up_sum[:, t * WIDTH : (t + 1) * WIDTH], 0.0
                )

    def keep_resid(rows, back):
        m.resid_grad[rows, :] = back
        m.resid_low[rows, :] = back.astype(BF)

    def resid_back():
        sides["part"].wait()
        norm_back(
            lambda rows: m.mlp_part[rows_of_shift(rows, core * TOK), :] + m.mlp_came[rows, :],
            lambda rows: cot[0, rows, :].astype(F32),
            mlp_gain,
            m.hat2,
            m.fac2,
            m.vec,
            (5, 6, 4),
            keep_resid,
        )
        m.attended_grad[own, :] = dot_rt(m.resid_low[...], m.proj_w[...]).astype(BF)
        grad = m.attended_grad.at[own]
        sides["grad_far"] = side(9, grad, grad, at.across)
        sides["grad_sib"] = side(8, grad, grad, at.sibling)

    def parts(v):
        found = []
        for _ in range(3):
            found.append(v.astype(BF))
            v = v - found[-1].astype(F32)
        return found

    def extend():
        feature = lax.broadcasted_iota(jnp.int32, (WIDTH, 128), 0)
        head_of = (feature // 64 + 16 == lax.broadcasted_iota(jnp.int32, (WIDTH, 128), 1)).astype(BF)
        means = m.attended_grad[own, :].astype(F32) * m.attended_full[...]
        sums = sum(dot(p, head_of) for p in parts(means))
        ext = image_own
        for j, p in enumerate(parts(-(m.stat[...] + sums))):
            to = lax.broadcasted_iota(jnp.int32, (128, 128), 1)
            of = lax.broadcasted_iota(jnp.int32, (128, 128), 0)
            spot = jnp.where(
                of < 12, 4 + 3 * of + j, jnp.where((of >= 16) & (of < 28), 3 * of - 8 + j, -1)
            )
            ext = ext + dot(p, (to == spot).astype(BF))
        m.query_ext[own, :] = ext.astype(BF)
        ext = m.query_ext.at[own]
        sides["ext_far"] = side(12, ext, ext, at.across)
        sides["ext_sib"] = side(11, ext, ext, at.sibling)
        m.resid_half[two, :] = m.resid_low[:, cut(core * 384, 384)]
        sides["resid"] = side(
            14, m.resid_low.at[:, cut((1 - core) * 384, 384)], m.resid_half.at[two], at.sibling
        )

    def picks(i):
        a, b = lane - 4 - 6 * i, lane - 40 - 6 * i
        first = jnp.where((lane < 4) | ((a >= 0) & (a < 3)), 1.0, 0.0).astype(BF)
        second = jnp.where((lane < 4) | ((a >= 3) & (a < 6)), 1.0, 0.0).astype(BF)
        third = jnp.where((b >= 0) & (b < 3), 1.0, 0.0).astype(BF)
        fourth = jnp.where((b >= 3) & (b < 6), 1.0, 0.0).astype(BF)
        return (lambda v: jnp.concatenate((v * first, v * second), axis=0)), (
            lambda v: jnp.concatenate((v * third, v * fourth), axis=0)
        )

    def query_side(pairs):
        for i in pairs:
            cols = slice(i * 128, (i + 1) * 128)
            of_scores, of_means = picks(i)
            ext, k = m.query_ext[own, :], m.keys[:, cols]
            p = jnp.exp(
                dot_rt(beside(both(m.queries[own, cols]), of_scores(ext)), beside(k, m.key_ext[...]))
            )
            y = dot_rt(
                beside(both(m.attended_grad[own, cols]), of_means(ext)),
                beside(m.values[:, cols], m.key_ext[...]),
            )
            g = joined(dot((p * y).astype(BF), k)) * SCALE
            m.vec[2:3, cols] = jnp.sum(g, axis=0, keepdims=True)
            m.qkv_low[:, cols] = g.astype(BF)
        if PAIRS - 1 in pairs:
            sides["query"] = share(15, 0, m.query_half)

    def key_side(chip, first, pairs):
        rows = chip_rows(chip)
        for i in pairs:
            cols = slice(i * 128, (i + 1) * 128)
            of_scores, of_means = picks(i)
            q, g, ext = m.queries[rows, cols], m.attended_grad[rows, cols], m.key_ext[own, :]
            other = m.query_ext[rows, :]
            p = jnp.exp(dot_rt(beside(both(m.keys[own, cols]), of_scores(ext)), beside(q, other)))
            y = dot_rt(beside(both(m.values[own, cols]), of_means(ext)), beside(g, other))
            dv = joined(dot(p.astype(BF), g))
            dk = joined(dot((p * y).astype(BF), q))
            if first:
                m.value_grad[:, cols] = dv
                m.key_grad[:, cols] = dk
            else:
                dv = dv + m.value_grad[:, cols]
                dk = dk + m.key_grad[:, cols]
                m.vec[3:4, cols] = jnp.sum(dv, axis=0, keepdims=True)
                m.qkv_low[:, WIDTH + i * 128 : WIDTH + (i + 1) * 128] = dk.astype(BF)
                m.qkv_low[:, 2 * WIDTH + i * 128 : 2 * WIDTH + (i + 1) * 128] = dv.astype(BF)
        if not first and PAIRS - 1 in pairs:
            sides["keys"] = share(16, 1, m.keys_half.at[:, :384])
            sides["values"] = share(17, 2, m.keys_half.at[:, 384:])

    def share(i, part, target):
        target.at[two][...] = m.qkv_low[:, cut(part * WIDTH + core * 384, 384)]
        return side(
            i, m.qkv_low.at[:, cut(part * WIDTH + (1 - core) * 384, 384)], target.at[two], at.sibling
        )

    def near_ready():
        sides["grad_sib"].wait()
        sides["ext_sib"].wait()

    def proj_ready():
        att_sib.wait()
        sides["resid"].wait()
        sides["query"].wait()

    def far_here():
        project_queries(chip_rows(1 - at.chip))
        sides["grad_far"].wait()
        sides["grad_pass"] = side(
            10, m.attended_grad.at[far], m.attended_grad.at[far], at.sibling
        )
        sides["ext_far"].wait()
        sides["ext_pass"] = side(13, m.query_ext.at[far], m.query_ext.at[far], at.sibling)

    def far_ready():
        sides["grad_pass"].wait()
        sides["ext_pass"].wait()

    def keys_ready():
        sides["keys"].wait()
        sides["values"].wait()

    def keep_input(rows, back):
        input_grad[0, rows, :] = back.astype(BF)

    def input_back():
        m.attn_grad[...] = dot_rt(m.qkv_low[...], m.qkv_w[...])
        norm_back(
            lambda rows: m.attn_grad[rows, :],
            lambda rows: m.resid_grad[rows, :],
            attn_gain,
            m.hat1,
            m.fac1,
            m.vec,
            (0, 1),
            keep_input,
        )

    def vec_step(s):
        if s > 0:
            sides["vec"].wait()
            m.vec[...] = m.vec[...] + m.vec_came[s - 1]
        if s > DIMS:
            vec_out[...] = m.vec[...]
            return
        copy = pltpu.make_async_remote_copy(
            src_ref=m.vec,
            dst_ref=m.vec_came.at[s],
            send_sem=m.vec_send.at[s],
            recv_sem=m.vec_recv.at[s],
            device_id=(at.partners + (at.sibling,))[s],
            device_id_type=MESH,
        )
        copy.start()
        sides["vec"] = copy

    def feed_out():
        m.out_part[...] = dot(m.hidden[...], m.down_w[...])
        sides["out"] = side(7, m.out_part.at[two_other], m.out_came, at.sibling)

    def close():
        sides["out"].wait()
        block_output[0] = (
            m.resid[...] + (m.out_part[two, :] + m.out_came[...]) + down_bias[...]
        ).astype(BF)

    near, other_chip = at.chip, 1 - at.chip
    pieces = dict(
        mlp_back=mlp_back,
        resid_back=resid_back,
        extend=extend,
        query1=lambda: query_side(range(3)),
        query2=lambda: query_side(range(3, 6)),
        near_ready=near_ready,
        near1=lambda: key_side(near, True, range(3)),
        near2=lambda: key_side(near, True, range(3, 6)),
        proj_ready=proj_ready,
        far_here=far_here,
        far_ready=far_ready,
        far1=lambda: key_side(other_chip, False, range(3)),
        far2=lambda: key_side(other_chip, False, range(3, 6)),
        keys_ready=keys_ready,
        input_back=input_back,
        feed_out=feed_out,
        close=close,
    )
    for step in PLAN:
        if isinstance(step, str):
            pieces[step]()
        elif len(step) == 1:
            vec_step(step[0])
        elif len(step) == 2:
            start(*step)
        else:
            ex.finish(*step)

    for w in range(len(WIDTHS)):
        ex.done(w)


PLAN = (
    (0, 4), (0, 5), (0, 1), (1, 2), "mlp_back", (0, 0), (0, 3), (0, 2),
    (1, 3), (1, 0), (1, 1), "resid_back", "extend", "query1", (1, 4), "query2",
    (0, 5, 0), "near_ready", (1, 5), (0, 0, 0), (0, 3, 0), "proj_ready", (1, 2, 0), (2, 2),
    "near1", (2, 1), (2, 0), (2, 5), "near2", (0, 2, 0), (0, 4, 0), "far_here",
    (2, 3), (1, 1, 0), (2, 4), (0, 1, 0), (1, 0, 0), "far_ready", "far1", "far2",
    (0, 0, 1), (1, 5, 0), (1, 3, 0), (2, 1, 0), (0, 5, 1), (1, 4, 0), "keys_ready", (2, 2, 0),
    (2, 0, 0), (0, 2, 1), (3, 0), (3, 4), (3, 1), (2, 5, 0), (0, 3, 1), (1, 1, 1),
    (3, 5), (1, 0, 1), "input_back", (3, 2), (0, 1, 1), (2, 4, 0), (3, 3), (0, 4, 1),
    (1, 5, 1), (1, 4, 1), (0, 5, 2), (2, 2, 1), (2, 3, 0), (2, 0, 1), (3, 0, 0), (0, 0, 2),
    (0, 3, 2), (3, 1, 0), (0,), (1, 3, 1), (2, 1, 1), (1, 1, 2), (1, 2, 1), (1, 0, 2),
    (2, 5, 1), (0, 2, 2), (1, 5, 2), (0, 4, 2), (3, 5, 0), (3, 4, 0), (2, 2, 2), (0, 5, 3),
    (1, 4, 2), (0, 1, 2), (3, 2, 0), (2, 4, 1), (3, 3, 0), (2, 3, 1), (0, 3, 3), (2, 1, 2),
    (3, 1, 1), (1, 3, 2), (1,), (2, 5, 2), (1, 1, 3), (0, 0, 3), (0, 2, 3), (2, 0, 2),
    (1, 0, 3), (0, 4, 3), (3, 0, 1), (3, 5, 1), (1, 2, 2), (1, 5, 3), (3, 4, 1), (1, 4, 3),
    (2, 4, 2), (2, 2, 3), (0, 5, 4), (0, 1, 3), (2, 3, 2), (3, 2, 1), (3, 3, 1), (0, 3, 4),
    (3, 1, 2), (2, 5, 3), (1, 3, 3), (2, 0, 3), (1, 1, 4), (0, 4, 4), (2, 1, 3), (3, 5, 2),
    (0, 0, 4), (3, 0, 2), (0, 2, 4), (1, 2, 3), (2,), (1, 0, 4), (1, 4, 4), (2, 2, 4),
    (0, 5, 5), (2, 4, 3), (2, 3, 3), (1, 5, 4), (0, 1, 4), (0, 3, 5), (3, 2, 2), (2, 5, 4),
    (3, 3, 2), (3, 1, 3), (3, 4, 2), (3, 5, 3), (1, 3, 4), (0, 0, 5), (0, 2, 5), (0, 4, 5),
    (3, 0, 3), (1, 1, 5), (2, 1, 4), (1, 2, 4), (1, 0, 5), (1, 4, 5), (2, 2, 5), (3,),
    (2, 0, 4), (0, 1, 5), (0, 5, 6), (1, 5, 5), (2, 3, 4), (0, 3, 6), (3, 2, 3), (3, 5, 4),
    (3, 4, 3), (2, 4, 4), (2, 5, 5), (0, 2, 6), (3, 1, 4), (0, 4, 6), (0, 0, 6), (2, 1, 5),
    (3, 0, 4), (1, 3, 5), (1, 2, 5), (1, 0, 6), (1, 1, 6), (1, 4, 6), (2, 2, 6), (4,),
    (0, 5, 7), (0, 1, 6), (3, 4, 4), (2, 0, 5), (0, 3, 7), (2, 3, 5), (3, 2, 4), (3, 1, 5),
    (2, 1, 6), (3, 3, 3), (0, 2, 7), (0, 4, 7), (0, 0, 7), (2, 4, 5), (1, 3, 6), (1, 5, 6),
    (1, 2, 6), (3, 0, 5), (2, 2, 7), (2, 5, 6), (3, 5, 5), (3, 2, 5), (0, 5, 8), (2, 0, 6),
    (3, 3, 4), (1, 4, 7), (0, 3, 8), (0, 1, 7), (1, 1, 7), (3, 4, 5), (1, 0, 7), "feed_out",
    (3, 1, 6), (0, 2, 8), (2, 3, 6), (3, 3, 5), (3, 2, 6), (5,), (0, 4, 8), (2, 0, 7),
    (3, 5, 6), (2, 4, 6), (3, 4, 6), (1, 3, 7), (1, 5, 7), (1, 2, 7), (3, 0, 6), (0, 0, 8),
    (2, 1, 7), (1, 1, 8), (3, 3, 6), (0, 5, 9), (0, 1, 8), (2, 2, 8), (3, 1, 7), (0, 3, 9),
    (3, 4, 7), (2, 4, 7), (2, 3, 7), (6,), (1, 0, 8), (1, 4, 8), (0, 2, 9), (3, 5, 7),
    "close", (2, 5, 7), (2, 0, 8), (3, 2, 7), (0, 4, 9), (3, 0, 7), (3, 3, 7), (7,),
    (2, 1, 8), (1, 3, 8), (1, 5, 8), (1, 2, 8), (0, 0, 9), (0, 1, 9), (3, 4, 8), (2, 3, 8),
    (3, 5, 8), (3, 2, 8), (3, 1, 8), (3, 0, 8), (2, 4, 8), (3, 3, 8), (2, 5, 8),
)


def rows_of_shift(rows, shift):
    return pl.ds(pl.multiple_of(rows.start + shift, 16), rows.size)


def spread_kernel(
    wide,
    slim,
    vec,
    block_output_in,
    input_grad_in,
    block_output,
    input_grad,
    attn_gain,
    attn_shift,
    qkv,
    query_bias,
    value_bias,
    proj,
    proj_bias,
    mlp_gain,
    mlp_shift,
    up,
    up_bias,
    down,
    down_bias,
):
    rows = rows_of(pl.program_id(0) * SPREAD_ROWS, SPREAD_ROWS)
    for c in range(2):
        up[:, c * HALF : (c + 1) * HALF] = wide[1, c, rows, :].astype(F32)
        proj[:, c * 384 : (c + 1) * 384] = slim[0, c, rows, :384].astype(F32)
        for part in range(3):
            first = part * WIDTH + c * 384
            source = slim[0, c, rows, 384:] if part == 0 else slim[1, c, rows, (part - 1) * 384 : part * 384]
            qkv[:, first : first + 384] = source.astype(F32)
        for h in range(2):
            down[2 * c + h] = wide[0, c, rows, h * WIDTH : (h + 1) * WIDTH].astype(F32)

    @pl.when(pl.program_id(0) == 0)
    def _():
        block_output[...] = block_output_in[...]
        input_grad[...] = input_grad_in[...]
        for row, ref in enumerate(
            (attn_gain, attn_shift, query_bias, value_bias, proj_bias, mlp_gain, mlp_shift, down_bias)
        ):
            ref[...] = vec[row]
        for t in range(4):
            up_bias[t * WIDTH : (t + 1) * WIDTH] = vec[8 + t]


SPREAD_ROWS = 64


def spread(*given):
    rows = SPREAD_ROWS
    line = lambda n: (jax.ShapeDtypeStruct((n,), F32), pl.BlockSpec((n,), lambda i: (0,)))
    flat = lambda n: (jax.ShapeDtypeStruct((WIDTH, n), F32), pl.BlockSpec((rows, n), lambda i: (i, 0)))
    tokens = (jax.ShapeDtypeStruct((1, TOK, WIDTH), BF), pl.BlockSpec((1, TOK, WIDTH), lambda i: (0, 0, 0)))
    outs = [
        tokens,
        tokens,
        line(WIDTH),
        line(WIDTH),
        flat(3 * WIDTH),
        line(WIDTH),
        line(WIDTH),
        flat(WIDTH),
        line(WIDTH),
        line(WIDTH),
        line(WIDTH),
        flat(HIDDEN),
        line(HIDDEN),
        (
            jax.ShapeDtypeStruct((4, WIDTH, WIDTH), F32),
            pl.BlockSpec((4, rows, WIDTH), lambda i: (0, i, 0)),
        ),
        line(WIDTH),
    ]
    return pl.pallas_call(
        spread_kernel,
        grid=(WIDTH // rows,),
        out_shape=[o[0] for o in outs],
        in_specs=[pl.BlockSpec(memory_space=pltpu.VMEM)] * len(given),
        out_specs=[o[1] for o in outs],
        compiler_params=pltpu.CompilerParams(vmem_limit_bytes=24 << 20),
    )(*(pltpu.with_memory_space_constraint(v, pltpu.VMEM) for v in given))


def body(
    block_input,
    out_cotangent,
    image_lengths,
    span_order,
    attn_gain,
    attn_shift,
    qkv_weight,
    query_bias,
    value_bias,
    proj_weight,
    proj_bias,
    mlp_gain,
    mlp_shift,
    up_weight,
    up_bias,
    down_weight,
    down_bias,
):
    vmem = pl.BlockSpec(memory_space=pltpu.VMEM)
    hbm = pl.BlockSpec(memory_space=pl.ANY)
    held = scratch()
    block_output, input_grad, wide, slim, vec = pl.pallas_call(
        kernel,
        out_shape=[
            pltpu.VMEM((1, TOK, WIDTH), BF),
            pltpu.VMEM((1, TOK, WIDTH), BF),
            pltpu.VMEM((2, 2, WIDTH, HALF), BF),
            pltpu.VMEM((2, 2, WIDTH, WIDTH), BF),
            pltpu.VMEM((16, WIDTH), F32),
        ],
        in_specs=[pl.BlockSpec(memory_space=pltpu.SMEM)] * 2 + [vmem] * 11 + [hbm] * 4,
        out_specs=[vmem] * 5,
        scratch_shapes=[held[name] for name in NAMES],
        compiler_params=pltpu.CompilerParams(
            collective_id=0, has_side_effects=True, vmem_limit_bytes=VMEM_LIMIT
        ),
    )(
        image_lengths,
        span_order,
        block_input,
        out_cotangent,
        attn_gain,
        attn_shift,
        query_bias,
        value_bias,
        proj_bias,
        mlp_gain,
        mlp_shift,
        up_bias,
        down_bias,
        qkv_weight,
        proj_weight,
        up_weight,
        down_weight,
    )
    outs = list(spread(wide, slim, vec, block_output, input_grad))
    outs[13] = outs[13].reshape(HIDDEN, WIDTH)
    return tuple(outs)


VMEM_LIMIT = 46 << 20


def solution(mesh):
    tokens = P("rows", "seq", None)
    return jax.shard_map(
        body,
        mesh=mesh,
        in_specs=(tokens, tokens, P("rows", None), P("rows", None)) + (P(),) * 13,
        out_specs=(tokens, tokens) + (P(),) * 13,
        check_vma=False,
    )
```

```python
from types import SimpleNamespace

import jax
import jax.numpy as jnp
from jax import lax
from jax.experimental import pallas as pl
from jax.experimental.pallas import tpu as pltpu
from jax.sharding import PartitionSpec as P

MESH = pl.DeviceIdType.MESH
BF, F32 = jnp.bfloat16, jnp.float32
WIDTH = 768
HIDDEN = 3072
HALF = HIDDEN // 2
TOK = 128
LEN = 512
PAIRS = 6
SCALE = 64**-0.5
EPSILON = 1e-6

DIMS = 6
DOWN, UP, PROJ, KEYS = range(4)
WIDTHS = (HALF, HALF, WIDTH, WIDTH)
HALVINGS = (4, 3, 3, 3)

TAIL = (
    0.14361835615286447,
    0.14366105191010822,
    0.12424683572786965,
    0.09467827005043768,
    0.003990377379362003,
    0.09912410558005538,
    -0.21460327937017376,
    0.13425173188400444,
    -0.02896737861797067,
)
DENSITY = 0.3989422804014327


def rows_of(start, size):
    return pl.ds(pl.multiple_of(start, size), size)


def dot(a, b):
    return lax.dot_general(a, b, (((1,), (0,)), ((), ())), preferred_element_type=F32)


def dot_rt(a, b):
    return lax.dot_general(a, b, (((1,), (1,)), ((), ())), preferred_element_type=F32)


def dot_lt(a, b):
    return lax.dot_general(a, b, (((0,), (0,)), ((), ())), preferred_element_type=F32)


def place():
    row, seq = lax.axis_index("rows"), lax.axis_index("seq")
    x, y, z_lo = row % 4, (row // 4) % 4, row // 16
    z_hi, core = seq // 2, seq % 2
    z = z_hi * 2 + z_lo

    def device(x, y, z, core):
        return ((z % 2) * 16 + y * 4 + x, (z // 2) * 2 + core)

    near = lambda v: v + 1 - 2 * (v % 2)
    far = lambda v: 3 - v
    first = lambda v: (v % 2 + v // 2) % 2
    return SimpleNamespace(
        seq=seq,
        core=core,
        chip=z_hi,
        partners=(
            device(near(x), y, z, core),
            device(far(x), y, z, core),
            device(x, near(y), z, core),
            device(x, far(y), z, core),
            device(x, y, near(z), core),
            device(x, y, far(z), core),
        ),
        bits=(first(x), x // 2, first(y), y // 2, first(z), z // 2),
        sibling=(row, z_hi * 2 + 1 - core),
        across=(row, (1 - z_hi) * 2 + core),
    )


class Exchange:
    def __init__(self, at, grads, whole, landing, send_sem, recv_sem, over_sem):
        self.at = at
        self.grads, self.whole, self.landing = grads, whole, landing
        self.send_sem, self.recv_sem, self.over_sem = send_sem, recv_sem, over_sem
        self.copies = {}

    def dim(self, k, s):
        return (k + s) % DIMS

    def rows(self, k, s):
        low = TOK * k
        for t in range(min(s, 3)):
            low = low + self.at.bits[self.dim(k, t)] * (64 >> t)
        return low

    def block(self, w, k, s, mine, whole=False):
        held = self.whole[w].at[self.at.core] if whole else self.grads[w]
        bit = self.at.bits[self.dim(k, s)]
        pick = bit if mine else 1 - bit
        if w == DOWN:
            half = lambda p: pl.ds(pl.multiple_of(p * WIDTH, 128), WIDTH)
            if s == 0:
                return held.at[pl.ds(TOK * k, TOK), half(pick)]
            low = TOK * k + pick * (64 >> (s - 1))
            for t in range(1, s):
                low = low + self.at.bits[self.dim(k, t)] * (64 >> (t - 1))
            return held.at[pl.ds(pl.multiple_of(low, 16), 64 >> (s - 1)), half(self.at.bits[k])]
        if s < 3:
            size = 64 >> s
            return held.at[pl.ds(pl.multiple_of(self.rows(k, s) + pick * size, 16), size)]
        width = WIDTHS[w] // 2
        return held.at[
            pl.ds(pl.multiple_of(self.rows(k, 3), 16), 16),
            pl.ds(pl.multiple_of(pick * width, 128), width),
        ]

    def slot(self, w, k, s):
        held = self.landing[w].at[k]
        if w == DOWN:
            return held.at[pl.ds((0, 64, 96, 112, 128)[s - 1], (64, 32, 16, 16, 16)[s - 1]), pl.ds(0, WIDTH)]
        if s < 3:
            return held.at[pl.ds((0, 64, 96)[s], 64 >> s)]
        if HALVINGS[w] == 3:
            return held.at[pl.ds(64 + 16 * s, 16)]
        width = WIDTHS[w] // 2
        return held.at[pl.ds((112, 112, 128)[s - 3], 16), pl.ds((0, width, 0)[s - 3], width)]

    def start(self, w, k, s=0):
        last = HALVINGS[w] - 1
        if s <= last:
            src, dst, d = self.block(w, k, s, False), self.slot(w, k, s), self.dim(k, s)
        elif s < DIMS:
            src, dst, d = self.block(w, k, last, True), self.slot(w, k, s), self.dim(k, s)
        else:
            t = last + DIMS - s
            src = dst = self.block(w, k, t, True, True)
            d = self.dim(k, t)
        copy = pltpu.make_async_remote_copy(
            src_ref=src,
            dst_ref=dst,
            send_sem=self.send_sem.at[w, k],
            recv_sem=self.recv_sem.at[w, k, s],
            device_id=self.at.partners[d],
            device_id_type=MESH,
        )
        copy.start()
        self.copies[w, k, s] = copy

    def over(self, w, k, part):
        half = self.block(w, k, 0, part == 0, True)
        self.crossing(w, half, half).start()

    def crossing(self, w, src, dst):
        return pltpu.make_async_remote_copy(
            src_ref=src,
            dst_ref=dst,
            send_sem=self.over_sem.at[0, w],
            recv_sem=self.over_sem.at[1, w],
            device_id=self.at.sibling,
            device_id_type=MESH,
        )

    def done(self, w):
        self.crossing(w, self.whole[w].at[self.at.core], self.whole[w].at[1 - self.at.core]).wait()

    def finish(self, w, k, s):
        steps, last = DIMS + HALVINGS[w], HALVINGS[w] - 1
        self.copies[w, k, s].wait()
        if s < DIMS:
            kept, slot = self.block(w, k, min(s, last), True), self.slot(w, k, s)
            total = (kept[...].astype(F32) + slot[...].astype(F32)).astype(BF)
            if s < DIMS - 1:
                kept[...] = total
            else:
                self.block(w, k, last, True, True)[...] = total
        if s < steps - 1:
            self.start(w, k, s + 1)
        if s >= steps - 2:
            self.over(w, k, s - (steps - 2))


def normalize(load, gain, shift, normed, factor, result, base):
    def step(i, carry):
        rows = rows_of(i * 16, 16)
        v = load(rows)
        c = v - jnp.mean(v, axis=1, keepdims=True)
        f = lax.rsqrt(jnp.mean(c * c, axis=1, keepdims=True) + EPSILON)
        n = c * f
        normed[rows, :] = n
        factor[rows, :] = f
        result[rows_of(base + i * 16, 16), :] = (n * gain[...] + shift[...]).astype(BF)
        return carry

    lax.fori_loop(0, TOK // 16, step, 0, unroll=True)


def folded(v):
    return jnp.sum(v.reshape(2, 8, WIDTH), axis=0)


def norm_back(load_grad, load_rest, gain, normed, factor, vec, where, keep):
    zero = jnp.zeros((8, WIDTH), F32)

    def step(i, carry):
        rows = rows_of(i * 16, 16)
        e, n = load_grad(rows), normed[rows, :]
        g = e * gain[...]
        a = jnp.mean(g, axis=1, keepdims=True)
        b = jnp.mean(g * n, axis=1, keepdims=True)
        back = load_rest(rows) + factor[rows, :] * (g - a - n * b)
        keep(rows, back)
        return carry[0] + folded(e * n), carry[1] + folded(e), carry[2] + folded(back)

    sums = lax.fori_loop(0, TOK // 16, step, (zero, zero, zero), unroll=True)
    for row, total in zip(where, sums):
        vec[row : row + 1, :] = jnp.sum(total, axis=0, keepdims=True)


def scratch():
    v = pltpu.VMEM
    dma = pltpu.SemaphoreType.DMA
    sets = len(WIDTHS)
    return dict(
        qkv_w=v((WIDTH, 3 * WIDTH), BF),
        proj_w=v((WIDTH, WIDTH), BF),
        up_w=v((WIDTH, HALF), BF),
        down_w=v((HALF, WIDTH), BF),
        lines=v((8, WIDTH), F32),
        up_bias_half=v((1, HALF), F32),
        up_sum=v((1, HALF), F32),
        normed_in=v((LEN, WIDTH), BF),
        queries=v((LEN, WIDTH), BF),
        keys=v((LEN, WIDTH), BF),
        values=v((LEN, WIDTH), BF),
        key_ext=v((LEN, 128), BF),
        query_ext=v((LEN, 128), BF),
        stat=v((TOK, 128), F32),
        hat1=v((TOK, WIDTH), F32),
        fac1=v((TOK, 1), F32),
        attended_full=v((TOK, WIDTH), F32),
        attended=v((2 * TOK, WIDTH), BF),
        resid=v((TOK, WIDTH), F32),
        hat2=v((TOK, WIDTH), F32),
        fac2=v((TOK, 1), F32),
        mlp_in=v((2 * TOK, WIDTH), BF),
        cot2=v((2 * TOK, WIDTH), BF),
        hidden_grad=v((2 * TOK, HALF), F32),
        hidden=v((2 * TOK, HALF), BF),
        cot_near=v((2, DIMS, TOK, WIDTH), BF),
        hidden_near=v((DIMS, 2 * TOK, 128), BF),
        up_low=v((2 * TOK, HALF), BF),
        mlp_part=v((2 * TOK, WIDTH), F32),
        mlp_came=v((TOK, WIDTH), F32),
        out_part=v((2 * TOK, WIDTH), F32),
        out_came=v((TOK, WIDTH), F32),
        resid_grad=v((TOK, WIDTH), F32),
        resid_low=v((TOK, WIDTH), BF),
        attended_grad=v((LEN, WIDTH), BF),
        qkv_low=v((TOK, 3 * WIDTH), BF),
        resid_half=v((2 * TOK, 384), BF),
        query_half=v((2 * TOK, 384), BF),
        keys_half=v((2 * TOK, WIDTH), BF),
        key_grad=v((TOK, WIDTH), F32),
        value_grad=v((TOK, WIDTH), F32),
        attn_grad=v((TOK, WIDTH), F32),
        vec=v((16, WIDTH), F32),
        vec_came=v((DIMS + 1, 16, WIDTH), F32),
        grads_wide=v((2, WIDTH, HALF), BF),
        grads_slim=v((2, WIDTH, WIDTH), BF),
        landing_wide=v((2, DIMS, 160, HALF), BF),
        landing_slim=v((2, DIMS, 160, WIDTH), BF),
        send_sem=dma((sets, DIMS)),
        recv_sem=dma((sets, DIMS, DIMS + max(HALVINGS))),
        over_sem=dma((2, sets)),
        side_send=dma((22,)),
        side_recv=dma((22,)),
        vec_send=dma((DIMS + 1,)),
        vec_recv=dma((DIMS + 1,)),
        load_sem=dma((4,)),
        near_sem=dma((4,)),
        slice_sem=dma((1 + DIMS,)),
    )


NAMES = tuple(scratch())


def kernel(
    lengths,
    order,
    x,
    cot,
    attn_gain,
    attn_shift,
    query_bias,
    value_bias,
    proj_bias,
    mlp_gain,
    mlp_shift,
    up_bias,
    down_bias,
    qkv_weight,
    proj_weight,
    up_weight,
    down_weight,
    block_output,
    input_grad,
    whole_wide,
    whole_slim,
    vec_out,
    *refs,
):
    m = SimpleNamespace(**dict(zip(NAMES, refs)))
    at = place()
    core, seq = at.core, at.seq
    pair_of = lambda wide, slim: (wide.at[0], wide.at[1], slim.at[0], slim.at[1])
    grads = pair_of(m.grads_wide, m.grads_slim)
    ex = Exchange(
        at,
        grads,
        pair_of(whole_wide, whole_slim),
        pair_of(m.landing_wide, m.landing_slim),
        m.send_sem,
        m.recv_sem,
        m.over_sem,
    )

    barrier = pltpu.get_barrier_semaphore()
    for device in at.partners + (at.sibling, at.across):
        pl.semaphore_signal(barrier, inc=1, device_id=device, device_id_type=MESH)

    loads = [
        pltpu.make_async_copy(src, dst, m.load_sem.at[i])
        for i, (src, dst) in enumerate(
            (
                (qkv_weight, m.qkv_w),
                (down_weight.at[rows_of(core * HALF, HALF)], m.down_w),
                (proj_weight, m.proj_w),
                (up_weight.at[:, rows_of(core * HALF, HALF)], m.up_w),
            )
        )
    ]
    for load in loads:
        load.start()

    def side(i, src, dst, device):
        copy = pltpu.make_async_remote_copy(
            src_ref=src,
            dst_ref=dst,
            send_sem=m.side_send.at[i],
            recv_sem=m.side_recv.at[i],
            device_id=device,
            device_id_type=MESH,
        )
        copy.start()
        return copy

    own = rows_of(seq * TOK, TOK)
    two = rows_of(core * TOK, TOK)
    two_other = rows_of((1 - core) * TOK, TOK)
    far_block = (1 - at.chip) * 2 + core
    far = rows_of(far_block * TOK, TOK)
    chip_rows = lambda chip: rows_of(chip * 2 * TOK, 2 * TOK)
    cut = lambda start, size: pl.ds(pl.multiple_of(start, 128), size)

    vectors = (attn_gain, attn_shift, query_bias, value_bias, proj_bias, mlp_gain, mlp_shift, down_bias)
    for i, vector in enumerate(vectors):
        m.lines[i : i + 1, :] = vector[...][None]
    attn_gain, attn_shift, query_bias, value_bias, proj_bias, mlp_gain, mlp_shift, down_bias = (
        m.lines.at[i : i + 1] for i in range(8)
    )

    normalize(
        lambda rows: x[0, rows, :].astype(F32), attn_gain, attn_shift, m.hat1, m.fac1, m.normed_in, seq * TOK
    )
    m.cot2[two, :] = cot[0]

    pl.semaphore_wait(barrier, DIMS + 2)
    in_far = []
    for i in range(2):
        piece = m.normed_in.at[rows_of((seq * 2 + i) * 64, 64)]
        in_far.append(side((1, 18)[i], piece, piece, at.across))
    in_sib = side(0, m.normed_in.at[own], m.normed_in.at[own], at.sibling)
    cot_sib = side(3, m.cot2.at[two], m.cot2.at[two], at.sibling)

    def near_copy(i, src, dst, device):
        return pltpu.make_async_remote_copy(
            src_ref=src,
            dst_ref=dst,
            send_sem=m.near_sem.at[i],
            recv_sem=m.near_sem.at[i + 1],
            device_id=device,
            device_id_type=MESH,
        )

    for d in range(DIMS):
        near_copy(0, m.cot2.at[two], m.cot_near.at[core, d], at.partners[d]).start()

    ends = [lengths[0, 0]]
    for i in (1, 2):
        ends.append(ends[-1] + lengths[0, i])
    lane = lax.broadcasted_iota(jnp.int32, (1, 128), 1)
    token = lax.broadcasted_iota(jnp.int32, (TOK, 128), 0)

    def image(j):
        t = token + order[0, j] * TOK
        return sum((t >= end).astype(jnp.int32) for end in ends)

    for j in range(4):
        other = jnp.where(lane == image(j), 0.0, -1e30)
        m.key_ext[j * TOK : (j + 1) * TOK, :] = jnp.where(lane < 4, other, jnp.where(lane < 76, 1.0, 0.0)).astype(BF)
    image_own = jnp.where(lane == image(seq), 1.0, 0.0)
    m.query_ext[own, :] = image_own.astype(BF)
    m.up_bias_half[...] = jnp.where(core == 0, up_bias[:HALF], up_bias[HALF:])[None]
    m.vec[...] = jnp.zeros((16, WIDTH), F32)
    m.vec[7:8, :] = jnp.sum(
        jnp.sum(cot[0].astype(F32).reshape(TOK // 8, 8, WIDTH), axis=0), axis=0, keepdims=True
    )
    m.stat[...] = jnp.zeros((TOK, 128), F32)
    low_lanes = (lane < 64).astype(BF)
    high_lanes = (lane >= 64).astype(BF)

    def both(v):
        return jnp.concatenate((v * low_lanes, v * high_lanes), axis=0)

    def joined(v):
        return jnp.where(lane < 64, v[:TOK], v[TOK:])

    def beside(a, b):
        return jnp.concatenate((a, b), axis=1)

    def project_keys(rows):
        a = m.normed_in[rows, :]
        m.keys[rows, :] = dot(a, m.qkv_w[:, WIDTH : 2 * WIDTH]).astype(BF)
        m.values[rows, :] = (dot(a, m.qkv_w[:, 2 * WIDTH :]) + value_bias[...]).astype(BF)

    def project_queries(rows):
        part = dot(m.normed_in[rows, :], m.qkv_w[:, :WIDTH])
        m.queries[rows, :] = ((part + query_bias[...]) * SCALE).astype(BF)

    loads[0].wait()
    in_sib.wait()
    project_keys(chip_rows(at.chip))
    project_queries(chip_rows(at.chip))
    loads[1].wait()
    cot_sib.wait()
    m.hidden_grad[...] = dot_rt(m.cot2[...], m.down_w[...])
    in_pass = []
    for i in range(2):
        in_far[i].wait()
        piece = m.normed_in.at[rows_of((far_block * 2 + i) * 64, 64)]
        in_pass.append(side((2, 19)[i], piece, piece, at.sibling))
    project_keys(far)
    for copy in in_pass:
        copy.wait()
    project_keys(rows_of(((1 - at.chip) * 2 + 1 - core) * TOK, TOK))

    def attend(i, carry):
        cols = rows_of(i * 128, 128)
        ext = m.query_ext[own, :]
        s = dot_rt(
            beside(both(m.queries[own, cols]), jnp.concatenate((ext, ext), axis=0)),
            beside(m.keys[:, cols], m.key_ext[...]),
        )
        top = jnp.max(s, axis=1, keepdims=True)
        e = jnp.exp(s - top).astype(BF)
        out = dot(e, beside(m.values[:, cols], jnp.ones((LEN, 128), BF)))
        total = out[:, 128:]
        out = joined(out[:, :128] * (1.0 / total))
        m.attended_full[:, cols] = out
        m.attended[two, cols] = out.astype(BF)
        logs = top + jnp.log(total)
        m.stat[...] = jnp.where(
            lane == 2 * i, logs[:TOK], jnp.where(lane == 2 * i + 1, logs[TOK:], m.stat[...])
        )
        return carry

    lax.fori_loop(0, PAIRS, attend, 0, unroll=True)

    loads[2].wait()
    m.resid[...] = x[0].astype(F32) + dot(m.attended[two, :], m.proj_w[...]) + proj_bias[...]
    normalize(lambda rows: m.resid[rows, :], mlp_gain, mlp_shift, m.hat2, m.fac2, m.mlp_in, core * TOK)
    mlp_sib = side(4, m.mlp_in.at[two], m.mlp_in.at[two], at.sibling)
    att_sib = side(5, m.attended.at[two], m.attended.at[two], at.sibling)
    near_copy(0, m.cot_near.at[core], m.cot_near.at[core], at.sibling).wait()
    near_pass = near_copy(2, m.cot_near.at[core], m.cot_near.at[core], at.sibling)
    near_pass.start()
    loads[3].wait()

    def slice_copy(k, src, dst):
        return pltpu.make_async_remote_copy(
            src_ref=src,
            dst_ref=dst,
            send_sem=m.slice_sem.at[0],
            recv_sem=m.slice_sem.at[1 + k],
            device_id=at.partners[k],
            device_id_type=MESH,
        )

    slices = []

    def feed(rows, first):
        for i in range(3):
            cols = slice(i * 512, (i + 1) * 512)
            u = dot(m.mlp_in[rows, :], m.up_w[:, cols]) + m.up_bias_half[:, cols]
            t = 1.0 / (1.0 + 0.36 * jnp.abs(u))
            tail = jnp.full_like(t, TAIL[-1])
            for c in TAIL[-2::-1]:
                tail = tail * t + c
            e = jnp.exp(-0.5 * (u * u))
            tail = tail * (t * e)
            phi = jnp.where(u >= 0, 1.0 - tail, tail)
            m.hidden[rows, cols] = (u * phi).astype(BF)
            g = m.hidden_grad[rows, cols] * (phi + u * (DENSITY * e))
            m.up_low[rows, cols] = g.astype(BF)
            total = jnp.sum(g.reshape(TOK // 8, 8, 512), axis=0)
            total = jnp.sum(total, axis=0, keepdims=True)
            m.up_sum[:, cols] = total if first else m.up_sum[:, cols] + total
            if not first:
                for k in (2 * i, 2 * i + 1):
                    units = cut(256 * k + 128 * (1 - at.bits[k]), 128)
                    slices.append(slice_copy(k, m.hidden.at[:, units], m.hidden_near.at[k]))
                    slices[k].start()

    feed(two, True)
    mlp_sib.wait()
    feed(two_other, False)

    def block_of(k):
        return slice(k * TOK, (k + 1) * TOK)

    def start(w, k):
        block = block_of(k)
        if w == DOWN:
            if near_waits:
                near_waits.pop().wait()
            slices[k].wait_recv()
            units = cut(256 * k + 128 * at.bits[k], 128)
            total = dot_lt(m.hidden[:, units], m.cot2[...])
            for c in range(2):
                total = total + dot_lt(m.hidden_near[k, c * TOK : (c + 1) * TOK], m.cot_near[c, k])
            grads[w][block, cut(at.bits[k] * WIDTH, WIDTH)] = total.astype(BF)
            ex.start(w, k, 1)
            return
        if w == UP:
            grads[w][block, :] = dot_lt(m.mlp_in[:, block], m.up_low[...]).astype(BF)
        elif w == PROJ:
            grads[w][block, :384] = dot_lt(m.attended[:, block], m.resid_half[...]).astype(BF)
            grads[w][block, 384:] = dot_lt(
                m.normed_in[chip_rows(at.chip), block], m.query_half[...]
            ).astype(BF)
        else:
            grads[w][block, :] = dot_lt(
                m.normed_in[chip_rows(at.chip), block], m.keys_half[...]
            ).astype(BF)
        ex.start(w, k)

    sides = {}
    near_waits = [near_pass]

    def mlp_back():
        m.mlp_part[...] = dot_rt(m.up_low[...], m.up_w[...])
        sides["part"] = side(6, m.mlp_part.at[two_other], m.mlp_came, at.sibling)
        for h in range(2):
            for t in range(2):
                m.vec[8 + 2 * h + t : 9 + 2 * h + t, :] = jnp.where(
                    core == h, m.up_sum[:, t * WIDTH : (t + 1) * WIDTH], 0.0
                )

    def keep_resid(rows, back):
        m.resid_grad[rows, :] = back
        m.resid_low[rows, :] = back.astype(BF)

    def resid_back():
        sides["part"].wait()
        norm_back(
            lambda rows: m.mlp_part[rows_of_shift(rows, core * TOK), :] + m.mlp_came[rows, :],
            lambda rows: cot[0, rows, :].astype(F32),
            mlp_gain,
            m.hat2,
            m.fac2,
            m.vec,
            (5, 6, 4),
            keep_resid,
        )
        m.attended_grad[own, :] = dot_rt(m.resid_low[...], m.proj_w[...]).astype(BF)
        grad = m.attended_grad.at[own]
        for i in range(2):
            piece = m.attended_grad.at[rows_of((seq * 2 + i) * 64, 64)]
            sides["grad_far", i] = side((9, 20)[i], piece, piece, at.across)
        sides["grad_sib"] = side(8, grad, grad, at.sibling)

    def parts(v):
        found = []
        for _ in range(3):
            found.append(v.astype(BF))
            v = v - found[-1].astype(F32)
        return found

    def extend():
        feature = lax.broadcasted_iota(jnp.int32, (WIDTH, 128), 0)
        head_of = (feature // 64 + 16 == lax.broadcasted_iota(jnp.int32, (WIDTH, 128), 1)).astype(BF)
        means = m.attended_grad[own, :].astype(F32) * m.attended_full[...]
        sums = sum(dot(p, head_of) for p in parts(means))
        ext = image_own
        for j, p in enumerate(parts(-(m.stat[...] + sums))):
            to = lax.broadcasted_iota(jnp.int32, (128, 128), 1)
            of = lax.broadcasted_iota(jnp.int32, (128, 128), 0)
            spot = jnp.where(
                of < 12, 4 + 3 * of + j, jnp.where((of >= 16) & (of < 28), 3 * of - 8 + j, -1)
            )
            ext = ext + dot(p, (to == spot).astype(BF))
        m.query_ext[own, :] = ext.astype(BF)
        ext = m.query_ext.at[own]
        sides["ext_far"] = side(12, ext, ext, at.across)
        sides["ext_sib"] = side(11, ext, ext, at.sibling)
        m.resid_half[two, :] = m.resid_low[:, cut(core * 384, 384)]
        sides["resid"] = side(
            14, m.resid_low.at[:, cut((1 - core) * 384, 384)], m.resid_half.at[two], at.sibling
        )

    def picks(i):
        a, b = lane - 4 - 6 * i, lane - 40 - 6 * i
        first = jnp.where((lane < 4) | ((a >= 0) & (a < 3)), 1.0, 0.0).astype(BF)
        second = jnp.where((lane < 4) | ((a >= 3) & (a < 6)), 1.0, 0.0).astype(BF)
        third = jnp.where((b >= 0) & (b < 3), 1.0, 0.0).astype(BF)
        fourth = jnp.where((b >= 3) & (b < 6), 1.0, 0.0).astype(BF)
        return (lambda v: jnp.concatenate((v * first, v * second), axis=0)), (
            lambda v: jnp.concatenate((v * third, v * fourth), axis=0)
        )

    def query_side(pairs):
        for i in pairs:
            cols = slice(i * 128, (i + 1) * 128)
            of_scores, of_means = picks(i)
            ext, k = m.query_ext[own, :], m.keys[:, cols]
            p = jnp.exp(
                dot_rt(beside(both(m.queries[own, cols]), of_scores(ext)), beside(k, m.key_ext[...]))
            )
            y = dot_rt(
                beside(both(m.attended_grad[own, cols]), of_means(ext)),
                beside(m.values[:, cols], m.key_ext[...]),
            )
            g = joined(dot((p * y).astype(BF), k)) * SCALE
            m.vec[2:3, cols] = jnp.sum(g, axis=0, keepdims=True)
            m.qkv_low[:, cols] = g.astype(BF)
        if PAIRS - 1 in pairs:
            sides["query"] = share(15, 0, m.query_half)

    def key_side(chip, first, pairs):
        rows = chip_rows(chip)
        for i in pairs:
            cols = slice(i * 128, (i + 1) * 128)
            of_scores, of_means = picks(i)
            q, g, ext = m.queries[rows, cols], m.attended_grad[rows, cols], m.key_ext[own, :]
            other = m.query_ext[rows, :]
            p = jnp.exp(dot_rt(beside(both(m.keys[own, cols]), of_scores(ext)), beside(q, other)))
            y = dot_rt(beside(both(m.values[own, cols]), of_means(ext)), beside(g, other))
            dv = joined(dot(p.astype(BF), g))
            dk = joined(dot((p * y).astype(BF), q))
            if first:
                m.value_grad[:, cols] = dv
                m.key_grad[:, cols] = dk
            else:
                dv = dv + m.value_grad[:, cols]
                dk = dk + m.key_grad[:, cols]
                m.vec[3:4, cols] = jnp.sum(dv, axis=0, keepdims=True)
                m.qkv_low[:, WIDTH + i * 128 : WIDTH + (i + 1) * 128] = dk.astype(BF)
                m.qkv_low[:, 2 * WIDTH + i * 128 : 2 * WIDTH + (i + 1) * 128] = dv.astype(BF)
        if not first and PAIRS - 1 in pairs:
            sides["keys"] = share(16, 1, m.keys_half.at[:, :384])
            sides["values"] = share(17, 2, m.keys_half.at[:, 384:])

    def share(i, part, target):
        target.at[two][...] = m.qkv_low[:, cut(part * WIDTH + core * 384, 384)]
        return side(
            i, m.qkv_low.at[:, cut(part * WIDTH + (1 - core) * 384, 384)], target.at[two], at.sibling
        )

    def near_ready():
        sides["grad_sib"].wait()
        sides["ext_sib"].wait()

    def proj_ready():
        att_sib.wait()
        sides["resid"].wait()
        sides["query"].wait()

    def far_here():
        project_queries(chip_rows(1 - at.chip))
        for i in range(2):
            sides["grad_far", i].wait()
            piece = m.attended_grad.at[rows_of((far_block * 2 + i) * 64, 64)]
            sides["grad_pass", i] = side((10, 21)[i], piece, piece, at.sibling)
        sides["ext_far"].wait()
        sides["ext_pass"] = side(13, m.query_ext.at[far], m.query_ext.at[far], at.sibling)

    def far_ready():
        for i in range(2):
            sides["grad_pass", i].wait()
        sides["ext_pass"].wait()

    def keys_ready():
        sides["keys"].wait()
        sides["values"].wait()

    def keep_input(rows, back):
        input_grad[0, rows, :] = back.astype(BF)

    def input_back():
        m.attn_grad[...] = dot_rt(m.qkv_low[...], m.qkv_w[...])
        norm_back(
            lambda rows: m.attn_grad[rows, :],
            lambda rows: m.resid_grad[rows, :],
            attn_gain,
            m.hat1,
            m.fac1,
            m.vec,
            (0, 1),
            keep_input,
        )

    def vec_step(s):
        if s > 0:
            sides["vec"].wait()
            m.vec[...] = m.vec[...] + m.vec_came[s - 1]
        if s > DIMS:
            vec_out[...] = m.vec[...]
            return
        copy = pltpu.make_async_remote_copy(
            src_ref=m.vec,
            dst_ref=m.vec_came.at[s],
            send_sem=m.vec_send.at[s],
            recv_sem=m.vec_recv.at[s],
            device_id=(at.partners + (at.sibling,))[s],
            device_id_type=MESH,
        )
        copy.start()
        sides["vec"] = copy

    def feed_out():
        m.out_part[...] = dot(m.hidden[...], m.down_w[...])
        sides["out"] = side(7, m.out_part.at[two_other], m.out_came, at.sibling)

    def close():
        sides["out"].wait()
        block_output[0] = (
            m.resid[...] + (m.out_part[two, :] + m.out_came[...]) + down_bias[...]
        ).astype(BF)

    near, other_chip = at.chip, 1 - at.chip
    pieces = dict(
        mlp_back=mlp_back,
        resid_back=resid_back,
        extend=extend,
        query1=lambda: query_side(range(3)),
        query2=lambda: query_side(range(3, 6)),
        near_ready=near_ready,
        near1=lambda: key_side(near, True, range(3)),
        near2=lambda: key_side(near, True, range(3, 6)),
        proj_ready=proj_ready,
        far_here=far_here,
        far_ready=far_ready,
        far1=lambda: key_side(other_chip, False, range(3)),
        far2=lambda: key_side(other_chip, False, range(3, 6)),
        keys_ready=keys_ready,
        input_back=input_back,
        feed_out=feed_out,
        close=close,
    )
    for step in PLAN:
        if isinstance(step, str):
            pieces[step]()
        elif len(step) == 1:
            vec_step(step[0])
        elif len(step) == 2:
            start(*step)
        else:
            ex.finish(*step)

    for w in range(len(WIDTHS)):
        ex.done(w)
    slice_copy(0, m.hidden_near, m.hidden_near).wait_send()


PLAN = (
    "mlp_back", (1, 3), (1, 2), (1, 5), (1, 4), (1, 0), (1, 1), "resid_back",
    "extend", "query1", "query2", (0, 5), "near_ready", (0, 1), (0, 2), (0, 4),
    (0, 0), "proj_ready", (2, 0), (2, 3), "near1", (0, 3), (1, 1, 0), (1, 0, 0),
    (2, 2), (1, 2, 0), (2, 1), "near2", (0, 5, 1), (1, 4, 0), (1, 5, 0), (2, 4),
    (0, 2, 1), (0, 1, 1), (0, 0, 1), (2, 5), "far_here", (1, 1, 1), (2, 0, 0), (2, 3, 0),
    (1, 0, 1), "far_ready", "far1", "far2", (1, 2, 1), (0, 4, 1), (2, 4, 0), (0, 0, 2),
    (1, 5, 1), (2, 1, 0), (0, 3, 1), "keys_ready", (3, 0), (1, 3, 0), (3, 1), (0, 2, 2),
    (0, 1, 2), (0, 5, 2), (3, 2), (2, 2, 0), (3, 4), (3, 3), (2, 3, 1), (1, 0, 2),
    (1, 4, 1), (1, 2, 2), (2, 0, 1), (0, 4, 2), (2, 4, 1), (3, 5), (1, 5, 2), (2, 5, 0),
    (1, 1, 2), "input_back", (0,), (3, 0, 0), (3, 1, 0), (0, 5, 3), (0, 2, 3), (1, 3, 1),
    (1, 4, 2), (0, 3, 2), (3, 2, 0), (2, 3, 2), (0, 0, 3), (1, 2, 3), (2, 4, 2), (2, 1, 1),
    (3, 3, 0), (2, 0, 2), (2, 5, 1), (2, 2, 1), (0, 4, 3), (3, 4, 0), (1, 0, 3), (3, 5, 0),
    (3, 0, 1), (1,), (3, 1, 1), (1, 1, 3), (1, 5, 3), (0, 2, 4), (0, 5, 4), (1, 3, 2),
    (1, 4, 3), (0, 0, 4), (3, 2, 1), (0, 3, 3), (0, 1, 3), (2, 5, 2), (2, 4, 3), (2, 3, 3),
    (3, 3, 1), (0, 4, 4), (2, 0, 3), (2, 2, 2), (1, 2, 4), (3, 0, 2), (3, 4, 1), (3, 1, 2),
    (2,), (2, 1, 2), (1, 0, 4), (3, 5, 1), (1, 1, 4), (0, 2, 5), (1, 5, 4), (0, 0, 5),
    (0, 3, 4), (0, 5, 5), (3, 2, 2), (2, 5, 3), (1, 3, 3), (0, 1, 4), (2, 4, 4), (1, 4, 4),
    (3, 0, 3), (2, 3, 4), (3, 3, 2), (3, 1, 3), (1, 2, 5), (2, 0, 4), (2, 2, 3), (3,),
    (3, 5, 2), (0, 4, 5), (1, 0, 5), (2, 1, 3), (0, 3, 5), (3, 4, 2), (1, 1, 5), (0, 5, 6),
    (1, 5, 5), (2, 5, 4), (0, 1, 5), (2, 4, 5), (1, 3, 4), (3, 0, 4), (0, 0, 6), (2, 3, 5),
    (3, 1, 4), (0, 2, 6), (3, 2, 3), (3, 3, 3), (2, 0, 5), (3, 5, 3), (2, 2, 4), (0, 4, 6),
    (1, 4, 5), (1, 2, 6), (0, 3, 6), "feed_out", (2, 5, 5), (2, 4, 6), (4,), (3, 0, 5),
    (1, 0, 6), (2, 1, 4), (3, 1, 5), (3, 4, 3), (1, 1, 6), (1, 3, 5), (2, 3, 6), (1, 5, 6),
    (0, 1, 6), (3, 3, 4), (3, 5, 4), (0, 4, 7), (2, 2, 5), (3, 2, 4), (0, 2, 7), (3, 0, 6),
    (0, 3, 7), (2, 1, 5), (2, 5, 6), (3, 4, 4), (3, 1, 6), (5,), (0, 5, 7), (0, 0, 7),
    (2, 3, 7), (1, 4, 6), (0, 1, 7), (2, 0, 6), (3, 2, 5), (1, 3, 6), (3, 5, 5), (3, 3, 5),
    (3, 0, 7), (1, 2, 7), (0, 4, 8), (2, 5, 7), (2, 2, 6), (1, 1, 7), (2, 1, 6), (1, 5, 7),
    (3, 2, 6), (3, 4, 5), "close", (6,), (0, 3, 8), (1, 0, 7), (7,), (3, 3, 6),
    (1, 4, 7), (0, 1, 8), (2, 4, 7), (1, 3, 7), (3, 5, 6), (0, 0, 8), (3, 0, 8), (3, 4, 6),
    (2, 2, 7), (3, 2, 7), (1, 2, 8), (0, 2, 8), (0, 4, 9), (0, 5, 8), (2, 0, 7), (2, 1, 7),
    (2, 3, 8), (3, 3, 7), (2, 2, 8), (0, 3, 9), (3, 1, 7), (3, 5, 7), (1, 1, 8), (1, 0, 8),
    (2, 5, 8), (3, 4, 7), (1, 5, 8), (0, 1, 9), (3, 2, 8), (1, 4, 8), (1, 3, 8), (2, 1, 8),
    (0, 0, 9), (2, 4, 8), (0, 5, 9), (3, 3, 8), (3, 1, 8), (0, 2, 9), (2, 0, 8), (3, 5, 8),
    (3, 4, 8),
)


def rows_of_shift(rows, shift):
    return pl.ds(pl.multiple_of(rows.start + shift, 16), rows.size)


def spread_kernel(
    wide,
    slim,
    vec,
    block_output_in,
    input_grad_in,
    block_output,
    input_grad,
    attn_gain,
    attn_shift,
    qkv,
    query_bias,
    value_bias,
    proj,
    proj_bias,
    mlp_gain,
    mlp_shift,
    up,
    up_bias,
    down,
    down_bias,
):
    rows = rows_of(pl.program_id(0) * SPREAD_ROWS, SPREAD_ROWS)
    for c in range(2):
        up[:, c * HALF : (c + 1) * HALF] = wide[1, c, rows, :].astype(F32)
        proj[:, c * 384 : (c + 1) * 384] = slim[0, c, rows, :384].astype(F32)
        for part in range(3):
            first = part * WIDTH + c * 384
            source = slim[0, c, rows, 384:] if part == 0 else slim[1, c, rows, (part - 1) * 384 : part * 384]
            qkv[:, first : first + 384] = source.astype(F32)
        for h in range(2):
            down[c, h] = wide[0, c, rows, h * WIDTH : (h + 1) * WIDTH].astype(F32)

    @pl.when(pl.program_id(0) == 0)
    def _():
        block_output[...] = block_output_in[...]
        input_grad[...] = input_grad_in[...]
        for row, ref in enumerate(
            (attn_gain, attn_shift, query_bias, value_bias, proj_bias, mlp_gain, mlp_shift, down_bias)
        ):
            ref[...] = vec[row]
        for t in range(4):
            up_bias[t * WIDTH : (t + 1) * WIDTH] = vec[8 + t]


SPREAD_ROWS = 128


def spread(*given):
    rows = SPREAD_ROWS
    line = lambda n: (jax.ShapeDtypeStruct((n,), F32), pl.BlockSpec((n,), lambda i: (0,)))
    flat = lambda n: (jax.ShapeDtypeStruct((WIDTH, n), F32), pl.BlockSpec((rows, n), lambda i: (i, 0)))
    tokens = (jax.ShapeDtypeStruct((1, TOK, WIDTH), BF), pl.BlockSpec((1, TOK, WIDTH), lambda i: (0, 0, 0)))
    outs = [
        tokens,
        tokens,
        line(WIDTH),
        line(WIDTH),
        flat(3 * WIDTH),
        line(WIDTH),
        line(WIDTH),
        flat(WIDTH),
        line(WIDTH),
        line(WIDTH),
        line(WIDTH),
        flat(HIDDEN),
        line(HIDDEN),
        (
            jax.ShapeDtypeStruct((2, 2 * DIMS, TOK, WIDTH), F32),
            pl.BlockSpec((2, 2, TOK, WIDTH), lambda i: (0, i, 0, 0)),
        ),
        line(WIDTH),
    ]
    return pl.pallas_call(
        spread_kernel,
        grid=(WIDTH // rows,),
        out_shape=[o[0] for o in outs],
        in_specs=[pl.BlockSpec(memory_space=pltpu.VMEM)] * len(given),
        out_specs=[o[1] for o in outs],
        compiler_params=pltpu.CompilerParams(vmem_limit_bytes=24 << 20),
    )(*(pltpu.with_memory_space_constraint(v, pltpu.VMEM) for v in given))


def body(
    block_input,
    out_cotangent,
    image_lengths,
    span_order,
    attn_gain,
    attn_shift,
    qkv_weight,
    query_bias,
    value_bias,
    proj_weight,
    proj_bias,
    mlp_gain,
    mlp_shift,
    up_weight,
    up_bias,
    down_weight,
    down_bias,
):
    vmem = pl.BlockSpec(memory_space=pltpu.VMEM)
    hbm = pl.BlockSpec(memory_space=pl.ANY)
    held = scratch()
    block_output, input_grad, wide, slim, vec = pl.pallas_call(
        kernel,
        out_shape=[
            pltpu.VMEM((1, TOK, WIDTH), BF),
            pltpu.VMEM((1, TOK, WIDTH), BF),
            pltpu.VMEM((2, 2, WIDTH, HALF), BF),
            pltpu.VMEM((2, 2, WIDTH, WIDTH), BF),
            pltpu.VMEM((16, WIDTH), F32),
        ],
        in_specs=[pl.BlockSpec(memory_space=pltpu.SMEM)] * 2 + [vmem] * 11 + [hbm] * 4,
        out_specs=[vmem] * 5,
        scratch_shapes=[held[name] for name in NAMES],
        compiler_params=pltpu.CompilerParams(
            collective_id=0, has_side_effects=True, vmem_limit_bytes=VMEM_LIMIT
        ),
    )(
        image_lengths,
        span_order,
        block_input,
        out_cotangent,
        attn_gain,
        attn_shift,
        query_bias,
        value_bias,
        proj_bias,
        mlp_gain,
        mlp_shift,
        up_bias,
        down_bias,
        qkv_weight,
        proj_weight,
        up_weight,
        down_weight,
    )
    outs = list(spread(wide, slim, vec, block_output, input_grad))
    outs[13] = outs[13].reshape(HIDDEN, WIDTH)
    return tuple(outs)


VMEM_LIMIT = 46 << 20


def solution(mesh):
    tokens = P("rows", "seq", None)
    return jax.shard_map(
        body,
        mesh=mesh,
        in_specs=(tokens, tokens, P("rows", None), P("rows", None)) + (P(),) * 13,
        out_specs=(tokens, tokens) + (P(),) * 13,
        check_vma=False,
    )
```

```python
from types import SimpleNamespace

import jax
import jax.numpy as jnp
from jax import lax
from jax.experimental import pallas as pl
from jax.experimental.pallas import tpu as pltpu
from jax.sharding import PartitionSpec as P

MESH = pl.DeviceIdType.MESH
BF, F32 = jnp.bfloat16, jnp.float32
WIDTH = 768
HIDDEN = 3072
HALF = HIDDEN // 2
TOK = 128
LEN = 512
PAIRS = 6
SCALE = 64**-0.5
EPSILON = 1e-6

DIMS = 6
DOWN, UP, PROJ, KEYS = range(4)
WIDTHS = (HALF, HALF, WIDTH, WIDTH)
HALVINGS = (4, 3, 3, 3)

TAIL = (
    0.14361835615286447,
    0.14366105191010822,
    0.12424683572786965,
    0.09467827005043768,
    0.003990377379362003,
    0.09912410558005538,
    -0.21460327937017376,
    0.13425173188400444,
    -0.02896737861797067,
)
DENSITY = 0.3989422804014327


def rows_of(start, size):
    return pl.ds(pl.multiple_of(start, size), size)


def dot(a, b):
    return lax.dot_general(a, b, (((1,), (0,)), ((), ())), preferred_element_type=F32)


def dot_rt(a, b):
    return lax.dot_general(a, b, (((1,), (1,)), ((), ())), preferred_element_type=F32)


def dot_lt(a, b):
    return lax.dot_general(a, b, (((0,), (0,)), ((), ())), preferred_element_type=F32)


def place():
    row, seq = lax.axis_index("rows"), lax.axis_index("seq")
    x, y, z_lo = row % 4, (row // 4) % 4, row // 16
    z_hi, core = seq // 2, seq % 2
    z = z_hi * 2 + z_lo

    def device(x, y, z, core):
        return ((z % 2) * 16 + y * 4 + x, (z // 2) * 2 + core)

    near = lambda v: v + 1 - 2 * (v % 2)
    far = lambda v: 3 - v
    first = lambda v: (v % 2 + v // 2) % 2
    return SimpleNamespace(
        seq=seq,
        core=core,
        chip=z_hi,
        partners=(
            device(near(x), y, z, core),
            device(far(x), y, z, core),
            device(x, near(y), z, core),
            device(x, far(y), z, core),
            device(x, y, near(z), core),
            device(x, y, far(z), core),
        ),
        bits=(first(x), x // 2, first(y), y // 2, first(z), z // 2),
        sibling=(row, z_hi * 2 + 1 - core),
        across=(row, (1 - z_hi) * 2 + core),
    )


class Exchange:
    def __init__(self, at, grads, whole, landing, send_sem, recv_sem, over_sem):
        self.at = at
        self.grads, self.whole, self.landing = grads, whole, landing
        self.send_sem, self.recv_sem, self.over_sem = send_sem, recv_sem, over_sem
        self.copies = {}

    def dim(self, k, s):
        return (k + s) % DIMS

    def rows(self, k, s):
        low = TOK * k
        for t in range(min(s, 3)):
            low = low + self.at.bits[self.dim(k, t)] * (64 >> t)
        return low

    def block(self, w, k, s, mine, whole=False):
        held = self.whole[w].at[self.at.core] if whole else self.grads[w]
        bit = self.at.bits[self.dim(k, s)]
        pick = bit if mine else 1 - bit
        if w == DOWN:
            half = lambda p: pl.ds(pl.multiple_of(p * WIDTH, 128), WIDTH)
            if s == 0:
                return held.at[pl.ds(TOK * k, TOK), half(pick)]
            low = TOK * k + pick * (64 >> (s - 1))
            for t in range(1, s):
                low = low + self.at.bits[self.dim(k, t)] * (64 >> (t - 1))
            return held.at[pl.ds(pl.multiple_of(low, 16), 64 >> (s - 1)), half(self.at.bits[k])]
        if s < 3:
            size = 64 >> s
            return held.at[pl.ds(pl.multiple_of(self.rows(k, s) + pick * size, 16), size)]
        width = WIDTHS[w] // 2
        return held.at[
            pl.ds(pl.multiple_of(self.rows(k, 3), 16), 16),
            pl.ds(pl.multiple_of(pick * width, 128), width),
        ]

    def slot(self, w, k, s):
        held = self.landing[w].at[k]
        if w == DOWN:
            return held.at[pl.ds((0, 64, 96, 112, 128)[s - 1], (64, 32, 16, 16, 16)[s - 1]), pl.ds(0, WIDTH)]
        if s < 3:
            return held.at[pl.ds((0, 64, 96)[s], 64 >> s)]
        if HALVINGS[w] == 3:
            return held.at[pl.ds(64 + 16 * s, 16)]
        width = WIDTHS[w] // 2
        return held.at[pl.ds((112, 112, 128)[s - 3], 16), pl.ds((0, width, 0)[s - 3], width)]

    def start(self, w, k, s=0):
        last = HALVINGS[w] - 1
        if s <= last:
            src, dst, d = self.block(w, k, s, False), self.slot(w, k, s), self.dim(k, s)
        elif s < DIMS:
            src, dst, d = self.block(w, k, last, True), self.slot(w, k, s), self.dim(k, s)
        else:
            t = last + DIMS - s
            src = dst = self.block(w, k, t, True, True)
            d = self.dim(k, t)
        copy = pltpu.make_async_remote_copy(
            src_ref=src,
            dst_ref=dst,
            send_sem=self.send_sem.at[w, k],
            recv_sem=self.recv_sem.at[w, k, s - (w == DOWN)],
            device_id=self.at.partners[d],
            device_id_type=MESH,
        )
        copy.start()
        self.copies[w, k, s] = copy

    def over(self, w, k, part):
        half = self.block(w, k, 0, part == 0, True)
        self.crossing(w, half, half).start()

    def crossing(self, w, src, dst):
        return pltpu.make_async_remote_copy(
            src_ref=src,
            dst_ref=dst,
            send_sem=self.over_sem.at[0, w],
            recv_sem=self.over_sem.at[1, w],
            device_id=self.at.sibling,
            device_id_type=MESH,
        )

    def done(self, w):
        self.crossing(w, self.whole[w].at[self.at.core], self.whole[w].at[1 - self.at.core]).wait()

    def finish(self, w, k, s):
        steps, last = DIMS + HALVINGS[w], HALVINGS[w] - 1
        self.copies[w, k, s].wait()
        if s < DIMS:
            kept, slot = self.block(w, k, min(s, last), True), self.slot(w, k, s)
            total = (kept[...].astype(F32) + slot[...].astype(F32)).astype(BF)
            if s < DIMS - 1:
                kept[...] = total
            else:
                self.block(w, k, last, True, True)[...] = total
        if s < steps - 1:
            self.start(w, k, s + 1)
        if s >= steps - 2:
            self.over(w, k, s - (steps - 2))


def normalize(load, gain, shift, normed, factor, result, base):
    def step(i, carry):
        rows = rows_of(i * 16, 16)
        v = load(rows)
        c = v - jnp.mean(v, axis=1, keepdims=True)
        f = lax.rsqrt(jnp.mean(c * c, axis=1, keepdims=True) + EPSILON)
        n = c * f
        normed[rows, :] = n
        factor[rows, :] = f
        result[rows_of(base + i * 16, 16), :] = (n * gain[...] + shift[...]).astype(BF)
        return carry

    lax.fori_loop(0, TOK // 16, step, 0, unroll=True)


def folded(v):
    return jnp.sum(v.reshape(2, 8, WIDTH), axis=0)


def norm_back(load_grad, load_rest, gain, normed, factor, vec, where, keep):
    zero = jnp.zeros((8, WIDTH), F32)

    def step(i, carry):
        rows = rows_of(i * 16, 16)
        e, n = load_grad(rows), normed[rows, :]
        g = e * gain[...]
        a = jnp.mean(g, axis=1, keepdims=True)
        b = jnp.mean(g * n, axis=1, keepdims=True)
        back = load_rest(rows) + factor[rows, :] * (g - a - n * b)
        keep(rows, back)
        return carry[0] + folded(e * n), carry[1] + folded(e), carry[2] + folded(back)

    sums = lax.fori_loop(0, TOK // 16, step, (zero, zero, zero), unroll=True)
    for row, total in zip(where, sums):
        vec[row : row + 1, :] = jnp.sum(total, axis=0, keepdims=True)


def scratch():
    v = pltpu.VMEM
    dma = pltpu.SemaphoreType.DMA
    sets = len(WIDTHS)
    return dict(
        qkv_w=v((WIDTH, 3 * WIDTH), BF),
        proj_w=v((WIDTH, WIDTH), BF),
        up_w=v((WIDTH, HALF), BF),
        down_w=v((HALF, WIDTH), BF),
        lines=v((8, WIDTH), F32),
        up_bias_half=v((1, HALF), F32),
        up_sum=v((1, HALF), F32),
        normed_in=v((LEN, WIDTH), BF),
        queries=v((LEN, WIDTH), BF),
        keys=v((LEN, WIDTH), BF),
        values=v((LEN, WIDTH), BF),
        key_ext=v((LEN, 128), BF),
        query_ext=v((LEN, 128), BF),
        stat=v((TOK, 128), F32),
        hat1=v((TOK, WIDTH), F32),
        fac1=v((TOK, 1), F32),
        attended_full=v((TOK, WIDTH), F32),
        attended=v((2 * TOK, WIDTH), BF),
        resid=v((TOK, WIDTH), F32),
        hat2=v((TOK, WIDTH), F32),
        fac2=v((TOK, 1), F32),
        mlp_in=v((2 * TOK, WIDTH), BF),
        cot2=v((2 * TOK, WIDTH), BF),
        hidden_grad=v((2 * TOK, HALF), F32),
        hidden=v((2 * TOK, HALF), BF),
        cot_near=v((2, DIMS, TOK, WIDTH), BF),
        hidden_near=v((DIMS, 2 * TOK, 128), BF),
        up_low=v((2 * TOK, HALF), BF),
        mlp_part=v((2 * TOK, WIDTH), F32),
        mlp_came=v((TOK, WIDTH), F32),
        out_part=v((2 * TOK, WIDTH), F32),
        out_came=v((TOK, WIDTH), F32),
        resid_grad=v((TOK, WIDTH), F32),
        resid_low=v((TOK, WIDTH), BF),
        attended_grad=v((LEN, WIDTH), BF),
        qkv_low=v((TOK, 3 * WIDTH), BF),
        resid_half=v((2 * TOK, 384), BF),
        query_half=v((2 * TOK, 384), BF),
        keys_half=v((2 * TOK, WIDTH), BF),
        key_grad=v((TOK, WIDTH), F32),
        value_grad=v((TOK, WIDTH), F32),
        attn_grad=v((TOK, WIDTH), F32),
        vec=v((16, WIDTH), F32),
        vec_came=v((DIMS + 1, 16, WIDTH), F32),
        grads_wide=v((2, WIDTH, HALF), BF),
        grads_slim=v((2, WIDTH, WIDTH), BF),
        landing_wide=v((2, DIMS, 160, HALF), BF),
        landing_slim=v((2, DIMS, 160, WIDTH), BF),
        send_sem=dma((sets, DIMS)),
        recv_sem=dma((sets, DIMS, DIMS + max(HALVINGS[0] - 1, *HALVINGS[1:]))),
        over_sem=dma((2, sets)),
        side_send=dma((22,)),
        side_recv=dma((22,)),
        vec_send=dma((DIMS + 1,)),
        vec_recv=dma((DIMS + 1,)),
        load_sem=dma((4,)),
        near_sem=dma((4,)),
        slice_sem=dma((1 + DIMS,)),
    )


NAMES = tuple(scratch())


def kernel(
    lengths,
    order,
    x,
    cot,
    attn_gain,
    attn_shift,
    query_bias,
    value_bias,
    proj_bias,
    mlp_gain,
    mlp_shift,
    up_bias,
    down_bias,
    qkv_weight,
    proj_weight,
    up_weight,
    down_weight,
    block_output,
    input_grad,
    whole_wide,
    whole_slim,
    vec_out,
    *refs,
):
    m = SimpleNamespace(**dict(zip(NAMES, refs)))
    at = place()
    core, seq = at.core, at.seq
    pair_of = lambda wide, slim: (wide.at[0], wide.at[1], slim.at[0], slim.at[1])
    grads = pair_of(m.grads_wide, m.grads_slim)
    ex = Exchange(
        at,
        grads,
        pair_of(whole_wide, whole_slim),
        pair_of(m.landing_wide, m.landing_slim),
        m.send_sem,
        m.recv_sem,
        m.over_sem,
    )

    barrier = pltpu.get_barrier_semaphore()
    for device in at.partners + (at.sibling, at.across):
        pl.semaphore_signal(barrier, inc=1, device_id=device, device_id_type=MESH)

    loads = [
        pltpu.make_async_copy(src, dst, m.load_sem.at[i])
        for i, (src, dst) in enumerate(
            (
                (qkv_weight, m.qkv_w),
                (down_weight.at[rows_of(core * HALF, HALF)], m.down_w),
                (proj_weight, m.proj_w),
                (up_weight.at[:, rows_of(core * HALF, HALF)], m.up_w),
            )
        )
    ]
    for load in loads:
        load.start()

    def side(i, src, dst, device):
        copy = pltpu.make_async_remote_copy(
            src_ref=src,
            dst_ref=dst,
            send_sem=m.side_send.at[i],
            recv_sem=m.side_recv.at[i],
            device_id=device,
            device_id_type=MESH,
        )
        copy.start()
        return copy

    own = rows_of(seq * TOK, TOK)
    two = rows_of(core * TOK, TOK)
    two_other = rows_of((1 - core) * TOK, TOK)
    far_block = (1 - at.chip) * 2 + core
    far = rows_of(far_block * TOK, TOK)
    chip_rows = lambda chip: rows_of(chip * 2 * TOK, 2 * TOK)
    cut = lambda start, size: pl.ds(pl.multiple_of(start, 128), size)

    vectors = (attn_gain, attn_shift, query_bias, value_bias, proj_bias, mlp_gain, mlp_shift, down_bias)
    for i, vector in enumerate(vectors):
        m.lines[i : i + 1, :] = vector[...][None]
    attn_gain, attn_shift, query_bias, value_bias, proj_bias, mlp_gain, mlp_shift, down_bias = (
        m.lines.at[i : i + 1] for i in range(8)
    )

    normalize(
        lambda rows: x[0, rows, :].astype(F32), attn_gain, attn_shift, m.hat1, m.fac1, m.normed_in, seq * TOK
    )
    m.cot2[two, :] = cot[0]

    pl.semaphore_wait(barrier, DIMS + 2)
    in_far = []
    for i in range(2):
        piece = m.normed_in.at[rows_of((seq * 2 + i) * 64, 64)]
        in_far.append(side((1, 18)[i], piece, piece, at.across))
    in_sib = side(0, m.normed_in.at[own], m.normed_in.at[own], at.sibling)
    cot_sib = side(3, m.cot2.at[two], m.cot2.at[two], at.sibling)

    def near_copy(i, src, dst, device):
        return pltpu.make_async_remote_copy(
            src_ref=src,
            dst_ref=dst,
            send_sem=m.near_sem.at[i],
            recv_sem=m.near_sem.at[i + 1],
            device_id=device,
            device_id_type=MESH,
        )

    for d in range(DIMS):
        near_copy(0, m.cot2.at[two], m.cot_near.at[core, d], at.partners[d]).start()

    ends = [lengths[0, 0]]
    for i in (1, 2):
        ends.append(ends[-1] + lengths[0, i])
    lane = lax.broadcasted_iota(jnp.int32, (1, 128), 1)
    token = lax.broadcasted_iota(jnp.int32, (TOK, 128), 0)

    def image(j):
        t = token + order[0, j] * TOK
        return sum((t >= end).astype(jnp.int32) for end in ends)

    for j in range(4):
        other = jnp.where(lane == image(j), 0.0, -1e30)
        m.key_ext[j * TOK : (j + 1) * TOK, :] = jnp.where(lane < 4, other, jnp.where(lane < 76, 1.0, 0.0)).astype(BF)
    image_own = jnp.where(lane == image(seq), 1.0, 0.0)
    m.query_ext[own, :] = image_own.astype(BF)
    m.up_bias_half[...] = jnp.where(core == 0, up_bias[:HALF], up_bias[HALF:])[None]
    m.vec[...] = jnp.zeros((16, WIDTH), F32)
    m.vec[7:8, :] = jnp.sum(
        jnp.sum(cot[0].astype(F32).reshape(TOK // 8, 8, WIDTH), axis=0), axis=0, keepdims=True
    )
    m.stat[...] = jnp.zeros((TOK, 128), F32)
    low_lanes = (lane < 64).astype(BF)
    high_lanes = (lane >= 64).astype(BF)

    def both(v):
        return jnp.concatenate((v * low_lanes, v * high_lanes), axis=0)

    def joined(v):
        return jnp.where(lane < 64, v[:TOK], v[TOK:])

    def beside(a, b):
        return jnp.concatenate((a, b), axis=1)

    def project_keys(rows):
        a = m.normed_in[rows, :]
        m.keys[rows, :] = dot(a, m.qkv_w[:, WIDTH : 2 * WIDTH]).astype(BF)
        m.values[rows, :] = (dot(a, m.qkv_w[:, 2 * WIDTH :]) + value_bias[...]).astype(BF)

    def project_queries(rows):
        part = dot(m.normed_in[rows, :], m.qkv_w[:, :WIDTH])
        m.queries[rows, :] = ((part + query_bias[...]) * SCALE).astype(BF)

    loads[0].wait()
    in_sib.wait()
    project_keys(chip_rows(at.chip))
    project_queries(chip_rows(at.chip))
    loads[1].wait()
    cot_sib.wait()
    m.hidden_grad[...] = dot_rt(m.cot2[...], m.down_w[...])
    in_pass = []
    for i in range(2):
        in_far[i].wait()
        piece = m.normed_in.at[rows_of((far_block * 2 + i) * 64, 64)]
        in_pass.append(side((2, 19)[i], piece, piece, at.sibling))
    project_keys(far)
    for copy in in_pass:
        copy.wait()
    project_keys(rows_of(((1 - at.chip) * 2 + 1 - core) * TOK, TOK))

    def attend(i, carry):
        cols = rows_of(i * 128, 128)
        ext = m.query_ext[own, :]
        s = dot_rt(
            beside(both(m.queries[own, cols]), jnp.concatenate((ext, ext), axis=0)),
            beside(m.keys[:, cols], m.key_ext[...]),
        )
        top = jnp.max(s, axis=1, keepdims=True)
        e = jnp.exp(s - top).astype(BF)
        out = dot(e, beside(m.values[:, cols], jnp.ones((LEN, 128), BF)))
        total = out[:, 128:]
        out = joined(out[:, :128] * (1.0 / total))
        m.attended_full[:, cols] = out
        m.attended[two, cols] = out.astype(BF)
        logs = top + jnp.log(total)
        m.stat[...] = jnp.where(
            lane == 2 * i, logs[:TOK], jnp.where(lane == 2 * i + 1, logs[TOK:], m.stat[...])
        )
        return carry

    lax.fori_loop(0, PAIRS, attend, 0, unroll=True)

    loads[2].wait()
    m.resid[...] = x[0].astype(F32) + dot(m.attended[two, :], m.proj_w[...]) + proj_bias[...]
    normalize(lambda rows: m.resid[rows, :], mlp_gain, mlp_shift, m.hat2, m.fac2, m.mlp_in, core * TOK)
    mlp_sib = side(4, m.mlp_in.at[two], m.mlp_in.at[two], at.sibling)
    att_sib = side(5, m.attended.at[two], m.attended.at[two], at.sibling)
    near_copy(0, m.cot_near.at[core], m.cot_near.at[core], at.sibling).wait()
    near_pass = near_copy(2, m.cot_near.at[core], m.cot_near.at[core], at.sibling)
    near_pass.start()
    loads[3].wait()

    def slice_copy(k, src, dst):
        return pltpu.make_async_remote_copy(
            src_ref=src,
            dst_ref=dst,
            send_sem=m.slice_sem.at[0],
            recv_sem=m.slice_sem.at[1 + k],
            device_id=at.partners[k],
            device_id_type=MESH,
        )

    slices = []

    def feed(rows, first):
        for i in range(3):
            cols = slice(i * 512, (i + 1) * 512)
            u = dot(m.mlp_in[rows, :], m.up_w[:, cols]) + m.up_bias_half[:, cols]
            t = 1.0 / (1.0 + 0.36 * jnp.abs(u))
            tail = jnp.full_like(t, TAIL[-1])
            for c in TAIL[-2::-1]:
                tail = tail * t + c
            e = jnp.exp(-0.5 * (u * u))
            tail = tail * (t * e)
            phi = jnp.where(u >= 0, 1.0 - tail, tail)
            m.hidden[rows, cols] = (u * phi).astype(BF)
            g = m.hidden_grad[rows, cols] * (phi + u * (DENSITY * e))
            m.up_low[rows, cols] = g.astype(BF)
            total = jnp.sum(g.reshape(TOK // 8, 8, 512), axis=0)
            total = jnp.sum(total, axis=0, keepdims=True)
            m.up_sum[:, cols] = total if first else m.up_sum[:, cols] + total
            if not first:
                for k in (2 * i, 2 * i + 1):
                    units = cut(256 * k + 128 * (1 - at.bits[k]), 128)
                    slices.append(slice_copy(k, m.hidden.at[:, units], m.hidden_near.at[k]))
                    slices[k].start()

    feed(two, True)
    mlp_sib.wait()
    feed(two_other, False)

    def block_of(k):
        return slice(k * TOK, (k + 1) * TOK)

    def start(w, k):
        block = block_of(k)
        if w == DOWN:
            if near_waits:
                near_waits.pop().wait()
            slices[k].wait_recv()
            units = cut(256 * k + 128 * at.bits[k], 128)
            total = dot_lt(m.hidden[:, units], m.cot2[...])
            for c in range(2):
                total = total + dot_lt(m.hidden_near[k, c * TOK : (c + 1) * TOK], m.cot_near[c, k])
            grads[w][block, cut(at.bits[k] * WIDTH, WIDTH)] = total.astype(BF)
            ex.start(w, k, 1)
            return
        if w == UP:
            grads[w][block, :] = dot_lt(m.mlp_in[:, block], m.up_low[...]).astype(BF)
        elif w == PROJ:
            grads[w][block, :384] = dot_lt(m.attended[:, block], m.resid_half[...]).astype(BF)
            grads[w][block, 384:] = dot_lt(
                m.normed_in[chip_rows(at.chip), block], m.query_half[...]
            ).astype(BF)
        else:
            grads[w][block, :] = dot_lt(
                m.normed_in[chip_rows(at.chip), block], m.keys_half[...]
            ).astype(BF)
        ex.start(w, k)

    sides = {}
    near_waits = [near_pass]

    def mlp_back():
        m.mlp_part[...] = dot_rt(m.up_low[...], m.up_w[...])
        sides["part"] = side(6, m.mlp_part.at[two_other], m.mlp_came, at.sibling)
        for h in range(2):
            for t in range(2):
                m.vec[8 + 2 * h + t : 9 + 2 * h + t, :] = jnp.where(
                    core == h, m.up_sum[:, t * WIDTH : (t + 1) * WIDTH], 0.0
                )

    def keep_resid(rows, back):
        m.resid_grad[rows, :] = back
        m.resid_low[rows, :] = back.astype(BF)

    def resid_back():
        sides["part"].wait()
        norm_back(
            lambda rows: m.mlp_part[rows_of_shift(rows, core * TOK), :] + m.mlp_came[rows, :],
            lambda rows: cot[0, rows, :].astype(F32),
            mlp_gain,
            m.hat2,
            m.fac2,
            m.vec,
            (5, 6, 4),
            keep_resid,
        )
        m.attended_grad[own, :] = dot_rt(m.resid_low[...], m.proj_w[...]).astype(BF)
        grad = m.attended_grad.at[own]
        for i in range(2):
            piece = m.attended_grad.at[rows_of((seq * 2 + i) * 64, 64)]
            sides["grad_far", i] = side((9, 20)[i], piece, piece, at.across)
        sides["grad_sib"] = side(8, grad, grad, at.sibling)

    def parts(v):
        found = []
        for _ in range(3):
            found.append(v.astype(BF))
            v = v - found[-1].astype(F32)
        return found

    def extend():
        feature = lax.broadcasted_iota(jnp.int32, (WIDTH, 128), 0)
        head_of = (feature // 64 + 16 == lax.broadcasted_iota(jnp.int32, (WIDTH, 128), 1)).astype(BF)
        means = m.attended_grad[own, :].astype(F32) * m.attended_full[...]
        sums = sum(dot(p, head_of) for p in parts(means))
        ext = image_own
        for j, p in enumerate(parts(-(m.stat[...] + sums))):
            to = lax.broadcasted_iota(jnp.int32, (128, 128), 1)
            of = lax.broadcasted_iota(jnp.int32, (128, 128), 0)
            spot = jnp.where(
                of < 12, 4 + 3 * of + j, jnp.where((of >= 16) & (of < 28), 3 * of - 8 + j, -1)
            )
            ext = ext + dot(p, (to == spot).astype(BF))
        m.query_ext[own, :] = ext.astype(BF)
        ext = m.query_ext.at[own]
        sides["ext_far"] = side(12, ext, ext, at.across)
        sides["ext_sib"] = side(11, ext, ext, at.sibling)
        m.resid_half[two, :] = m.resid_low[:, cut(core * 384, 384)]
        sides["resid"] = side(
            14, m.resid_low.at[:, cut((1 - core) * 384, 384)], m.resid_half.at[two], at.sibling
        )

    def picks(i):
        a, b = lane - 4 - 6 * i, lane - 40 - 6 * i
        first = jnp.where((lane < 4) | ((a >= 0) & (a < 3)), 1.0, 0.0).astype(BF)
        second = jnp.where((lane < 4) | ((a >= 3) & (a < 6)), 1.0, 0.0).astype(BF)
        third = jnp.where((b >= 0) & (b < 3), 1.0, 0.0).astype(BF)
        fourth = jnp.where((b >= 3) & (b < 6), 1.0, 0.0).astype(BF)
        return (lambda v: jnp.concatenate((v * first, v * second), axis=0)), (
            lambda v: jnp.concatenate((v * third, v * fourth), axis=0)
        )

    def query_side(pairs):
        for i in pairs:
            cols = slice(i * 128, (i + 1) * 128)
            of_scores, of_means = picks(i)
            ext, k = m.query_ext[own, :], m.keys[:, cols]
            p = jnp.exp(
                dot_rt(beside(both(m.queries[own, cols]), of_scores(ext)), beside(k, m.key_ext[...]))
            )
            y = dot_rt(
                beside(both(m.attended_grad[own, cols]), of_means(ext)),
                beside(m.values[:, cols], m.key_ext[...]),
            )
            g = joined(dot((p * y).astype(BF), k)) * SCALE
            m.vec[2:3, cols] = jnp.sum(g, axis=0, keepdims=True)
            m.qkv_low[:, cols] = g.astype(BF)
        if PAIRS - 1 in pairs:
            sides["query"] = share(15, 0, m.query_half)

    def key_side(chip, first, pairs):
        rows = chip_rows(chip)
        for i in pairs:
            cols = slice(i * 128, (i + 1) * 128)
            of_scores, of_means = picks(i)
            q, g, ext = m.queries[rows, cols], m.attended_grad[rows, cols], m.key_ext[own, :]
            other = m.query_ext[rows, :]
            p = jnp.exp(dot_rt(beside(both(m.keys[own, cols]), of_scores(ext)), beside(q, other)))
            y = dot_rt(beside(both(m.values[own, cols]), of_means(ext)), beside(g, other))
            dv = joined(dot(p.astype(BF), g))
            dk = joined(dot((p * y).astype(BF), q))
            if first:
                m.value_grad[:, cols] = dv
                m.key_grad[:, cols] = dk
            else:
                dv = dv + m.value_grad[:, cols]
                dk = dk + m.key_grad[:, cols]
                m.vec[3:4, cols] = jnp.sum(dv, axis=0, keepdims=True)
                m.qkv_low[:, WIDTH + i * 128 : WIDTH + (i + 1) * 128] = dk.astype(BF)
                m.qkv_low[:, 2 * WIDTH + i * 128 : 2 * WIDTH + (i + 1) * 128] = dv.astype(BF)
        if not first and PAIRS - 1 in pairs:
            sides["keys"] = share(16, 1, m.keys_half.at[:, :384])
            sides["values"] = share(17, 2, m.keys_half.at[:, 384:])

    def share(i, part, target):
        target.at[two][...] = m.qkv_low[:, cut(part * WIDTH + core * 384, 384)]
        return side(
            i, m.qkv_low.at[:, cut(part * WIDTH + (1 - core) * 384, 384)], target.at[two], at.sibling
        )

    def near_ready():
        sides["grad_sib"].wait()
        sides["ext_sib"].wait()

    def proj_ready():
        att_sib.wait()
        sides["resid"].wait()
        sides["query"].wait()

    def far_here():
        project_queries(chip_rows(1 - at.chip))
        for i in range(2):
            sides["grad_far", i].wait()
            piece = m.attended_grad.at[rows_of((far_block * 2 + i) * 64, 64)]
            sides["grad_pass", i] = side((10, 21)[i], piece, piece, at.sibling)
        sides["ext_far"].wait()
        sides["ext_pass"] = side(13, m.query_ext.at[far], m.query_ext.at[far], at.sibling)

    def far_ready():
        for i in range(2):
            sides["grad_pass", i].wait()
        sides["ext_pass"].wait()

    def keys_ready():
        sides["keys"].wait()
        sides["values"].wait()

    def keep_input(rows, back):
        input_grad[0, rows, :] = back.astype(BF)

    def input_back():
        m.attn_grad[...] = dot_rt(m.qkv_low[...], m.qkv_w[...])
        norm_back(
            lambda rows: m.attn_grad[rows, :],
            lambda rows: m.resid_grad[rows, :],
            attn_gain,
            m.hat1,
            m.fac1,
            m.vec,
            (0, 1),
            keep_input,
        )

    def vec_step(s):
        if s > 0:
            sides["vec"].wait()
            m.vec[...] = m.vec[...] + m.vec_came[s - 1]
        if s > DIMS:
            vec_out[...] = m.vec[...]
            return
        copy = pltpu.make_async_remote_copy(
            src_ref=m.vec,
            dst_ref=m.vec_came.at[s],
            send_sem=m.vec_send.at[s],
            recv_sem=m.vec_recv.at[s],
            device_id=(at.partners + (at.sibling,))[s],
            device_id_type=MESH,
        )
        copy.start()
        sides["vec"] = copy

    def feed_out():
        m.out_part[...] = dot(m.hidden[...], m.down_w[...])
        sides["out"] = side(7, m.out_part.at[two_other], m.out_came, at.sibling)

    def close():
        sides["out"].wait()
        block_output[0] = (
            m.resid[...] + (m.out_part[two, :] + m.out_came[...]) + down_bias[...]
        ).astype(BF)

    near, other_chip = at.chip, 1 - at.chip
    pieces = dict(
        mlp_back=mlp_back,
        resid_back=resid_back,
        extend=extend,
        query1=lambda: query_side(range(3)),
        query2=lambda: query_side(range(3, 6)),
        near_ready=near_ready,
        near1=lambda: key_side(near, True, range(3)),
        near2=lambda: key_side(near, True, range(3, 6)),
        proj_ready=proj_ready,
        far_here=far_here,
        far_ready=far_ready,
        far1=lambda: key_side(other_chip, False, range(3)),
        far2=lambda: key_side(other_chip, False, range(3, 6)),
        keys_ready=keys_ready,
        input_back=input_back,
        feed_out=feed_out,
        close=close,
    )
    for step in PLAN:
        if isinstance(step, str):
            pieces[step]()
        elif len(step) == 1:
            vec_step(step[0])
        elif len(step) == 2:
            start(*step)
        else:
            ex.finish(*step)

    for w in range(len(WIDTHS)):
        ex.done(w)
    slice_copy(0, m.hidden_near, m.hidden_near).wait_send()


PLAN = (
    "mlp_back", (1, 3), (1, 2), (1, 5), (1, 4), (1, 0), (1, 1), "resid_back",
    "extend", "query1", "query2", (0, 5), "near_ready", (0, 1), (0, 2), (0, 4),
    (0, 0), "proj_ready", (2, 0), (2, 3), "near1", (0, 3), (1, 1, 0), (1, 0, 0),
    (2, 2), (1, 2, 0), (2, 1), "near2", (0, 5, 1), (1, 4, 0), (1, 5, 0), (2, 4),
    (0, 2, 1), (0, 1, 1), (0, 0, 1), (2, 5), "far_here", (1, 1, 1), (2, 0, 0), (2, 3, 0),
    (1, 0, 1), "far_ready", "far1", "far2", (1, 2, 1), (0, 4, 1), (2, 4, 0), (0, 0, 2),
    (1, 5, 1), (2, 1, 0), (0, 3, 1), "keys_ready", (3, 0), (1, 3, 0), (3, 1), (0, 2, 2),
    (0, 1, 2), (0, 5, 2), (3, 2), (2, 2, 0), (3, 4), (3, 3), (2, 3, 1), (1, 0, 2),
    (1, 4, 1), (1, 2, 2), (2, 0, 1), (0, 4, 2), (2, 4, 1), (3, 5), (1, 5, 2), (2, 5, 0),
    (1, 1, 2), "input_back", (0,), (3, 0, 0), (3, 1, 0), (0, 5, 3), (0, 2, 3), (1, 3, 1),
    (1, 4, 2), (0, 3, 2), (3, 2, 0), (2, 3, 2), (0, 0, 3), (1, 2, 3), (2, 4, 2), (2, 1, 1),
    (3, 3, 0), (2, 0, 2), (2, 5, 1), (2, 2, 1), (0, 4, 3), (3, 4, 0), (1, 0, 3), (3, 5, 0),
    (3, 0, 1), (1,), (3, 1, 1), (1, 1, 3), (1, 5, 3), (0, 2, 4), (0, 5, 4), (1, 3, 2),
    (1, 4, 3), (0, 0, 4), (3, 2, 1), (0, 3, 3), (0, 1, 3), (2, 5, 2), (2, 4, 3), (2, 3, 3),
    (3, 3, 1), (0, 4, 4), (2, 0, 3), (2, 2, 2), (1, 2, 4), (3, 0, 2), (3, 4, 1), (3, 1, 2),
    (2,), (2, 1, 2), (1, 0, 4), (3, 5, 1), (1, 1, 4), (0, 2, 5), (1, 5, 4), (0, 0, 5),
    (0, 3, 4), (0, 5, 5), (3, 2, 2), (2, 5, 3), (1, 3, 3), (0, 1, 4), (2, 4, 4), (1, 4, 4),
    (3, 0, 3), (2, 3, 4), (3, 3, 2), (3, 1, 3), (1, 2, 5), (2, 0, 4), (2, 2, 3), (3,),
    (3, 5, 2), (0, 4, 5), (1, 0, 5), (2, 1, 3), (0, 3, 5), (3, 4, 2), (1, 1, 5), (0, 5, 6),
    (1, 5, 5), (2, 5, 4), (0, 1, 5), (2, 4, 5), (1, 3, 4), (3, 0, 4), (0, 0, 6), (2, 3, 5),
    (3, 1, 4), (0, 2, 6), (3, 2, 3), (3, 3, 3), (2, 0, 5), (3, 5, 3), (2, 2, 4), (0, 4, 6),
    (1, 4, 5), (1, 2, 6), (0, 3, 6), "feed_out", (2, 5, 5), (2, 4, 6), (4,), (3, 0, 5),
    (1, 0, 6), (2, 1, 4), (3, 1, 5), (3, 4, 3), (1, 1, 6), (1, 3, 5), (2, 3, 6), (1, 5, 6),
    (0, 1, 6), (3, 3, 4), (3, 5, 4), (0, 4, 7), (2, 2, 5), (3, 2, 4), (0, 2, 7), (3, 0, 6),
    (0, 3, 7), (2, 1, 5), (2, 5, 6), (3, 4, 4), (3, 1, 6), (5,), (0, 5, 7), (0, 0, 7),
    (2, 3, 7), (1, 4, 6), (0, 1, 7), (2, 0, 6), (3, 2, 5), (1, 3, 6), (3, 5, 5), (3, 3, 5),
    (3, 0, 7), (1, 2, 7), (0, 4, 8), (2, 5, 7), (2, 2, 6), (1, 1, 7), (2, 1, 6), (1, 5, 7),
    (3, 2, 6), (3, 4, 5), "close", (6,), (0, 3, 8), (1, 0, 7), (7,), (3, 3, 6),
    (1, 4, 7), (0, 1, 8), (2, 4, 7), (1, 3, 7), (3, 5, 6), (0, 0, 8), (3, 0, 8), (3, 4, 6),
    (2, 2, 7), (3, 2, 7), (1, 2, 8), (0, 2, 8), (0, 4, 9), (0, 5, 8), (2, 0, 7), (2, 1, 7),
    (2, 3, 8), (3, 3, 7), (2, 2, 8), (0, 3, 9), (3, 1, 7), (3, 5, 7), (1, 1, 8), (1, 0, 8),
    (2, 5, 8), (3, 4, 7), (1, 5, 8), (0, 1, 9), (3, 2, 8), (1, 4, 8), (1, 3, 8), (2, 1, 8),
    (0, 0, 9), (2, 4, 8), (0, 5, 9), (3, 3, 8), (3, 1, 8), (0, 2, 9), (2, 0, 8), (3, 5, 8),
    (3, 4, 8),
)


def rows_of_shift(rows, shift):
    return pl.ds(pl.multiple_of(rows.start + shift, 16), rows.size)


def spread_kernel(
    wide,
    slim,
    vec,
    block_output_in,
    input_grad_in,
    block_output,
    input_grad,
    attn_gain,
    attn_shift,
    qkv,
    query_bias,
    value_bias,
    proj,
    proj_bias,
    mlp_gain,
    mlp_shift,
    up,
    up_bias,
    down,
    down_bias,
):
    rows = rows_of(pl.program_id(0) * SPREAD_ROWS, SPREAD_ROWS)
    for c in range(2):
        up[:, c * HALF : (c + 1) * HALF] = wide[1, c, rows, :].astype(F32)
        proj[:, c * 384 : (c + 1) * 384] = slim[0, c, rows, :384].astype(F32)
        for part in range(3):
            first = part * WIDTH + c * 384
            source = slim[0, c, rows, 384:] if part == 0 else slim[1, c, rows, (part - 1) * 384 : part * 384]
            qkv[:, first : first + 384] = source.astype(F32)
        for h in range(2):
            down[c, h] = wide[0, c, rows, h * WIDTH : (h + 1) * WIDTH].astype(F32)

    @pl.when(pl.program_id(0) == 0)
    def _():
        block_output[...] = block_output_in[...]
        input_grad[...] = input_grad_in[...]
        for row, ref in enumerate(
            (attn_gain, attn_shift, query_bias, value_bias, proj_bias, mlp_gain, mlp_shift, down_bias)
        ):
            ref[...] = vec[row]
        for t in range(4):
            up_bias[t * WIDTH : (t + 1) * WIDTH] = vec[8 + t]


SPREAD_ROWS = 128


def spread(*given):
    rows = SPREAD_ROWS
    line = lambda n: (jax.ShapeDtypeStruct((n,), F32), pl.BlockSpec((n,), lambda i: (0,)))
    flat = lambda n: (jax.ShapeDtypeStruct((WIDTH, n), F32), pl.BlockSpec((rows, n), lambda i: (i, 0)))
    tokens = (jax.ShapeDtypeStruct((1, TOK, WIDTH), BF), pl.BlockSpec((1, TOK, WIDTH), lambda i: (0, 0, 0)))
    outs = [
        tokens,
        tokens,
        line(WIDTH),
        line(WIDTH),
        flat(3 * WIDTH),
        line(WIDTH),
        line(WIDTH),
        flat(WIDTH),
        line(WIDTH),
        line(WIDTH),
        line(WIDTH),
        flat(HIDDEN),
        line(HIDDEN),
        (
            jax.ShapeDtypeStruct((2, 2 * DIMS, TOK, WIDTH), F32),
            pl.BlockSpec((2, 2, TOK, WIDTH), lambda i: (0, i, 0, 0)),
        ),
        line(WIDTH),
    ]
    return pl.pallas_call(
        spread_kernel,
        grid=(WIDTH // rows,),
        out_shape=[o[0] for o in outs],
        in_specs=[pl.BlockSpec(memory_space=pltpu.VMEM)] * len(given),
        out_specs=[o[1] for o in outs],
        compiler_params=pltpu.CompilerParams(vmem_limit_bytes=24 << 20),
    )(*(pltpu.with_memory_space_constraint(v, pltpu.VMEM) for v in given))


def body(
    block_input,
    out_cotangent,
    image_lengths,
    span_order,
    attn_gain,
    attn_shift,
    qkv_weight,
    query_bias,
    value_bias,
    proj_weight,
    proj_bias,
    mlp_gain,
    mlp_shift,
    up_weight,
    up_bias,
    down_weight,
    down_bias,
):
    vmem = pl.BlockSpec(memory_space=pltpu.VMEM)
    hbm = pl.BlockSpec(memory_space=pl.ANY)
    held = scratch()
    block_output, input_grad, wide, slim, vec = pl.pallas_call(
        kernel,
        out_shape=[
            pltpu.VMEM((1, TOK, WIDTH), BF),
            pltpu.VMEM((1, TOK, WIDTH), BF),
            pltpu.VMEM((2, 2, WIDTH, HALF), BF),
            pltpu.VMEM((2, 2, WIDTH, WIDTH), BF),
            pltpu.VMEM((16, WIDTH), F32),
        ],
        in_specs=[pl.BlockSpec(memory_space=pltpu.SMEM)] * 2 + [vmem] * 11 + [hbm] * 4,
        out_specs=[vmem] * 5,
        scratch_shapes=[held[name] for name in NAMES],
        compiler_params=pltpu.CompilerParams(
            collective_id=0, has_side_effects=True, vmem_limit_bytes=VMEM_LIMIT
        ),
    )(
        image_lengths,
        span_order,
        block_input,
        out_cotangent,
        attn_gain,
        attn_shift,
        query_bias,
        value_bias,
        proj_bias,
        mlp_gain,
        mlp_shift,
        up_bias,
        down_bias,
        qkv_weight,
        proj_weight,
        up_weight,
        down_weight,
    )
    outs = list(spread(wide, slim, vec, block_output, input_grad))
    outs[13] = outs[13].reshape(HIDDEN, WIDTH)
    return tuple(outs)


VMEM_LIMIT = 46 << 20


def solution(mesh):
    tokens = P("rows", "seq", None)
    return jax.shard_map(
        body,
        mesh=mesh,
        in_specs=(tokens, tokens, P("rows", None), P("rows", None)) + (P(),) * 13,
        out_specs=(tokens, tokens) + (P(),) * 13,
        check_vma=False,
    )
```
